32 devices in a mesh: dp: 4 (over z), expert: 8 (over y, x, core).
Axes of the slice: x: 2, y: 2, z: 4, core: 2. Of those that a mesh axis runs over, the one named last changes fastest.
Arguments:
- tokens: bfloat16 [12288, 768], P(('dp', 'expert')), may hold values from -6 to 6
- segments: int32 [32, 384], P(('dp', 'expert')), may hold values from 0 to 3, never falling along the last dimension, each value on 1 to 192 neighbouring positions
- routes: int32 [12288, 1], P(('dp', 'expert')), may hold values from 0 to 7; in each aligned block of 384 rows (0 to 383, 384 to 767, ...) at most 96 rows name the same one
- norm_gains: bfloat16 [3, 768], P(None, 'expert'), may hold values from 0.099609375 to 1.8984375
- norm_shifts: bfloat16 [3, 768], P(None, 'expert'), may hold values from -1 to 1
- project_in: bfloat16 [768, 2304], P(None, 'expert'), may hold values from -0.21875 to 0.21875
- project_out: bfloat16 [768, 768], P(None, 'expert'), may hold values from -0.625 to 0.625
- dense_up: bfloat16 [768, 3072], P(None, 'expert'), may hold values from -0.21875 to 0.21875
- dense_down: bfloat16 [3072, 768], P(None, 'expert'), may hold values from -0.109375 to 0.109375
- centroids: bfloat16 [8, 768], P(None, 'expert'), may hold values from -0.15625 to 0.15625
- expert_up: bfloat16 [8, 768, 3072], P('expert', None, 'dp'), may hold values from -0.21875 to 0.21875
- expert_down: bfloat16 [8, 768, 3072], P('expert', None, 'dp'), may hold values from -0.109375 to 0.109375
- cotangent: bfloat16 [12288, 768], P(('dp', 'expert')), may hold values from -6 to 6
Outputs:
- output: bfloat16 [12288, 768], P(('dp', 'expert'))
- tokens_grad: float32 [12288, 768], P(('dp', 'expert'))
- gains_grad: float32 [3, 768], P(None, 'expert')
- shifts_grad: float32 [3, 768], P(None, 'expert')
- project_in_grad: float32 [768, 2304], P(None, 'expert')
- project_out_grad: float32 [768, 768], P(None, 'expert')
- dense_up_grad: float32 [768, 3072], P(None, 'expert')
- dense_down_grad: float32 [3072, 768], P(None, 'expert')
- centroids_grad: float32 [8, 768], P(None, 'expert')
- expert_up_grad: float32 [8, 768, 3072], P('expert', None, 'dp')
- expert_down_grad: float32 [8, 768, 3072], P('expert', None, 'dp')
The draws below stay inside these ranges and needn't reach their ends.
Inputs may be any that keep to these rules, and one draw needn't show every extreme that they name: `routes`: among the 384 tokens of one packed row no expert is chosen more than 96 times, and in every draw some expert is chosen exactly 96 times by some row. `segments`: each packed row holds 4 documents numbered in order, never falling; a document has at most 192 tokens and one has exactly that many.
All inputs are finite; a program needn't handle non-finite values.
Results may differ from the reference program's by a relative error of at most 0.019.
Values may be sent and summed in bfloat16 or wider, within the bound.
No kernel may reach another device: no remote copies, remote signals or barrier semaphores. Data moves between devices by JAX's collectives and lax.ppermute only.
A program may use at most 192 MiB of HBM per device.

```python
import math
import jax
import jax.numpy as jnp
import numpy as np
from jax import lax

D = 768
FF = 3072
HEAD_DIM = 64
HEADS = 12
TOK_DEV = 384
DOCS = 4
EXPERTS = 8
SEQS = 32
TOKENS = 12288
CAP = 96


def shard_levels(own_key, dims, cuts, least, high):
    factor_of, own = 1.0, jax.random.fold_in(own_key, 6)
    for dim, blocks in cuts:
        heights = jnp.exp(jax.random.uniform(jax.random.fold_in(own, dim), (blocks,), jnp.float32, least / len(cuts), high / len(cuts)))
        factor_of = factor_of * jnp.repeat(heights, dims[dim] // blocks).reshape([-1 if axis == dim else 1 for axis in range(len(dims))])
    return factor_of


def split_up(amount, total, bound, lean):
    loads = [(1 << 20) // math.isqrt(grade ** lean) + 1 for grade in range(2, amount + 1)]
    spare, counts = total - bound - (amount - 1), [1] * (amount - 1)
    while spare > 0:
        free = [i for i in range(amount - 1) if counts[i] < bound]
        mass, remaining = sum([loads[i] for i in free]), spare
        for i in free:
            extra = min(bound - counts[i], max(1, remaining * loads[i] // mass), spare)
            counts[i] = counts[i] + extra
            spare = spare - extra
    return np.array([bound] + counts)


def uneven_parts(key, number_of, total, most, slope):
    if number_of == 2:
        one = jax.random.randint(key, (), max(1, total - most), min(most, total - 1) + 1)
        return jnp.stack([one, total - one])
    lengths = jnp.asarray(split_up(number_of, total, most, slope), jnp.int32)
    twos = (number_of - 1) // 2
    source_of, taker = lengths[1:1 + 2 * twos:2], lengths[2:2 + 2 * twos:2]
    room = jnp.minimum(source_of - 1, most - taker)
    shifted = jax.random.randint(jax.random.fold_in(key, 1), (twos,), 0, 1 << 20) % (room + 1)
    lengths = lengths.at[1:1 + 2 * twos:2].set(source_of - shifted).at[2:2 + 2 * twos:2].set(taker + shifted)
    return lengths[jax.random.permutation(jax.random.fold_in(key, 2), number_of)]


def routed_block(key, own, number, rows, amount, top, bound, skew):
    order = jax.random.permutation(key, amount)
    heavy_load, ordinary = shares(amount, rows * top, bound, skew, True), shares(amount, rows * top, bound, skew, False)
    places = jnp.arange(amount)

    def named(tallies, offset_by):
        used = int((tallies > 0).sum())
        fixed = max(1, used // 4)
        moved = fixed + (places - fixed + offset_by * (used - fixed)) % max(1, amount - fixed)
        return jnp.zeros((amount,), jnp.int32).at[order[jnp.where(places < fixed, places, moved)]].set(jnp.asarray(tallies, jnp.int32))

    tallies = jnp.where(number % 4 == 0, named(heavy_load, number // 4), named(ordinary, number - number // 4 - 1))
    mixed = jax.random.permutation(jax.random.fold_in(own, 3), amount)
    giver, sink = mixed[0:amount // 2 * 2:2], mixed[1:amount // 2 * 2:2]
    slack = jnp.minimum(tallies[giver] - 1, bound - tallies[sink]) // 2
    slack = jnp.where((giver == order[0]) | (sink == order[0]) | (tallies[sink] == 0), 0, jnp.maximum(slack, 0))
    moved = jax.random.randint(jax.random.fold_in(own, 4), (amount // 2,), 0, 1 << 20) % (slack + 1)
    tallies = tallies.at[giver].add(-moved).at[sink].add(moved)
    members = jnp.searchsorted(jnp.cumsum(tallies), jnp.arange(rows * top), side="right").astype(jnp.int32)
    grid = members.reshape(top, rows).T
    grid = grid[jax.random.permutation(jax.random.fold_in(own, 1), rows)]
    offset_by = jax.random.randint(jax.random.fold_in(own, 2), (rows, 1), 0, top)
    return jnp.take_along_axis(grid, (jnp.arange(top)[None, :] + offset_by) % top, axis=1)


def shares(count, total, bound, lean, full):
    weights = [(1 << 20) // math.isqrt(rank ** lean) + 1 for rank in range(1, count + 1)]
    largest = bound if full else min(bound, max(-(-total // count), total * weights[0] // sum(weights)))
    least = 1 if total - largest >= count - 1 else 0
    given, rest = [largest] + [least] * (count - 1), total - largest - least * (count - 1)
    while rest > 0:
        candidates = [i for i in range(1, count) if given[i] < largest] or [i for i in range(1, count) if given[i] < bound]
        mass, left = sum([weights[i] for i in candidates]), rest
        for i in candidates:
            extra = min(bound - given[i], max(1, left * weights[i] // mass), rest)
            given[i] = given[i] + extra
            rest = rest - extra
    return np.array(given)


def bell_draw(own_key, dims, deviation, limit, shards=(), kind=jnp.bfloat16):
    drawn = jax.random.normal(own_key, dims, jnp.float32) * deviation
    if len(shards) > 0:
        drawn = shard_levels(own_key, dims, shards, -0.22, 0.18) * drawn
    return jnp.clip(drawn, min=-limit, max=limit).astype(kind)


def setup_inputs(seed: int = 0) -> dict:
    seeds = jax.random.split(jax.random.key(seed), 14)
    tokens = bell_draw(seeds[0], (TOKENS, D), 1.0, 6.0, ((0, 32),))
    segments = jax.vmap(lambda own: jnp.searchsorted(jnp.cumsum(uneven_parts(own, DOCS, TOK_DEV, TOK_DEV // 2, 1)), jnp.arange(TOK_DEV), side="right"))(jax.random.split(seeds[1], SEQS)).reshape((SEQS, TOK_DEV)).astype(jnp.int32)
    routes_keys = jax.random.split(jax.random.fold_in(seeds[2], 1), TOKENS // TOK_DEV)
    routes_turns = jax.random.permutation(jax.random.fold_in(seeds[2], 3), TOKENS // TOK_DEV)
    routes = jax.vmap(lambda own, number: routed_block(jax.random.fold_in(seeds[2], 2), own, number, TOK_DEV, EXPERTS, 1, CAP, 1))(routes_keys, routes_turns).reshape((TOKENS, 1))
    norm_gains = jnp.clip(1.0 + 0.18 * jax.random.normal(seeds[3], (3, D), jnp.float32), 0.099609375, 1.8984375).astype(jnp.bfloat16)
    norm_shifts = bell_draw(seeds[4], (3, D), 0.2, 1.0, ((1, 8),))
    project_in = bell_draw(seeds[5], (D, 3 * D), D ** -0.5, 0.21875, ((1, 8),))
    project_out = bell_draw(seeds[6], (D, D), (D // 8) ** -0.5, 0.625, ((1, 8),))
    dense_up = bell_draw(seeds[7], (D, FF), D ** -0.5, 0.21875, ((1, 8),))
    dense_down = bell_draw(seeds[8], (FF, D), FF ** -0.5, 0.109375, ((1, 8),))
    centroids = bell_draw(seeds[9], (EXPERTS, D), (2 * D) ** -0.5, 0.15625, ((1, 8),))
    expert_up = bell_draw(seeds[10], (EXPERTS, D, FF), D ** -0.5, 0.21875, ((0, 8), (2, 4)))
    expert_down = bell_draw(seeds[11], (EXPERTS, D, FF), FF ** -0.5, 0.109375, ((0, 8), (2, 4)))
    cotangent = bell_draw(seeds[12], (TOKENS, D), 1.0, 6.0, ((0, 32),))
    return dict(tokens=tokens, segments=segments, routes=routes, norm_gains=norm_gains, norm_shifts=norm_shifts, project_in=project_in, project_out=project_out, dense_up=dense_up, dense_down=dense_down, centroids=centroids, expert_up=expert_up, expert_down=expert_down, cotangent=cotangent)


highest = lax.Precision.HIGHEST

@jax.custom_vjp
def low(v):
    return lax.optimization_barrier(v.astype(jnp.bfloat16)).astype(jnp.float32)

@jax.custom_vjp
def low_back(v):
    return v

def low_keep(v):
    return (low(v), None)

def low_pass(kept, grad):
    return (grad,)

def back_keep(v):
    return (v, None)

def back_low(kept, grad):
    return (low(grad),)
low.defvjp(low_keep, low_pass)
low_back.defvjp(back_keep, back_low)

def layer_norm(rows, gain, shift):
    average = lax.optimization_barrier(jnp.mean(rows, axis=-1, keepdims=True))
    centred = rows - average
    spread = lax.optimization_barrier(jnp.mean(centred * centred, axis=-1, keepdims=True))
    return centred * lax.rsqrt(spread + 1e-05) * gain + shift

def smooth(values):
    return jax.nn.gelu(values, approximate=True)

def attend(projected, documents):
    groups, length = documents.shape
    parts = projected.reshape(groups, length, 3, HEADS, HEAD_DIM)
    queries = parts[:, :, 0]
    keys = parts[:, :, 1]
    values = parts[:, :, 2]
    scores = jnp.einsum('gqhd,gkhd->ghqk', queries, keys, precision=highest) * HEAD_DIM ** (-0.5)
    scores = low_back(scores)
    position = jnp.arange(length, dtype=jnp.int32)
    allowed = (documents[:, :, None] == documents[:, None, :]) & (position[None, :, None] >= position[None, None, :])
    scores = jnp.where(allowed[:, None], scores, -1000000000.0)
    row_max = lax.optimization_barrier(jnp.max(scores, axis=-1, keepdims=True))
    lifted = jnp.exp(scores - row_max)
    probs = lifted / lax.optimization_barrier(jnp.sum(lifted, axis=-1, keepdims=True))
    mixed = jnp.einsum('ghqk,gkhd->gqhd', low(probs), values, precision=highest)
    return mixed.reshape(groups * length, D)

def reference(tokens, segments, routes, norm_gains, norm_shifts, project_in, project_out, dense_up, dense_down, centroids, expert_up, expert_down, cotangent):
    grouping = math.gcd(SEQS, max(1, 4096 // TOK_DEV))
    flat_routes = routes[:, 0].astype(jnp.int32)
    per_row = flat_routes.reshape(SEQS, TOK_DEV)
    onehot = (per_row[:, :, None] == jnp.arange(EXPERTS, dtype=jnp.int32)[None, None, :]).astype(jnp.int32)
    ranks = lax.optimization_barrier(jnp.sum((jnp.cumsum(onehot, axis=1).astype(jnp.int32) - 1) * onehot, axis=-1)).astype(jnp.int32)
    slots = (jnp.arange(SEQS, dtype=jnp.int32)[:, None] * CAP + ranks).reshape(-1).astype(jnp.int32)
    table = jnp.full((EXPERTS, SEQS * CAP), TOKENS, jnp.int32).at[flat_routes, slots].set(jnp.arange(TOKENS, dtype=jnp.int32))

    def forward(rows, gains, shifts, whole_in, whole_out, whole_up, whole_down, whole_centroids, all_up, all_down):

        def dense_group(inputs):
            block_rows, documents = inputs
            first_in = low(layer_norm(block_rows, gains[0], shifts[0]))
            projected = low(low_back(jnp.dot(first_in, whole_in, precision=highest)))
            mixed = low(low_back(attend(projected.reshape(grouping, TOK_DEV, 3 * D), documents)))
            after_attn = block_rows + low_back(jnp.dot(mixed, whole_out, precision=highest))
            second_in = low(layer_norm(after_attn, gains[1], shifts[1]))
            widened = low_back(jnp.dot(second_in, whole_up, precision=highest))
            activated = low(smooth(widened))
            return after_attn + low_back(jnp.dot(activated, whole_down, precision=highest))
        hidden = lax.map(jax.checkpoint(dense_group), (rows.reshape(SEQS // grouping, grouping * TOK_DEV, D), segments.reshape(SEQS // grouping, grouping, TOK_DEV)))
        hidden = hidden.reshape(TOKENS, D)
        moe_in = layer_norm(hidden, gains[2], shifts[2])
        padded = jnp.concatenate([low(moe_in), jnp.zeros((1, D), jnp.float32)], axis=0)
        chosen = jnp.take(whole_centroids, flat_routes, axis=0)
        gates = jax.nn.sigmoid(lax.optimization_barrier(jnp.sum(moe_in * chosen, axis=-1)))

        def one_expert(inputs):
            rows_index, up_weight, down_weight = inputs
            arrived = low_back(padded[rows_index])
            expert_pre = low_back(jnp.dot(arrived, up_weight, precision=highest))
            expert_act = low(smooth(expert_pre))
            result = jnp.dot(expert_act, down_weight.T, precision=highest)
            return low(low_back(result))
        returned = lax.map(jax.checkpoint(one_expert), (table, all_up, all_down))
        combined = returned[flat_routes, slots]
        return hidden + gates[:, None] * combined
    floats = [item.astype(jnp.float32) for item in (tokens, norm_gains, norm_shifts, project_in, project_out, dense_up, dense_down, centroids, expert_up, expert_down)]
    output, pull = jax.vjp(forward, *floats)
    grads = pull(cotangent.astype(jnp.float32))
    return (output.astype(jnp.bfloat16), grads[0], grads[1], grads[2], grads[3], grads[4], grads[5], grads[6], grads[7], grads[8], grads[9])
```

```python
import functools

import jax
import jax.numpy as jnp
from jax import lax
from jax.experimental import pallas as pl
from jax.experimental.pallas import tpu as pltpu
from jax.sharding import PartitionSpec as P

HEAD_DIM = 64
EXTRA = 128
BF = jnp.bfloat16
F32 = jnp.float32
I32 = jnp.int32
ROOT = 0.7978845608028654
COST = dict(
    prepare=3, attend=16, widen=9, dispatch=10, expert_rows=4, expert=20, gate_back=10, widen_back=12, fold=1,
    second_back=14, attend_back=5, fold_again=1, project_back=2, tokens_back=2, fold_last=1, joined=1,
    combine=1, finish=1, settle=1,
)
WIDE = ("attend", "widen", "dispatch", "expert", "widen_back")
VMEM_LIMIT = 60 * 1024 * 1024


def mm(left, right):
    return lax.dot_general(left, right, (((1,), (0,)), ((), ())), preferred_element_type=F32)


def mm_t(left, right):
    return lax.dot_general(left, right, (((1,), (1,)), ((), ())), preferred_element_type=F32)


def t_mm(left, right):
    return lax.dot_general(left, right, (((0,), (0,)), ((), ())), preferred_element_type=F32)


def normalize(rows):
    share = 1.0 / rows.shape[-1]
    centred = rows - jnp.sum(rows, axis=-1, keepdims=True) * share
    spread = jnp.sum(centred * centred, axis=-1, keepdims=True) * share
    inverse = lax.rsqrt(spread + 1e-05)
    return centred * inverse, inverse


def normalize_back(grad, normal, inverse, gain):
    share = 1.0 / grad.shape[-1]
    scaled = grad * gain
    first = jnp.sum(scaled, axis=-1, keepdims=True) * share
    second = jnp.sum(scaled * normal, axis=-1, keepdims=True) * share
    rows = inverse * (scaled - first - normal * second)
    return rows, jnp.sum(grad * normal, axis=0, keepdims=True), jnp.sum(grad, axis=0, keepdims=True)


def smooth_and_slope(v):
    square = v * v
    bend = jnp.tanh(v * (ROOT + ROOT * 0.044715 * square))
    half = 0.5 + 0.5 * bend
    slope = half + 0.5 * v * (1.0 - bend * bend) * (ROOT + 3.0 * ROOT * 0.044715 * square)
    return v * half, slope


def split3(v):
    hi = v.astype(BF)
    rest = v - hi.astype(F32)
    mid = rest.astype(BF)
    return hi, mid, (rest - mid.astype(F32)).astype(BF)


def scalar_columns(v):
    hi, mid, low = split3(v)
    lane = lax.broadcasted_iota(I32, (v.shape[0], EXTRA), 1)
    out = jnp.where(lane == 0, hi.astype(F32), 0.0)
    out = jnp.where(lane == 1, mid.astype(F32), out)
    return jnp.where(lane == 2, low.astype(F32), out).astype(BF)


def columns_scalar(columns):
    return jnp.sum(columns.astype(F32), axis=-1, keepdims=True)


def bias_of(by_row, by_column):
    count = by_row.shape[0]
    row = lax.broadcasted_iota(I32, (count, count), 0)
    column = lax.broadcasted_iota(I32, (count, count), 1)
    allowed = (by_row == by_column) & (row >= column)
    return jnp.where(allowed, 0.0, -1000000000.0)


def half_masks():
    lane = lax.broadcasted_iota(I32, (1, 2 * HEAD_DIM), 1)
    first = jnp.where(lane < HEAD_DIM, 1.0, 0.0)
    return first.astype(BF), (1.0 - first).astype(BF)


BEFORE = []


def smallest(outs):
    return min(outs, key=lambda a: a.size * a.dtype.itemsize)


def call(kernel, outs, args, spaces, scratch, name, flops, moved, after=(), results=None):
    where = {"v": pltpu.VMEM, "a": pl.ANY}
    after = list(after) + BEFORE
    read, waited = len(args), len(after)
    args, spaces = list(args) + list(after), spaces + "a" * waited

    def body(*refs):
        kernel(*refs[:read], *refs[read + waited :])

    got = pl.pallas_call(
        body,
        out_shape=outs,
        in_specs=[pl.BlockSpec(memory_space=where[s]) for s in spaces],
        out_specs=[pl.BlockSpec(memory_space=where[s]) for s in results or "v" * len(outs)],
        scratch_shapes=scratch,
        compiler_params=pltpu.CompilerParams(vmem_limit_bytes=VMEM_LIMIT if name in WIDE else VMEM_LIMIT // 2),
        cost_estimate=pl.CostEstimate(flops=COST[name] * 1150000000, bytes_accessed=1000, transcendentals=0),
        name=name,
    )(*args)
    BEFORE[:] = [smallest(got)]
    return got


class Weight:
    def __init__(self, arrays, copies, shape):
        self.arrays, self.copies, self.shape = arrays, copies, shape

    def scratch(self):
        return [pltpu.VMEM(self.shape, BF), pltpu.SemaphoreType.DMA((len(self.copies),))]

    def start(self, refs, whole, sems):
        me = lax.axis_index("expert")
        running = []
        for i, (index, source, place) in enumerate(self.copies):
            copy = pltpu.make_async_copy(
                refs[index].at[source], whole.at[place(me)], sems.at[i]
            )
            copy.start()
            running.append(copy)
        return running


def row_place(k, size, offset, rows, step):
    def place(me):
        if k is None:
            return (pl.ds(offset, rows),)
        return (pl.ds(pl.multiple_of((me ^ k) * size + offset, step), rows),)

    return place


def column_place(k, size, offset, rows):
    def place(me):
        if k is None:
            return (pl.ds(0, rows),)
        start = pl.multiple_of((me ^ k) * size, 128)
        return (pl.ds(offset, rows), pl.ds(start, size))

    return place


class Links:
    def __init__(self, n, m):
        self.n, self.m = n, m
        self.cube = n == 8
        self.line = m == 4
        self.second = ()

    def hop(self, value, bit):
        return lax.ppermute(value, "expert", [(i, i ^ bit) for i in range(self.n)])

    def gated(self, value, gate):
        return lax.optimization_barrier((value, *gate))[0] if gate else value

    def start(self, shard, gate=()):
        if not self.cube:
            return [shard]
        shard = self.gated(shard, gate)
        return [shard, self.hop(shard, 2), self.hop(shard, 4)]

    def pieces(self, started, gate=()):
        shard, by_x, by_y = lax.optimization_barrier((*started, *gate))[:3] if gate else started
        half = shard.shape[0] // 2 // 16 * 16
        far_a = self.hop(by_y[:half], 2)
        far_b = self.hop(by_x[half:], 4)
        self.second = (far_a, far_b)
        return [
            (0, 0, shard), (1, 0, self.hop(shard, 1)), (2, 0, by_x), (3, 0, self.hop(by_x, 1)),
            (4, 0, by_y), (5, 0, self.hop(by_y, 1)), (6, 0, far_a), (6, half, far_b),
            (7, 0, self.hop(far_a, 1)), (7, half, self.hop(far_b, 1)),
        ]

    def by_rows(self, sizes, started, gate=()):
        group = started[0]
        weights, first = [], 0
        if not self.cube:
            whole = lax.all_gather(group, "expert", axis=0, tiled=False)
            for size in sizes:
                part = whole[:, first : first + size].reshape(-1, group.shape[1])
                copies = [(0, (pl.ds(0, part.shape[0]),), row_place(None, 0, 0, part.shape[0], 8))]
                weights.append(Weight([part], copies, part.shape))
                first += size
            return weights
        pieces = self.pieces(started, gate)
        for size in sizes:
            arrays, copies = [], []
            for k, row, array in pieces:
                low, high = max(first, row), min(first + size, row + array.shape[0])
                if low < high:
                    source = (pl.ds(low - row, high - low),)
                    place = row_place(k, size, low - first, high - low, 16 if size % 16 == 0 else 8)
                    copies.append((len(arrays), source, place))
                    arrays.append(array)
            weights.append(Weight(arrays, copies, (self.n * size, group.shape[1])))
            first += size
        return weights

    def by_columns(self, started, gate=()):
        shard = started[0]
        rows, size = shard.shape
        if not self.cube:
            whole = lax.all_gather(shard, "expert", axis=1, tiled=True)
            return Weight([whole], [(0, (pl.ds(0, rows),), column_place(None, 0, 0, rows))], whole.shape)
        arrays, copies = [], []
        for k, row, array in self.pieces(started, gate):
            source = (pl.ds(0, array.shape[0]),)
            copies.append((len(arrays), source, column_place(k, size, row, array.shape[0])))
            arrays.append(array)
        return Weight(arrays, copies, (rows, self.n * size))

    def exchange(self, rows, gate=()):
        blocks = self.gated(rows, gate).reshape(self.n, -1, rows.shape[1])
        got = lax.all_to_all(blocks, "expert", split_axis=0, concat_axis=0, tiled=True)
        return got.reshape(rows.shape)

    def sum_shapes(self, rows, width):
        if not self.cube:
            return [jax.ShapeDtypeStruct((self.n, rows, width), BF)]
        return [jax.ShapeDtypeStruct((self.n // 2, rows, width), BF)] * 2

    def write_sum(self, refs, whole, first, size):
        for k in range(self.n):
            if self.cube:
                me = lax.axis_index("expert")
                step = 16 if size % 16 == 0 else 8
                start = pl.multiple_of((me ^ k) * size, step)
                refs[k % 2][k // 2, first : first + size] = whole[pl.ds(start, size)]
            else:
                refs[0][k, first : first + size] = whole[k * size : (k + 1) * size]

    def twins(self, blocks):
        return [self.hop(blocks[1], 1)] if self.cube else []

    def fold(self, groups, twins, after=()):
        if not self.cube:
            return [jnp.concatenate([g[0] for g in groups], axis=1)]
        rows = [g[0].shape[1] for g in groups]
        total, columns = sum(rows), groups[0][0].shape[2]
        half = total // 2 // 16 * 16

        def kernel(*refs):
            count = len(groups)
            outs = refs[2 * count :]
            first = 0
            for even, odd in zip(refs[:count], refs[count : 2 * count]):
                for m in range(4):
                    value = (even[m].astype(F32) + odd[m].astype(F32)).astype(BF)
                    low, high = first, first + even.shape[1]
                    cut = min(max(half, low), high)
                    if low < cut:
                        outs[m % 2][m // 2, low:cut] = value[: cut - low]
                    if cut < high:
                        outs[2 + m // 2][m % 2, cut - half : high - half] = value[cut - low :]
                first += even.shape[1]

        outs = [jax.ShapeDtypeStruct((2, half, columns), BF)] * 2
        outs += [jax.ShapeDtypeStruct((2, total - half, columns), BF)] * 2
        args = [g[0] for g in groups] + list(twins)
        return list(call(kernel, outs, args, "v" * len(args), [], "fold", 0, 0, after))

    def across(self, kept):
        return [self.hop(kept[1], 2), self.hop(kept[3], 4)] if self.cube else []

    def fold_again(self, kept, got):
        if not self.cube:
            return kept

        def kernel(first, got_first, second, got_second, *outs):
            for i, (mine, other) in enumerate(((first, got_first), (second, got_second))):
                for j in range(2):
                    outs[2 * i + j][...] = (mine[j].astype(F32) + other[j].astype(F32)).astype(BF)

        outs = [jax.ShapeDtypeStruct(a.shape[1:], BF) for a in (kept[0], kept[0], kept[2], kept[2])]
        args = [kept[0], got[0], kept[2], got[1]]
        return list(call(kernel, outs, args, "vvvv", [], "fold_again", 0, 0))

    def across_again(self, kept):
        return [self.hop(kept[1], 4), self.hop(kept[3], 2)] if self.cube else []

    def fold_last(self, kept, got):
        if not self.cube:
            return lax.psum_scatter(kept[0], "expert", scatter_dimension=0, tiled=True)[0]
        half = kept[0].shape[0]

        def kernel(first, got_first, second, got_second, out):
            out[:half] = (first[...].astype(F32) + got_first[...].astype(F32)).astype(BF)
            out[half:] = (second[...].astype(F32) + got_second[...].astype(F32)).astype(BF)

        rows = half + kept[2].shape[0]
        outs = [jax.ShapeDtypeStruct((rows, kept[0].shape[1]), BF)]
        return call(kernel, outs, [kept[0], got[0], kept[2], got[1]], "vvvv", [], "fold_last", 0, 0)[0]

    def along(self, value, pairs):
        return lax.ppermute(value, "dp", pairs)

    def inward(self, value):
        return [self.along(value, [(0, 1), (3, 2)])] if self.line else []

    def middle(self, value):
        return [self.along(value, [(1, 2), (2, 1)])] if self.line else []

    def outward(self, value):
        return [self.along(value, [(1, 0), (2, 3)])] if self.line else []

    def joined(self, value, got):
        if not self.line:
            return value

        def kernel(mine, other, out):
            out[...] = (mine[...].astype(F32) + other[...].astype(F32)).astype(BF)

        outs = [jax.ShapeDtypeStruct(value.shape, BF)]
        return call(kernel, outs, [value, got[0]], "vv", [], "joined", 0, 0)[0]

    def settled(self, value, got):
        if not self.line:
            return lax.psum(value, "dp").astype(F32)
        place = lax.axis_index("dp")
        return jnp.where((place == 1) | (place == 2), value, got[0]).astype(F32)


    def settled_across(self, value, got, units):
        if not self.line:
            value = lax.psum(value, "dp").astype(F32)
            return value[:units].T, value[units:]

        def kernel(mine, other, up, out):
            place = lax.axis_index("dp")

            def write(ref):
                up[...] = ref[:units].astype(F32).T
                out[...] = ref[units:].astype(F32)

            middle = (place == 1) | (place == 2)
            pl.when(middle)(lambda: write(mine))
            pl.when(jnp.logical_not(middle))(lambda: write(other))

        rows, width = value.shape
        outs = [jax.ShapeDtypeStruct((width, units), F32), jax.ShapeDtypeStruct((rows - units, width), F32)]
        return call(kernel, outs, [value, got[0]], "vv", [], "settle", 0, 0)


def finish(parts):
    width = parts[0].shape[1]

    def kernel(*refs):
        ups, downs = refs[-2:]
        first = 0
        for ref in refs[:-2]:
            for i, out in enumerate((ups, downs)):
                out[:, first : first + ref.shape[2]] = ref[i].astype(F32)
            first += ref.shape[2]

    outs = [jax.ShapeDtypeStruct((width, sum(p.shape[2] for p in parts)), F32)] * 2
    return call(kernel, outs, parts, "v" * len(parts), [], "finish", 0, 0)


def prepare(links, routes, cotangent, capacity):
    count, width = cotangent.shape
    n = links.n
    total = n * capacity

    def kernel(by_row, by_column, cot, row_out, column_out, out):
        route_c, route_r = by_row[...], by_column[...]
        token = lax.broadcasted_iota(I32, (count, count), 0)
        other = lax.broadcasted_iota(I32, (count, count), 1)
        same = route_c == route_r
        rank_c = jnp.sum(jnp.where(same & (other < token), 1.0, 0.0), axis=1, keepdims=True)
        rank_r = jnp.sum(jnp.where(same & (token < other), 1.0, 0.0), axis=0, keepdims=True)
        slot_c = route_c * capacity + rank_c.astype(I32)
        slot_r = route_r * capacity + rank_r.astype(I32)
        column_out[...] = slot_c
        row_out[...] = slot_r
        place = lax.broadcasted_iota(I32, (total, count), 0)
        to_slots = jnp.where(place == slot_r, 1.0, 0.0).astype(BF)
        out[...] = mm(to_slots, cot[...]).astype(BF)

    outs = [jax.ShapeDtypeStruct((1, count), I32), jax.ShapeDtypeStruct((count, 1), I32)]
    outs.append(jax.ShapeDtypeStruct((total, width), BF))
    args = [routes, routes.reshape(1, count), cotangent]
    return call(
        kernel, outs, args, "vvv", [], "prepare", 2 * total * count * width, 4 * total * width
    )


def attend(n, tokens, segments, weight_small, weight_in, weight_out, after):
    count, width = tokens.shape
    pairs = width // (2 * HEAD_DIM)
    block = 128
    n_small, n_in, n_out = len(weight_small.arrays), len(weight_in.arrays), len(weight_out.arrays)
    small_rows, cols = weight_small.shape[0] // n, width // n

    def kernel(tok, seg_c, seg_r, *refs):
        small_refs, refs = refs[:n_small], refs[n_small:]
        in_refs, refs = refs[:n_in], refs[n_in:]
        out_refs, refs = refs[:n_out], refs[n_out:]
        first_ref, proj, mixed, lse, after_ref, second_ref, small_ref = refs[:7]
        w_small, small_sems, w_in, in_sems, w_out, out_sems, bias = refs[7:]
        small_copies = weight_small.start(small_refs, w_small, small_sems)
        in_copies = weight_in.start(in_refs, w_in, in_sems)
        out_copies = weight_out.start(out_refs, w_out, out_sems)
        rows = tok[...].astype(F32)
        normal, _ = normalize(rows)
        source = lax.broadcasted_iota(I32, (cols, width), 0)
        place = lax.broadcasted_iota(I32, (cols, width), 1)
        for copy in small_copies:
            copy.wait()
        small = jnp.zeros((small_rows, width), F32)
        for j in range(n):
            spread = jnp.where(place == source + j * cols, 1.0, 0.0).astype(BF)
            small += mm(w_small[j * small_rows : (j + 1) * small_rows, :cols], spread)
        small_ref[...] = small
        first = (normal * small_ref[0:1] + small_ref[3:4]).astype(BF)
        first_ref[...] = first
        bias[...] = bias_of(seg_c[...], seg_r[...])
        lse[...] = jnp.zeros_like(lse)
        for copy in in_copies:
            copy.wait()
        proj[...] = mm_t(first, w_in[...]).astype(BF)
        masks = half_masks()
        lane = lax.broadcasted_iota(I32, (block, 128), 1)

        def pair(i, carry):
            at = [pl.ds(pl.multiple_of(part * width + 128 * i, 128), 128) for part in range(3)]
            for b in range(count // block):
                mine, keys = pl.ds(b * block, block), pl.ds(0, (b + 1) * block)
                q, k, v = proj[mine, at[0]] * 0.125, proj[keys, at[1]], proj[keys, at[2]]
                got = jnp.zeros((block, 128), F32)
                kept = lse[mine]
                for h in range(2):
                    scores = mm_t(q * masks[h], k) + bias[mine, keys]
                    top = jnp.max(scores, axis=1, keepdims=True)
                    lifted = jnp.exp(scores - top)
                    totals = jnp.sum(lifted, axis=1, keepdims=True)
                    probs = (lifted * (1.0 / totals)).astype(BF)
                    got += mm(probs, v * masks[h])
                    kept = jnp.where(lane == 2 * i + h, top + jnp.log(totals), kept)
                lse[mine] = kept
                mixed[mine, at[0]] = got.astype(BF)
            return carry

        lax.fori_loop(0, pairs, pair, 0)
        for copy in out_copies:
            copy.wait()
        after = rows + mm_t(mixed[...], w_out[...])
        after_ref[...] = after
        normal, _ = normalize(after)
        second_ref[...] = (normal * small_ref[1:2] + small_ref[4:5]).astype(BF)

    shape = jax.ShapeDtypeStruct
    outs = [
        shape((count, width), BF), shape((count, 3 * width), BF), shape((count, width), BF),
        shape((count, 128), F32), shape((count, width), F32), shape((count, width), BF),
        shape((small_rows, width), F32),
    ]
    args = [tokens, segments.reshape(count, 1), segments]
    args += weight_small.arrays + weight_in.arrays + weight_out.arrays
    spaces = "vvv" + "a" * (n_small + n_in + n_out)
    scratch = weight_small.scratch() + weight_in.scratch() + weight_out.scratch() + [pltpu.VMEM((count, count), F32)]
    flops = 2 * count * width * (4 * width + 2 * count) * 2
    return call(kernel, outs, args, spaces, scratch, "attend", flops, 12 * count * width * 4, after)


def widen(second_in, weight_up, after):
    count = second_in.shape[0]
    hidden = weight_up.shape[1]
    pieces = len(weight_up.arrays)
    part = hidden // 4

    def kernel(second, *refs):
        up_refs, (act_ref, slope_ref, up, sems) = refs[:pieces], refs[pieces:]
        for copy in weight_up.start(up_refs, up, sems):
            copy.wait()
        rows = second[...]
        for i in range(4):
            at = pl.ds(i * part, part)
            value, slope = smooth_and_slope(mm(rows, up[:, at]))
            act_ref[:, at] = value.astype(BF)
            slope_ref[:, at] = slope.astype(BF)

    outs = [jax.ShapeDtypeStruct((count, hidden), BF)] * 2
    args = [second_in] + weight_up.arrays
    return call(
        kernel, outs, args, "v" + "a" * pieces, weight_up.scratch(), "widen",
        4 * count * hidden * second_in.shape[1], 8 * count * hidden, after,
    )


def dispatch(links, activated, after_attn, small, row_slots, routes, weight_down, total, after):
    count, width = after_attn.shape
    n = links.n
    pieces = len(weight_down.arrays)

    def kernel(act, after, small_ref, slot_r, route_c, *refs):
        down_refs, refs = refs[:pieces], refs[pieces:]
        hidden_ref, gates_ref, sent_ref = refs[:-2]
        down, sems = refs[-2:]
        for copy in weight_down.start(down_refs, down, sems):
            copy.wait()
        hidden = after[...] + mm_t(act[...], down[...])
        hidden_ref[...] = hidden
        normal, _ = normalize(hidden)
        moe_in = normal * small_ref[2:3] + small_ref[5:6]
        lane = lax.broadcasted_iota(I32, (count, n), 1)
        onehot = jnp.where(lane == route_c[...], 1.0, 0.0).astype(BF)
        chosen = mm(onehot, small_ref[6 : 6 + n].astype(BF))
        logit = jnp.sum(moe_in * chosen, axis=1, keepdims=True)
        gates = 1.0 / (1.0 + jnp.exp(-logit))
        gates_ref[...] = gates
        sent = jnp.concatenate([moe_in.astype(BF), scalar_columns(gates)], axis=1)
        place = lax.broadcasted_iota(I32, (total, count), 0)
        to_slots = jnp.where(place == slot_r[...], 1.0, 0.0).astype(BF)
        sent_ref[...] = mm(to_slots, sent).astype(BF)

    shape = jax.ShapeDtypeStruct
    outs = [shape((count, width), F32), shape((count, 1), F32)]
    outs.append(shape((total, width + EXTRA), BF))
    args = [activated, after_attn, small, row_slots, routes] + weight_down.arrays
    return call(
        kernel, outs, args, "vvvvv" + "a" * pieces, weight_down.scratch(), "dispatch",
        4 * count * width * 4 * width, 16 * count * width, after,
    )


def expert_rows(arrived, cots, width, after):
    total = arrived.shape[0]

    def kernel(arrived_ref, cot_ref, rows_ref, grads_ref, rows_across, grads_across):
        rows = arrived_ref[:, :width]
        rows_ref[...] = rows
        rows_across[...] = rows.T
        gates = columns_scalar(arrived_ref[:, width:])
        grads = (gates * cot_ref[...].astype(F32)).astype(BF)
        grads_ref[...] = grads
        grads_across[...] = grads.T

    outs = [jax.ShapeDtypeStruct((total, width), BF)] * 2 + [jax.ShapeDtypeStruct((width, total), BF)] * 2
    return call(kernel, outs, [arrived, cots], "vv", [], "expert_rows", 0, 0, after)


def expert(rows, grads, across, weights, sums, cot):
    total, width = rows.shape
    m, _, _, wide = weights.shape
    last, started = cot is not None, sums is not None

    def kernel(rows_ref, grads_ref, rows_across, grads_across, *refs):
        refs = list(refs)
        take = lambda k: [refs.pop(0) for _ in range(k)]
        carried = take(2) if started else None
        (cot_ref,) = take(1) if last else (None,)
        (weight_ref,) = take(1)
        (w_grads,) = take(1)
        outs = take(2)
        held, grad_held, sems, out_sems, out_sum, row_sum = refs
        entering = [pltpu.make_async_copy(weight_ref.at[i], held.at[i], sems.at[i]) for i in range(m)]
        for copy in entering:
            copy.start()
        r, g = rows_ref[...], grads_ref[...]
        leaving = []
        for i in range(m):
            entering[i].wait()
            up, down = held[i, 0], held[i, 1]
            value, slope = smooth_and_slope(mm(r, up))
            act = value.astype(BF)
            pre_grad = (mm(g, down) * slope).astype(BF)
            row_part, out_part = mm_t(pre_grad, up), mm_t(act, down)
            if i == 0 and started:
                row_part, out_part = row_part + carried[0][...], out_part + carried[1][...]
            if i > 0:
                row_part, out_part = row_part + row_sum[...], out_part + out_sum[...]
            row_sum[...] = row_part
            out_sum[...] = out_part
            grad_held[i, 0] = mm(rows_across[...], pre_grad).astype(BF)
            grad_held[i, 1] = mm(grads_across[...], act).astype(BF)
            copy = pltpu.make_async_copy(grad_held.at[i], w_grads.at[i], out_sems.at[i])
            copy.start()
            leaving.append(copy)
        if last:
            result = out_sum[...].astype(BF)
            gate_grad = jnp.sum(cot_ref[...].astype(F32) * result.astype(F32), axis=1, keepdims=True)
            outs[0][...] = jnp.concatenate([row_sum[...].astype(BF), scalar_columns(gate_grad)], axis=1)
            outs[1][...] = result
        else:
            outs[0][...] = row_sum[...]
            outs[1][...] = out_sum[...]
        for copy in leaving:
            copy.wait()

    shape = jax.ShapeDtypeStruct
    args = [rows, grads, *across] + (sums if started else []) + ([cot] if last else [])
    spaces = "v" * len(args) + "a"
    outs = [shape((m, 2, width, wide), BF)]
    if last:
        outs += [shape((total, width + EXTRA), BF), shape((total, width), BF)]
    else:
        outs += [shape((total, width), F32)] * 2
    scratch = [
        pltpu.VMEM((m, 2, width, wide), BF), pltpu.VMEM((m, 2, width, wide), BF),
        pltpu.SemaphoreType.DMA((m,)), pltpu.SemaphoreType.DMA((m,)),
        pltpu.VMEM((total, width), F32), pltpu.VMEM((total, width), F32),
    ]
    return call(kernel, outs, args + [weights], spaces, scratch, "expert", 0, 0, [], "avv")


def combine(returned, slots, hidden, gates):
    count, width = hidden.shape

    def kernel(slot_c, hidden_ref, gates_ref, got_ref, out):
        got = got_ref[...]
        place = lax.broadcasted_iota(I32, (count, got.shape[0]), 1)
        pick = jnp.where(place == slot_c[...], 1.0, 0.0).astype(BF)
        out[...] = (hidden_ref[...] + gates_ref[...] * mm(pick, got)).astype(BF)

    return call(
        kernel, [jax.ShapeDtypeStruct((count, width), BF)], [slots, hidden, gates, returned],
        "vvvv", [], "combine", 4 * count * count * width, 10 * count * width,
    )[0]


def gate_back(links, back, slots, routes, hidden, gates, small, cotangent, activated):
    count, width = hidden.shape
    n = links.n
    size = width // n
    units = activated.shape[1]

    def kernel(slot_c, route_c, hidden_ref, gates_ref, small_ref, cot, act, back_ref, *refs):
        got = back_ref[...]
        hidden_grad_ref, down_in_ref, small_out, centroid_out, *sums = refs[:-1]
        whole = refs[-1]
        place = lax.broadcasted_iota(I32, (count, got.shape[0]), 1)
        pick = jnp.where(place == slot_c[...], 1.0, 0.0).astype(BF)
        got = mm(pick, got)
        gates = gates_ref[...]
        logit_grad = columns_scalar(got[:, width:]) * gates * (1.0 - gates)
        lane = lax.broadcasted_iota(I32, (count, n), 1)
        onehot = jnp.where(lane == route_c[...], 1.0, 0.0).astype(BF)
        chosen = mm(onehot, small_ref[6 : 6 + n].astype(BF))
        normal, inverse = normalize(hidden_ref[...])
        gain = small_ref[2:3]
        moe_in = normal * gain + small_ref[5:6]
        terms = split3(logit_grad * moe_in)
        centroid_out[...] = t_mm(onehot, terms[0]) + t_mm(onehot, terms[1]) + t_mm(onehot, terms[2])
        moe_grad = got[:, :width] + logit_grad * chosen
        part, gain_grad, shift_grad = normalize_back(moe_grad, normal, inverse, gain)
        small_out[...] = jnp.concatenate([gain_grad, shift_grad], axis=0)
        hidden_grad = cot[...].astype(F32) + part
        hidden_grad_ref[...] = hidden_grad
        down_in = hidden_grad.astype(BF)
        down_in_ref[...] = down_in
        whole[...] = t_mm(down_in, act[...]).astype(BF)
        links.write_sum(sums, whole, 0, size)

    shape = jax.ShapeDtypeStruct
    outs = [
        shape((count, width), F32), shape((count, width), BF), shape((2, width), F32), shape((n, width), F32),
    ] + links.sum_shapes(size, units)
    args = [slots, routes, hidden, gates, small, cotangent, activated, back]
    hidden_grad, down_in, small_out, centroid_out, *sums = call(
        kernel, outs, args, "v" * len(args), [pltpu.VMEM((width, units), BF)], "gate_back",
        2 * count * width * units * 2, 8 * count * units,
    )
    return hidden_grad, down_in, small_out, centroid_out, sums


def widen_back(links, down_in, slope, second_in, weight_down):
    count, width = down_in.shape
    units = slope.shape[1]
    size = units // links.n
    pieces = len(weight_down.arrays)

    def kernel(down_in_ref, slope_ref, second, *refs):
        down_refs, refs = refs[:pieces], refs[pieces:]
        grad, *sums = refs[:-3]
        down, sems, whole = refs[-3:]
        for copy in weight_down.start(down_refs, down, sems):
            copy.wait()
        rows = down_in_ref[...]
        part = units // 4
        for i in range(4):
            at = pl.ds(i * part, part)
            piece = (mm(rows, down[:, at]) * slope_ref[:, at].astype(F32)).astype(BF)
            grad[:, at] = piece
            whole[at] = t_mm(piece, second[...]).astype(BF)
        links.write_sum(sums, whole, 0, size)

    outs = [jax.ShapeDtypeStruct((count, units), BF)] + links.sum_shapes(size, width)
    args = [down_in, slope, second_in]
    spaces = "vvv" + "a" * pieces
    scratch = weight_down.scratch() + [pltpu.VMEM((units, width), BF)]
    grad, *sums = call(
        kernel, outs, args + weight_down.arrays, spaces, scratch, "widen_back",
        4 * count * width * units, 8 * width * units,
    )
    return grad, sums


def second_back(links, widened_grad, after_attn, hidden_grad, mixed, small, weight_up, after):
    count, width = after_attn.shape
    n = links.n
    size = width // n
    pieces = len(weight_up.arrays)

    def kernel(grad, after_ref, hidden_grad_ref, mixed_ref, small_ref, *refs):
        up_refs, refs = refs[:pieces], refs[pieces:]
        after_grad_ref, attn_grad_ref, small_out, *sums = refs[:-3]
        up, sems, whole = refs[-3:]
        copies = weight_up.start(up_refs, up, sems)
        normal, inverse = normalize(after_ref[...])
        for copy in copies:
            copy.wait()
        second_grad = mm_t(grad[...], up[...])
        back, gain_grad, shift_grad = normalize_back(second_grad, normal, inverse, small_ref[1:2])
        small_out[...] = jnp.concatenate([gain_grad, shift_grad], axis=0)
        after_grad = hidden_grad_ref[...] + back
        after_grad_ref[...] = after_grad
        attn_grad = after_grad.astype(BF)
        attn_grad_ref[...] = attn_grad
        whole[...] = t_mm(attn_grad, mixed_ref[...]).astype(BF)
        links.write_sum(sums, whole, 0, size)

    shape = jax.ShapeDtypeStruct
    outs = [shape((count, width), F32), shape((count, width), BF), shape((2, width), F32)]
    outs += links.sum_shapes(size, width)
    args = [widened_grad, after_attn, hidden_grad, mixed, small]
    spaces = "vvvvv" + "a" * pieces
    scratch = weight_up.scratch() + [pltpu.VMEM((width, width), BF)]
    after_grad, attn_grad, small_out, *sums = call(
        kernel, outs, args + weight_up.arrays, spaces, scratch, "second_back",
        2 * count * width * 4 * width, 8 * width * 4 * width, after,
    )
    return after_grad, attn_grad, small_out, sums


def attend_back(attn_grad, projected, lse, segments, weight_out, after):
    count, width = attn_grad.shape
    pairs = width // (2 * HEAD_DIM)
    block = 128
    blocks = count // block
    n_out = len(weight_out.arrays)

    def kernel(attn_ref, proj, lse, seg_c, seg_r, *refs):
        out_refs, refs = refs[:n_out], refs[n_out:]
        grad, w_out, out_sems, bias, mixed_grad = refs
        copies = weight_out.start(out_refs, w_out, out_sems)
        bias[...] = bias_of(seg_c[...], seg_r[...])
        for copy in copies:
            copy.wait()
        mixed_grad[...] = mm(attn_ref[...], w_out[...]).astype(BF)
        masks = half_masks()
        lane = lax.broadcasted_iota(I32, (block, 128), 1)

        def pair(i, carry):
            at = [pl.ds(pl.multiple_of(part * width + 128 * i, 128), 128) for part in range(3)]
            k_grad = [jnp.zeros((block, 128), F32) for _ in range(blocks)]
            v_grad = [jnp.zeros((block, 128), F32) for _ in range(blocks)]
            for b in range(blocks):
                mine, keys = pl.ds(b * block, block), pl.ds(0, (b + 1) * block)
                q, k, v = proj[mine, at[0]] * 0.125, proj[keys, at[1]], proj[keys, at[2]]
                upper = mixed_grad[mine, at[0]]
                kept = lse[mine]
                q_grad = jnp.zeros((block, 128), F32)
                for h in range(2):
                    q_h, upper_h = q * masks[h], upper * masks[h]
                    log_total = jnp.sum(jnp.where(lane == 2 * i + h, kept, 0.0), axis=1, keepdims=True)
                    probs = jnp.exp(mm_t(q_h, k) + bias[mine, keys] - log_total)
                    probs_grad = mm_t(upper_h, v)
                    mean = jnp.sum(probs * probs_grad, axis=1, keepdims=True)
                    scores_grad = (probs * (probs_grad - mean)).astype(BF)
                    q_grad += mm(scores_grad, k * masks[h])
                    dv = t_mm(probs.astype(BF), upper_h)
                    dk = t_mm(scores_grad, q_h)
                    for c in range(b + 1):
                        v_grad[c] += dv[c * block : (c + 1) * block]
                        k_grad[c] += dk[c * block : (c + 1) * block]
                grad[mine, at[0]] = (q_grad * 0.125).astype(BF)
            for c in range(blocks):
                mine = pl.ds(c * block, block)
                grad[mine, at[1]] = k_grad[c].astype(BF)
                grad[mine, at[2]] = v_grad[c].astype(BF)
            return carry

        lax.fori_loop(0, pairs, pair, 0)

    args = [attn_grad, projected, lse, segments.reshape(count, 1), segments]
    spaces = "v" * len(args) + "a" * n_out
    scratch = weight_out.scratch() + [pltpu.VMEM((count, count), F32), pltpu.VMEM((count, width), BF)]
    return call(
        kernel, [jax.ShapeDtypeStruct((count, 3 * width), BF)], args + weight_out.arrays, spaces, scratch,
        "attend_back", 2 * count * width * (width + 5 * count) * 2, 12 * count * width * 4, after,
    )[0]


def project_back(links, projected_grad, first_in, after):
    width = first_in.shape[1]
    size = 3 * width // links.n

    def kernel(grad, first, *refs):
        whole = refs[-1]
        whole[...] = t_mm(grad[...], first[...]).astype(BF)
        links.write_sum(refs[:-1], whole, 0, size)

    return call(
        kernel, links.sum_shapes(size, width), [projected_grad, first_in], "vv",
        [pltpu.VMEM((3 * width, width), BF)], "project_back", 6 * width**3, 12 * width * width, after,
    )


def tokens_back(links, projected_grad, tokens, after_grad, small, smalls, centroid_grad, weight_in, after):
    count, width = tokens.shape
    n, n_in = links.n, len(weight_in.arrays)
    cols, rows = width // n, small.shape[0]

    def kernel(grad, tok, after_ref, small_ref, small_2, small_3, centroids, *refs):
        in_refs, refs = refs[:n_in], refs[n_in:]
        out, *sums = refs[:-2]
        w_in, sems = refs[-2:]
        copies = weight_in.start(in_refs, w_in, sems)
        normal, inverse = normalize(tok[...].astype(F32))
        for copy in copies:
            copy.wait()
        first_grad = mm(grad[...], w_in[...])
        back, gain_grad, shift_grad = normalize_back(first_grad, normal, inverse, small_ref[0:1])
        out[...] = after_ref[...] + back
        parts = [gain_grad, small_2[0:1], small_3[0:1], shift_grad, small_2[1:2], small_3[1:2]]
        parts += [centroids[...], jnp.zeros((rows - 6 - n, width), F32)]
        both = jnp.concatenate(parts, axis=0).astype(BF)
        me = lax.axis_index("expert") if links.cube else 0
        source = lax.broadcasted_iota(I32, (128, width), 0)
        place = lax.broadcasted_iota(I32, (128, width), 1)
        for k in range(n):
            mine = (place == source + (me ^ k) * cols) & (source < cols)
            block = mm_t(both, jnp.where(mine, 1.0, 0.0).astype(BF)).astype(BF)
            ref, i = (sums[k % 2], k // 2) if links.cube else (sums[0], k)
            ref[i] = jnp.zeros((rows, width), BF)
            ref[i, :, :128] = block

    outs = [jax.ShapeDtypeStruct((count, width), F32)] + links.sum_shapes(rows, width)
    args = [projected_grad, tokens, after_grad, small, *smalls, centroid_grad]
    out, *sums = call(
        kernel, outs, args + weight_in.arrays, "v" * len(args) + "a" * n_in, weight_in.scratch(),
        "tokens_back", 6 * count * width * width, 20 * count * width, after,
    )
    return out, sums


def on_device(
    n, m, tokens, segments, routes, norm_gains, norm_shifts, project_in, project_out,
    dense_up, dense_down, centroids, expert_up, expert_down, cotangent,
):
    count, width = tokens.shape
    BEFORE.clear()
    capacity = 2 * count // n
    total = n * capacity
    own_hidden = expert_up.shape[2]
    links = Links(n, m)
    cols = width // n

    def chunk(start, wide):
        part = slice(start, start + wide)
        return jnp.concatenate([expert_up[0][:, part], expert_down[0][:, part]], axis=0)

    chunks = [512, 256] if own_hidden == 768 and m == 4 else [own_hidden]
    gathered, start = [], 0
    for wide in chunks:
        whole = lax.all_gather(chunk(start, wide), "dp", axis=0, tiled=True)
        gathered.append(whole.reshape(m, 2, width, wide))
        start += wide

    pad = -(6 + n) % 16
    small = jnp.concatenate([norm_gains, norm_shifts, centroids], axis=0)
    small = jnp.pad(small, ((0, pad), (0, width - cols)))
    group = [project_in.T, project_out.T, small]
    started = links.start(jnp.concatenate(group, axis=0))
    weight_in, weight_out, weight_small = links.by_rows([a.shape[0] for a in group], started)
    started_up = links.start(dense_up, links.second)
    started_down = links.start(dense_down.T, links.second)

    row_slots, slots, cots = prepare(links, routes, cotangent, capacity)
    first_in, projected, mixed, lse, after_attn, second_in, small = attend(
        n, tokens, segments, weight_small, weight_in, weight_out, []
    )
    weight_up = links.by_columns(started_up, [small])
    (weight_down,) = links.by_rows([cols], started_down, [small])
    cots = links.exchange(cots, links.second)
    activated, slope = widen(second_in, weight_up, [])
    hidden, gates, sent = dispatch(
        links, activated, after_attn, small, row_slots, routes, weight_down, total, [cots]
    )
    rows, grads, *across = expert_rows(links.exchange(sent), cots, width, [])

    sums, expert_sums = None, []
    for c, whole in enumerate(gathered):
        last = c == len(chunks) - 1
        w_grads, *sums = expert(rows, grads, across, whole, sums, cots if last else None)
        expert_sums.append(w_grads)
    back, results = sums

    def own_sum(grads):
        sums = lax.psum_scatter(grads.reshape(-1, grads.shape[-1]), "dp", scatter_dimension=0, tiled=True)
        return sums.reshape(grads.shape[1:])

    summed = [own_sum(expert_sums[0])]
    back = links.exchange(back)
    returned = links.exchange(results, [back])

    hidden_grad, down_in, small_3, centroid_grad, sums_down = gate_back(
        links, back, slots, routes, hidden, gates, small, cotangent, activated
    )
    twin_down = links.twins(sums_down)
    widened_grad, sums_up = widen_back(links, down_in, slope, second_in, weight_down)
    twin_up = links.twins(sums_up)
    down = links.fold([sums_down], twin_down, [returned])
    down_got = links.across(down)
    after_grad, attn_grad, small_2, sums_out = second_back(
        links, widened_grad, after_attn, hidden_grad, mixed, small, weight_up, []
    )
    twin_out = links.twins(sums_out)
    projected_grad = attend_back(attn_grad, projected, lse, segments, weight_out, [])
    up = links.fold([sums_up, sums_out], twin_up + twin_out)
    up_got = links.across(up)
    down = links.fold_again(down, down_got)
    down_got = links.across_again(down)
    tokens_grad, sums_small = tokens_back(
        links, projected_grad, tokens, after_grad, small, [small_2, small_3], centroid_grad, weight_in, []
    )
    twin_small = links.twins(sums_small)
    for grads in expert_sums[1:]:
        summed.append(own_sum(links.gated(grads, summed + [sums_small[0]])))
    sums_in = project_back(links, projected_grad, first_in, [])
    twin_in = links.twins(sums_in)
    inner = links.fold([sums_in, sums_small], twin_in + twin_small)
    inner_got = links.across(inner)
    down = links.fold_last(down, down_got)
    down_got = links.inward(down)
    up = links.fold_again(up, up_got)
    up_got = links.across_again(up)
    inner = links.fold_again(inner, inner_got)
    inner_got = links.across_again(inner)
    up = links.fold_last(up, up_got)
    up_got = links.inward(up)
    inner = links.fold_last(inner, inner_got)
    inner_got = links.inward(inner)
    output = combine(returned, slots, hidden, gates)
    down = links.joined(down, down_got)
    down_got = links.middle(down)
    down = links.joined(down, down_got)
    down_got = links.outward(down)
    up = links.joined(up, up_got)
    up_got = links.middle(up)
    inner = links.joined(inner, inner_got)
    inner_got = links.middle(inner)
    up = links.joined(up, up_got)
    up_got = links.outward(up)
    inner = links.joined(inner, inner_got)
    inner_got = links.outward(inner)
    expert_sums = finish(summed)
    units, columns = dense_up.shape[1], project_in.shape[1]
    down_sum = links.settled(down, down_got)
    up_sum, out_sum = links.settled_across(up, up_got, units)
    inner_sum = links.settled(inner, inner_got)
    small_sum = inner_sum[columns:, :cols]

    return (
        output, tokens_grad, small_sum[:3], small_sum[3:6], inner_sum[:columns].T, out_sum.T, up_sum,
        down_sum.T, small_sum[6 : 6 + n], expert_sums[0][None], expert_sums[1][None],
    )


def solution(mesh):
    sizes = dict(mesh.shape)
    both, over = P(("dp", "expert"), None), P(None, "expert")
    expert_place = P("expert", None, "dp")
    return jax.shard_map(
        functools.partial(on_device, sizes["expert"], sizes["dp"]),
        mesh=mesh,
        in_specs=(both,) * 3 + (over,) * 7 + (expert_place,) * 2 + (both,),
        out_specs=(both,) * 2 + (over,) * 7 + (expert_place,) * 2,
        check_vma=False,
    )
```

```python
import functools

import jax
import jax.numpy as jnp
from jax import lax
from jax.experimental import pallas as pl
from jax.experimental.pallas import tpu as pltpu
from jax.sharding import PartitionSpec as P

HEAD_DIM = 64
EXTRA = 128
BF = jnp.bfloat16
F32 = jnp.float32
I32 = jnp.int32
ROOT = 0.7978845608028654
COST = dict(
    prepare=3, attend=16, widen=9, dispatch=10, expert_rows=4, expert=20, expert_last=10, expert_grads=6, gate_back=10, widen_back=12, fold=1,
    second_back=17, attend_back=2, fold_again=1, fold_wait=12, project_back=2, tokens_back=2, fold_last=1, joined=1,
    combine=1, finish=1, settle=1,
)
WIDE = ("attend", "widen", "dispatch", "expert", "expert_last", "widen_back", "settle")
VMEM_LIMIT = 60 * 1024 * 1024


def mm(left, right):
    return lax.dot_general(left, right, (((1,), (0,)), ((), ())), preferred_element_type=F32)


def mm_t(left, right):
    return lax.dot_general(left, right, (((1,), (1,)), ((), ())), preferred_element_type=F32)


def t_mm(left, right):
    return lax.dot_general(left, right, (((0,), (0,)), ((), ())), preferred_element_type=F32)


def normalize(rows):
    share = 1.0 / rows.shape[-1]
    centred = rows - jnp.sum(rows, axis=-1, keepdims=True) * share
    spread = jnp.sum(centred * centred, axis=-1, keepdims=True) * share
    inverse = lax.rsqrt(spread + 1e-05)
    return centred * inverse, inverse


def normalize_back(grad, normal, inverse, gain):
    share = 1.0 / grad.shape[-1]
    scaled = grad * gain
    first = jnp.sum(scaled, axis=-1, keepdims=True) * share
    second = jnp.sum(scaled * normal, axis=-1, keepdims=True) * share
    rows = inverse * (scaled - first - normal * second)
    return rows, jnp.sum(grad * normal, axis=0, keepdims=True), jnp.sum(grad, axis=0, keepdims=True)


def smooth_and_slope(v):
    square = v * v
    bend = jnp.tanh(v * (ROOT + ROOT * 0.044715 * square))
    half = 0.5 + 0.5 * bend
    slope = half + 0.5 * v * (1.0 - bend * bend) * (ROOT + 3.0 * ROOT * 0.044715 * square)
    return v * half, slope


def split3(v):
    hi = v.astype(BF)
    rest = v - hi.astype(F32)
    mid = rest.astype(BF)
    return hi, mid, (rest - mid.astype(F32)).astype(BF)


def scalar_columns(v):
    hi, mid, low = split3(v)
    lane = lax.broadcasted_iota(I32, (v.shape[0], EXTRA), 1)
    out = jnp.where(lane == 0, hi.astype(F32), 0.0)
    out = jnp.where(lane == 1, mid.astype(F32), out)
    return jnp.where(lane == 2, low.astype(F32), out).astype(BF)


def columns_scalar(columns):
    return jnp.sum(columns.astype(F32), axis=-1, keepdims=True)


def bias_of(by_row, by_column):
    count = by_row.shape[0]
    row = lax.broadcasted_iota(I32, (count, count), 0)
    column = lax.broadcasted_iota(I32, (count, count), 1)
    allowed = (by_row == by_column) & (row >= column)
    return jnp.where(allowed, 0.0, -1000000000.0)


def half_masks():
    lane = lax.broadcasted_iota(I32, (1, 2 * HEAD_DIM), 1)
    first = jnp.where(lane < HEAD_DIM, 1.0, 0.0)
    return first.astype(BF), (1.0 - first).astype(BF)


BEFORE = []


def smallest(outs):
    return min(outs, key=lambda a: a.size * a.dtype.itemsize)


def call(kernel, outs, args, spaces, scratch, name, flops, moved, after=(), results=None):
    where = {"v": pltpu.VMEM, "a": pl.ANY}
    after = list(after) + BEFORE
    read, waited = len(args), len(after)
    args, spaces = list(args) + list(after), spaces + "a" * waited

    def body(*refs):
        kernel(*refs[:read], *refs[read + waited :])

    got = pl.pallas_call(
        body,
        out_shape=outs,
        in_specs=[pl.BlockSpec(memory_space=where[s]) for s in spaces],
        out_specs=[pl.BlockSpec(memory_space=where[s]) for s in results or "v" * len(outs)],
        scratch_shapes=scratch,
        compiler_params=pltpu.CompilerParams(vmem_limit_bytes=VMEM_LIMIT if name in WIDE else VMEM_LIMIT // 2),
        cost_estimate=pl.CostEstimate(flops=COST[name] * 1150000000, bytes_accessed=1000, transcendentals=0),
        name=name,
    )(*args)
    BEFORE[:] = [smallest(got)]
    return got


class Weight:
    def __init__(self, arrays, copies, shape):
        self.arrays, self.copies, self.shape = arrays, copies, shape

    def scratch(self):
        return [pltpu.VMEM(self.shape, BF), pltpu.SemaphoreType.DMA((len(self.copies),))]

    def start(self, refs, whole, sems):
        me = lax.axis_index("expert")
        running = []
        for i, (index, source, place) in enumerate(self.copies):
            copy = pltpu.make_async_copy(
                refs[index].at[source], whole.at[place(me)], sems.at[i]
            )
            copy.start()
            running.append(copy)
        return running


def row_place(k, size, offset, rows, step):
    def place(me):
        if k is None:
            return (pl.ds(offset, rows),)
        return (pl.ds(pl.multiple_of((me ^ k) * size + offset, step), rows),)

    return place


def column_place(k, size, offset, rows):
    def place(me):
        if k is None:
            return (pl.ds(0, rows),)
        start = pl.multiple_of((me ^ k) * size, 128)
        return (pl.ds(offset, rows), pl.ds(start, size))

    return place


class Links:
    def __init__(self, n, m):
        self.n, self.m = n, m
        self.cube = n == 8
        self.line = m == 4
        self.second = ()

    def hop(self, value, bit):
        return lax.ppermute(value, "expert", [(i, i ^ bit) for i in range(self.n)])

    def gated(self, value, gate):
        return lax.optimization_barrier((value, *gate))[0] if gate else value

    def start(self, shard, gate=()):
        if not self.cube:
            return [shard]
        shard = self.gated(shard, gate)
        return [shard, self.hop(shard, 2), self.hop(shard, 4)]

    def pieces(self, started, gate=()):
        shard, by_x, by_y = lax.optimization_barrier((*started, *gate))[:3] if gate else started
        half = shard.shape[0] // 2 // 16 * 16
        far_a = self.hop(by_y[:half], 2)
        far_b = self.hop(by_x[half:], 4)
        self.second = (far_a, far_b)
        return [
            (0, 0, shard), (1, 0, self.hop(shard, 1)), (2, 0, by_x), (3, 0, self.hop(by_x, 1)),
            (4, 0, by_y), (5, 0, self.hop(by_y, 1)), (6, 0, far_a), (6, half, far_b),
            (7, 0, self.hop(far_a, 1)), (7, half, self.hop(far_b, 1)),
        ]

    def by_rows(self, sizes, started, gate=()):
        group = started[0]
        weights, first = [], 0
        if not self.cube:
            whole = lax.all_gather(group, "expert", axis=0, tiled=False)
            for size in sizes:
                part = whole[:, first : first + size].reshape(-1, group.shape[1])
                copies = [(0, (pl.ds(0, part.shape[0]),), row_place(None, 0, 0, part.shape[0], 8))]
                weights.append(Weight([part], copies, part.shape))
                first += size
            return weights
        pieces = self.pieces(started, gate)
        for size in sizes:
            arrays, copies = [], []
            for k, row, array in pieces:
                low, high = max(first, row), min(first + size, row + array.shape[0])
                if low < high:
                    source = (pl.ds(low - row, high - low),)
                    place = row_place(k, size, low - first, high - low, 16 if size % 16 == 0 else 8)
                    copies.append((len(arrays), source, place))
                    arrays.append(array)
            weights.append(Weight(arrays, copies, (self.n * size, group.shape[1])))
            first += size
        return weights

    def by_columns(self, started, gate=()):
        shard = started[0]
        rows, size = shard.shape
        if not self.cube:
            whole = lax.all_gather(shard, "expert", axis=1, tiled=True)
            return Weight([whole], [(0, (pl.ds(0, rows),), column_place(None, 0, 0, rows))], whole.shape)
        arrays, copies = [], []
        for k, row, array in self.pieces(started, gate):
            source = (pl.ds(0, array.shape[0]),)
            copies.append((len(arrays), source, column_place(k, size, row, array.shape[0])))
            arrays.append(array)
        return Weight(arrays, copies, (rows, self.n * size))

    def exchange(self, rows, gate=()):
        blocks = self.gated(rows, gate).reshape(self.n, -1, rows.shape[1])
        got = lax.all_to_all(blocks, "expert", split_axis=0, concat_axis=0, tiled=True)
        return got.reshape(rows.shape)

    def sum_shapes(self, rows, width):
        if not self.cube:
            return [jax.ShapeDtypeStruct((self.n, rows, width), BF)]
        return [jax.ShapeDtypeStruct((self.n // 2, rows, width), BF)] * 2

    def write_sum(self, refs, whole, first, size):
        for k in range(self.n):
            if self.cube:
                me = lax.axis_index("expert")
                step = 16 if size % 16 == 0 else 8
                start = pl.multiple_of((me ^ k) * size, step)
                refs[k % 2][k // 2, first : first + size] = whole[pl.ds(start, size)]
            else:
                refs[0][k, first : first + size] = whole[k * size : (k + 1) * size]

    def twins(self, blocks):
        return [self.hop(blocks[1], 1)] if self.cube else []

    def fold(self, groups, twins, after=()):
        if not self.cube:
            return [jnp.concatenate([g[0] for g in groups], axis=1)]
        rows = [g[0].shape[1] for g in groups]
        total, columns = sum(rows), groups[0][0].shape[2]
        half = total // 2 // 16 * 16

        def kernel(*refs):
            count = len(groups)
            outs = refs[2 * count :]
            first = 0
            for even, odd in zip(refs[:count], refs[count : 2 * count]):
                for m in range(4):
                    value = (even[m].astype(F32) + odd[m].astype(F32)).astype(BF)
                    low, high = first, first + even.shape[1]
                    cut = min(max(half, low), high)
                    if low < cut:
                        outs[m % 2][m // 2, low:cut] = value[: cut - low]
                    if cut < high:
                        outs[2 + m // 2][m % 2, cut - half : high - half] = value[cut - low :]
                first += even.shape[1]

        outs = [jax.ShapeDtypeStruct((2, half, columns), BF)] * 2
        outs += [jax.ShapeDtypeStruct((2, total - half, columns), BF)] * 2
        args = [g[0] for g in groups] + list(twins)
        return list(call(kernel, outs, args, "v" * len(args), [], "fold", 0, 0, after))

    def across(self, kept):
        return [self.hop(kept[1], 2), self.hop(kept[3], 4)] if self.cube else []

    def fold_again(self, kept, got, name="fold_again"):
        if not self.cube:
            return kept

        def kernel(first, got_first, second, got_second, *outs):
            for i, (mine, other) in enumerate(((first, got_first), (second, got_second))):
                for j in range(2):
                    outs[2 * i + j][...] = (mine[j].astype(F32) + other[j].astype(F32)).astype(BF)

        outs = [jax.ShapeDtypeStruct(a.shape[1:], BF) for a in (kept[0], kept[0], kept[2], kept[2])]
        args = [kept[0], got[0], kept[2], got[1]]
        return list(call(kernel, outs, args, "vvvv", [], name, 0, 0))

    def across_again(self, kept):
        return [self.hop(kept[1], 4), self.hop(kept[3], 2)] if self.cube else []

    def fold_last(self, kept, got):
        if not self.cube:
            return lax.psum_scatter(kept[0], "expert", scatter_dimension=0, tiled=True)[0]
        half = kept[0].shape[0]

        def kernel(first, got_first, second, got_second, out):
            out[:half] = (first[...].astype(F32) + got_first[...].astype(F32)).astype(BF)
            out[half:] = (second[...].astype(F32) + got_second[...].astype(F32)).astype(BF)

        rows = half + kept[2].shape[0]
        outs = [jax.ShapeDtypeStruct((rows, kept[0].shape[1]), BF)]
        return call(kernel, outs, [kept[0], got[0], kept[2], got[1]], "vvvv", [], "fold_last", 0, 0)[0]

    def along(self, value, pairs):
        return lax.ppermute(value, "dp", pairs)

    def inward(self, value):
        return [self.along(value, [(0, 1), (3, 2)])] if self.line else []

    def middle(self, value):
        return [self.along(value, [(1, 2), (2, 1)])] if self.line else []

    def outward(self, value):
        return [self.along(value, [(1, 0), (2, 3)])] if self.line else []

    def joined(self, value, got):
        if not self.line:
            return value

        def kernel(mine, other, out):
            out[...] = (mine[...].astype(F32) + other[...].astype(F32)).astype(BF)

        outs = [jax.ShapeDtypeStruct(value.shape, BF)]
        return call(kernel, outs, [value, got[0]], "vv", [], "joined", 0, 0)[0]

    def settled(self, value, got):
        if not self.line:
            return lax.psum(value, "dp").astype(F32)

        def kernel(mine, other, out):
            place = lax.axis_index("dp")

            def write(ref):
                out[...] = ref[...].astype(F32)

            middle = (place == 1) | (place == 2)
            pl.when(middle)(lambda: write(mine))
            pl.when(jnp.logical_not(middle))(lambda: write(other))

        outs = [jax.ShapeDtypeStruct(value.shape, F32)]
        return call(kernel, outs, [value, got[0]], "vv", [], "settle", 0, 0)[0]

    def settled_across(self, value, got, units):
        if not self.line:
            value = lax.psum(value, "dp").astype(F32)
            return value[:units].T, value[units:]

        def kernel(mine, other, up, out):
            place = lax.axis_index("dp")

            def write(ref):
                up[...] = ref[:units].astype(F32).T
                out[...] = ref[units:].astype(F32)

            middle = (place == 1) | (place == 2)
            pl.when(middle)(lambda: write(mine))
            pl.when(jnp.logical_not(middle))(lambda: write(other))

        rows, width = value.shape
        outs = [jax.ShapeDtypeStruct((width, units), F32), jax.ShapeDtypeStruct((rows - units, width), F32)]
        return call(kernel, outs, [value, got[0]], "vv", [], "settle", 0, 0)


def finish(parts):
    width = parts[0].shape[1]

    def kernel(*refs):
        ups, downs = refs[-2:]
        first = 0
        for ref in refs[:-2]:
            for i, out in enumerate((ups, downs)):
                out[:, first : first + ref.shape[2]] = ref[i].astype(F32)
            first += ref.shape[2]

    outs = [jax.ShapeDtypeStruct((width, sum(p.shape[2] for p in parts)), F32)] * 2
    return call(kernel, outs, parts, "v" * len(parts), [], "finish", 0, 0)


def prepare(links, routes, cotangent, capacity):
    count, width = cotangent.shape
    n = links.n
    total = n * capacity

    def kernel(by_row, by_column, cot, row_out, column_out, out):
        route_c, route_r = by_row[...], by_column[...]
        token = lax.broadcasted_iota(I32, (count, count), 0)
        other = lax.broadcasted_iota(I32, (count, count), 1)
        same = route_c == route_r
        rank_c = jnp.sum(jnp.where(same & (other < token), 1.0, 0.0), axis=1, keepdims=True)
        rank_r = jnp.sum(jnp.where(same & (token < other), 1.0, 0.0), axis=0, keepdims=True)
        slot_c = route_c * capacity + rank_c.astype(I32)
        slot_r = route_r * capacity + rank_r.astype(I32)
        column_out[...] = slot_c
        row_out[...] = slot_r
        place = lax.broadcasted_iota(I32, (total, count), 0)
        to_slots = jnp.where(place == slot_r, 1.0, 0.0).astype(BF)
        out[...] = mm(to_slots, cot[...]).astype(BF)

    outs = [jax.ShapeDtypeStruct((1, count), I32), jax.ShapeDtypeStruct((count, 1), I32)]
    outs.append(jax.ShapeDtypeStruct((total, width), BF))
    args = [routes, routes.reshape(1, count), cotangent]
    return call(
        kernel, outs, args, "vvv", [], "prepare", 2 * total * count * width, 4 * total * width
    )


def attend(n, tokens, segments, weight_small, weight_in, weight_out, after):
    count, width = tokens.shape
    pairs = width // (2 * HEAD_DIM)
    block = 128
    n_small, n_in, n_out = len(weight_small.arrays), len(weight_in.arrays), len(weight_out.arrays)
    small_rows, cols = weight_small.shape[0] // n, width // n

    def kernel(tok, seg_c, seg_r, *refs):
        small_refs, refs = refs[:n_small], refs[n_small:]
        in_refs, refs = refs[:n_in], refs[n_in:]
        out_refs, refs = refs[:n_out], refs[n_out:]
        first_ref, proj, mixed, lse, after_ref, second_ref, small_ref = refs[:7]
        w_small, small_sems, w_in, in_sems, w_out, out_sems, bias = refs[7:]
        small_copies = weight_small.start(small_refs, w_small, small_sems)
        in_copies = weight_in.start(in_refs, w_in, in_sems)
        out_copies = weight_out.start(out_refs, w_out, out_sems)
        rows = tok[...].astype(F32)
        normal, _ = normalize(rows)
        source = lax.broadcasted_iota(I32, (cols, width), 0)
        place = lax.broadcasted_iota(I32, (cols, width), 1)
        for copy in small_copies:
            copy.wait()
        small = jnp.zeros((small_rows, width), F32)
        for j in range(n):
            spread = jnp.where(place == source + j * cols, 1.0, 0.0).astype(BF)
            small += mm(w_small[j * small_rows : (j + 1) * small_rows, :cols], spread)
        small_ref[...] = small
        first = (normal * small_ref[0:1] + small_ref[3:4]).astype(BF)
        first_ref[...] = first
        bias[...] = bias_of(seg_c[...], seg_r[...])
        lse[...] = jnp.zeros_like(lse)
        for copy in in_copies:
            copy.wait()
        proj[...] = mm_t(first, w_in[...]).astype(BF)
        masks = half_masks()
        lane = lax.broadcasted_iota(I32, (block, 128), 1)

        def pair(i, carry):
            at = [pl.ds(pl.multiple_of(part * width + 128 * i, 128), 128) for part in range(3)]
            for b in range(count // block):
                mine, keys = pl.ds(b * block, block), pl.ds(0, (b + 1) * block)
                q, k, v = proj[mine, at[0]] * 0.125, proj[keys, at[1]], proj[keys, at[2]]
                got = jnp.zeros((block, 128), F32)
                kept = lse[mine]
                for h in range(2):
                    scores = mm_t(q * masks[h], k) + bias[mine, keys]
                    top = jnp.max(scores, axis=1, keepdims=True)
                    lifted = jnp.exp(scores - top)
                    totals = jnp.sum(lifted, axis=1, keepdims=True)
                    probs = (lifted * (1.0 / totals)).astype(BF)
                    got += mm(probs, v * masks[h])
                    kept = jnp.where(lane == 2 * i + h, top + jnp.log(totals), kept)
                lse[mine] = kept
                mixed[mine, at[0]] = got.astype(BF)
            return carry

        lax.fori_loop(0, pairs, pair, 0)
        for copy in out_copies:
            copy.wait()
        after = rows + mm_t(mixed[...], w_out[...])
        after_ref[...] = after
        normal, _ = normalize(after)
        second_ref[...] = (normal * small_ref[1:2] + small_ref[4:5]).astype(BF)

    shape = jax.ShapeDtypeStruct
    outs = [
        shape((count, width), BF), shape((count, 3 * width), BF), shape((count, width), BF),
        shape((count, 128), F32), shape((count, width), F32), shape((count, width), BF),
        shape((small_rows, width), F32),
    ]
    args = [tokens, segments.reshape(count, 1), segments]
    args += weight_small.arrays + weight_in.arrays + weight_out.arrays
    spaces = "vvv" + "a" * (n_small + n_in + n_out)
    scratch = weight_small.scratch() + weight_in.scratch() + weight_out.scratch() + [pltpu.VMEM((count, count), F32)]
    flops = 2 * count * width * (4 * width + 2 * count) * 2
    return call(kernel, outs, args, spaces, scratch, "attend", flops, 12 * count * width * 4, after)


def widen(second_in, weight_up, after):
    count = second_in.shape[0]
    hidden = weight_up.shape[1]
    pieces = len(weight_up.arrays)
    part = hidden // 4

    def kernel(second, *refs):
        up_refs, (act_ref, slope_ref, up, sems) = refs[:pieces], refs[pieces:]
        for copy in weight_up.start(up_refs, up, sems):
            copy.wait()
        rows = second[...]
        for i in range(4):
            at = pl.ds(i * part, part)
            value, slope = smooth_and_slope(mm(rows, up[:, at]))
            act_ref[:, at] = value.astype(BF)
            slope_ref[:, at] = slope.astype(BF)

    outs = [jax.ShapeDtypeStruct((count, hidden), BF)] * 2
    args = [second_in] + weight_up.arrays
    return call(
        kernel, outs, args, "v" + "a" * pieces, weight_up.scratch(), "widen",
        4 * count * hidden * second_in.shape[1], 8 * count * hidden, after,
    )


def dispatch(links, activated, after_attn, small, row_slots, routes, weight_down, total, after):
    count, width = after_attn.shape
    n = links.n
    pieces = len(weight_down.arrays)

    def kernel(act, after, small_ref, slot_r, route_c, *refs):
        down_refs, refs = refs[:pieces], refs[pieces:]
        hidden_ref, gates_ref, sent_ref = refs[:-2]
        down, sems = refs[-2:]
        for copy in weight_down.start(down_refs, down, sems):
            copy.wait()
        hidden = after[...] + mm_t(act[...], down[...])
        hidden_ref[...] = hidden
        normal, _ = normalize(hidden)
        moe_in = normal * small_ref[2:3] + small_ref[5:6]
        lane = lax.broadcasted_iota(I32, (count, n), 1)
        onehot = jnp.where(lane == route_c[...], 1.0, 0.0).astype(BF)
        chosen = mm(onehot, small_ref[6 : 6 + n].astype(BF))
        logit = jnp.sum(moe_in * chosen, axis=1, keepdims=True)
        gates = 1.0 / (1.0 + jnp.exp(-logit))
        gates_ref[...] = gates
        sent = jnp.concatenate([moe_in.astype(BF), scalar_columns(gates)], axis=1)
        place = lax.broadcasted_iota(I32, (total, count), 0)
        to_slots = jnp.where(place == slot_r[...], 1.0, 0.0).astype(BF)
        sent_ref[...] = mm(to_slots, sent).astype(BF)

    shape = jax.ShapeDtypeStruct
    outs = [shape((count, width), F32), shape((count, 1), F32)]
    outs.append(shape((total, width + EXTRA), BF))
    args = [activated, after_attn, small, row_slots, routes] + weight_down.arrays
    return call(
        kernel, outs, args, "vvvvv" + "a" * pieces, weight_down.scratch(), "dispatch",
        4 * count * width * 4 * width, 16 * count * width, after,
    )


def expert_rows(arrived, cots, width, after):
    total = arrived.shape[0]

    def kernel(arrived_ref, cot_ref, rows_ref, grads_ref, rows_across, grads_across):
        rows = arrived_ref[:, :width]
        rows_ref[...] = rows
        rows_across[...] = rows.T
        gates = columns_scalar(arrived_ref[:, width:])
        grads = (gates * cot_ref[...].astype(F32)).astype(BF)
        grads_ref[...] = grads
        grads_across[...] = grads.T

    outs = [jax.ShapeDtypeStruct((total, width), BF)] * 2 + [jax.ShapeDtypeStruct((width, total), BF)] * 2
    return call(kernel, outs, [arrived, cots], "vv", [], "expert_rows", 0, 0, after)


def expert(rows, grads, across, weights, sums, cot):
    total, width = rows.shape
    m, _, _, wide = weights.shape
    last, started = cot is not None, sums is not None

    def kernel(rows_ref, grads_ref, rows_across, grads_across, *refs):
        refs = list(refs)
        take = lambda k: [refs.pop(0) for _ in range(k)]
        carried = take(2) if started else None
        (cot_ref,) = take(1) if last else (None,)
        (weight_ref,) = take(1)
        if last:
            outs, (acts, pre_grads) = take(2), take(2)
            held, sems, out_sum, row_sum = refs
        else:
            (w_grads,), outs = take(1), take(2)
            held, sems, out_sum, row_sum, grad_held, out_sems = refs
        entering = [pltpu.make_async_copy(weight_ref.at[i], held.at[i], sems.at[i]) for i in range(m)]
        for copy in entering:
            copy.start()
        r, g = rows_ref[...], grads_ref[...]
        leaving = []
        for i in range(m):
            entering[i].wait()
            up, down = held[i, 0], held[i, 1]
            value, slope = smooth_and_slope(mm(r, up))
            act = value.astype(BF)
            pre_grad = (mm(g, down) * slope).astype(BF)
            row_part, out_part = mm_t(pre_grad, up), mm_t(act, down)
            if i == 0 and started:
                row_part, out_part = row_part + carried[0][...], out_part + carried[1][...]
            if i > 0:
                row_part, out_part = row_part + row_sum[...], out_part + out_sum[...]
            row_sum[...] = row_part
            out_sum[...] = out_part
            if last:
                acts[i] = act
                pre_grads[i] = pre_grad
            else:
                grad_held[i, 0] = mm(rows_across[...], pre_grad).astype(BF)
                grad_held[i, 1] = mm(grads_across[...], act).astype(BF)
                copy = pltpu.make_async_copy(grad_held.at[i], w_grads.at[i], out_sems.at[i])
                copy.start()
                leaving.append(copy)
        if last:
            result = out_sum[...].astype(BF)
            gate_grad = jnp.sum(cot_ref[...].astype(F32) * result.astype(F32), axis=1, keepdims=True)
            outs[0][...] = jnp.concatenate([row_sum[...].astype(BF), scalar_columns(gate_grad)], axis=1)
            outs[1][...] = result
        else:
            outs[0][...] = row_sum[...]
            outs[1][...] = out_sum[...]
        for copy in leaving:
            copy.wait()

    shape = jax.ShapeDtypeStruct
    args = [rows, grads, *across] + (sums if started else []) + ([cot] if last else [])
    spaces = "v" * len(args) + "a"
    scratch = [
        pltpu.VMEM((m, 2, width, wide), BF), pltpu.SemaphoreType.DMA((m,)),
        pltpu.VMEM((total, width), F32), pltpu.VMEM((total, width), F32),
    ]
    if last:
        outs = [shape((total, width + EXTRA), BF), shape((total, width), BF)] + [shape((m, total, wide), BF)] * 2
        return call(kernel, outs, args + [weights], spaces, scratch, "expert_last", 0, 0)
    outs = [shape((m, 2, width, wide), BF)] + [shape((total, width), F32)] * 2
    scratch += [pltpu.VMEM((m, 2, width, wide), BF), pltpu.SemaphoreType.DMA((m,))]
    return call(kernel, outs, args + [weights], spaces, scratch, "expert", 0, 0, [], "avv")


def expert_grads(across, acts, pre_grads):
    m, _, wide = acts.shape
    width = across[0].shape[0]

    def kernel(rows_across, grads_across, acts_ref, pre_ref, out):
        for i in range(m):
            out[i, 0] = mm(rows_across[...], pre_ref[i]).astype(BF)
            out[i, 1] = mm(grads_across[...], acts_ref[i]).astype(BF)

    outs = [jax.ShapeDtypeStruct((m, 2, width, wide), BF)]
    return call(kernel, outs, [*across, acts, pre_grads], "vvvv", [], "expert_grads", 0, 0)[0]


def combine(returned, slots, hidden, gates):
    count, width = hidden.shape

    def kernel(slot_c, hidden_ref, gates_ref, got_ref, out):
        got = got_ref[...]
        place = lax.broadcasted_iota(I32, (count, got.shape[0]), 1)
        pick = jnp.where(place == slot_c[...], 1.0, 0.0).astype(BF)
        out[...] = (hidden_ref[...] + gates_ref[...] * mm(pick, got)).astype(BF)

    return call(
        kernel, [jax.ShapeDtypeStruct((count, width), BF)], [slots, hidden, gates, returned],
        "vvvv", [], "combine", 4 * count * count * width, 10 * count * width,
    )[0]


def gate_back(links, back, slots, routes, hidden, gates, small, cotangent, activated):
    count, width = hidden.shape
    n = links.n
    size = width // n
    units = activated.shape[1]

    def kernel(slot_c, route_c, hidden_ref, gates_ref, small_ref, cot, act, back_ref, *refs):
        got = back_ref[...]
        hidden_grad_ref, down_in_ref, small_out, centroid_out, *sums = refs[:-1]
        whole = refs[-1]
        place = lax.broadcasted_iota(I32, (count, got.shape[0]), 1)
        pick = jnp.where(place == slot_c[...], 1.0, 0.0).astype(BF)
        got = mm(pick, got)
        gates = gates_ref[...]
        logit_grad = columns_scalar(got[:, width:]) * gates * (1.0 - gates)
        lane = lax.broadcasted_iota(I32, (count, n), 1)
        onehot = jnp.where(lane == route_c[...], 1.0, 0.0).astype(BF)
        chosen = mm(onehot, small_ref[6 : 6 + n].astype(BF))
        normal, inverse = normalize(hidden_ref[...])
        gain = small_ref[2:3]
        moe_in = normal * gain + small_ref[5:6]
        terms = split3(logit_grad * moe_in)
        centroid_out[...] = t_mm(onehot, terms[0]) + t_mm(onehot, terms[1]) + t_mm(onehot, terms[2])
        moe_grad = got[:, :width] + logit_grad * chosen
        part, gain_grad, shift_grad = normalize_back(moe_grad, normal, inverse, gain)
        small_out[...] = jnp.concatenate([gain_grad, shift_grad], axis=0)
        hidden_grad = cot[...].astype(F32) + part
        hidden_grad_ref[...] = hidden_grad
        down_in = hidden_grad.astype(BF)
        down_in_ref[...] = down_in
        whole[...] = t_mm(down_in, act[...]).astype(BF)
        links.write_sum(sums, whole, 0, size)

    shape = jax.ShapeDtypeStruct
    outs = [
        shape((count, width), F32), shape((count, width), BF), shape((2, width), F32), shape((n, width), F32),
    ] + links.sum_shapes(size, units)
    args = [slots, routes, hidden, gates, small, cotangent, activated, back]
    hidden_grad, down_in, small_out, centroid_out, *sums = call(
        kernel, outs, args, "v" * len(args), [pltpu.VMEM((width, units), BF)], "gate_back",
        2 * count * width * units * 2, 8 * count * units,
    )
    return hidden_grad, down_in, small_out, centroid_out, sums


def widen_back(links, down_in, slope, second_in, weight_down):
    count, width = down_in.shape
    units = slope.shape[1]
    size = units // links.n
    pieces = len(weight_down.arrays)

    def kernel(down_in_ref, slope_ref, second, *refs):
        down_refs, refs = refs[:pieces], refs[pieces:]
        grad, *sums = refs[:-3]
        down, sems, whole = refs[-3:]
        for copy in weight_down.start(down_refs, down, sems):
            copy.wait()
        rows = down_in_ref[...]
        part = units // 4
        for i in range(4):
            at = pl.ds(i * part, part)
            piece = (mm(rows, down[:, at]) * slope_ref[:, at].astype(F32)).astype(BF)
            grad[:, at] = piece
            whole[at] = t_mm(piece, second[...]).astype(BF)
        links.write_sum(sums, whole, 0, size)

    outs = [jax.ShapeDtypeStruct((count, units), BF)] + links.sum_shapes(size, width)
    args = [down_in, slope, second_in]
    spaces = "vvv" + "a" * pieces
    scratch = weight_down.scratch() + [pltpu.VMEM((units, width), BF)]
    grad, *sums = call(
        kernel, outs, args + weight_down.arrays, spaces, scratch, "widen_back",
        4 * count * width * units, 8 * width * units,
    )
    return grad, sums


def second_back(links, widened_grad, after_attn, hidden_grad, mixed, small, weight_up, after):
    count, width = after_attn.shape
    n = links.n
    size = width // n
    pieces = len(weight_up.arrays)

    def kernel(grad, after_ref, hidden_grad_ref, mixed_ref, small_ref, *refs):
        up_refs, refs = refs[:pieces], refs[pieces:]
        after_grad_ref, attn_grad_ref, small_out, *sums = refs[:-3]
        up, sems, whole = refs[-3:]
        copies = weight_up.start(up_refs, up, sems)
        normal, inverse = normalize(after_ref[...])
        for copy in copies:
            copy.wait()
        second_grad = mm_t(grad[...], up[...])
        back, gain_grad, shift_grad = normalize_back(second_grad, normal, inverse, small_ref[1:2])
        small_out[...] = jnp.concatenate([gain_grad, shift_grad], axis=0)
        after_grad = hidden_grad_ref[...] + back
        after_grad_ref[...] = after_grad
        attn_grad = after_grad.astype(BF)
        attn_grad_ref[...] = attn_grad
        whole[...] = t_mm(attn_grad, mixed_ref[...]).astype(BF)
        links.write_sum(sums, whole, 0, size)

    shape = jax.ShapeDtypeStruct
    outs = [shape((count, width), F32), shape((count, width), BF), shape((2, width), F32)]
    outs += links.sum_shapes(size, width)
    args = [widened_grad, after_attn, hidden_grad, mixed, small]
    spaces = "vvvvv" + "a" * pieces
    scratch = weight_up.scratch() + [pltpu.VMEM((width, width), BF)]
    after_grad, attn_grad, small_out, *sums = call(
        kernel, outs, args + weight_up.arrays, spaces, scratch, "second_back",
        2 * count * width * 4 * width, 8 * width * 4 * width, after,
    )
    return after_grad, attn_grad, small_out, sums


def attend_back(attn_grad, projected, lse, segments, weight_out, after):
    count, width = attn_grad.shape
    pairs = width // (2 * HEAD_DIM)
    block = 128
    blocks = count // block
    n_out = len(weight_out.arrays)

    def kernel(attn_ref, proj, lse, seg_c, seg_r, *refs):
        out_refs, refs = refs[:n_out], refs[n_out:]
        grad, w_out, out_sems, bias, mixed_grad = refs
        copies = weight_out.start(out_refs, w_out, out_sems)
        bias[...] = bias_of(seg_c[...], seg_r[...])
        for copy in copies:
            copy.wait()
        mixed_grad[...] = mm(attn_ref[...], w_out[...]).astype(BF)
        masks = half_masks()
        lane = lax.broadcasted_iota(I32, (block, 128), 1)

        def pair(i, carry):
            at = [pl.ds(pl.multiple_of(part * width + 128 * i, 128), 128) for part in range(3)]
            k_grad = [jnp.zeros((block, 128), F32) for _ in range(blocks)]
            v_grad = [jnp.zeros((block, 128), F32) for _ in range(blocks)]
            for b in range(blocks):
                mine, keys = pl.ds(b * block, block), pl.ds(0, (b + 1) * block)
                q, k, v = proj[mine, at[0]] * 0.125, proj[keys, at[1]], proj[keys, at[2]]
                upper = mixed_grad[mine, at[0]]
                kept = lse[mine]
                q_grad = jnp.zeros((block, 128), F32)
                for h in range(2):
                    q_h, upper_h = q * masks[h], upper * masks[h]
                    log_total = jnp.sum(jnp.where(lane == 2 * i + h, kept, 0.0), axis=1, keepdims=True)
                    probs = jnp.exp(mm_t(q_h, k) + bias[mine, keys] - log_total)
                    probs_grad = mm_t(upper_h, v)
                    mean = jnp.sum(probs * probs_grad, axis=1, keepdims=True)
                    scores_grad = (probs * (probs_grad - mean)).astype(BF)
                    q_grad += mm(scores_grad, k * masks[h])
                    dv = t_mm(probs.astype(BF), upper_h)
                    dk = t_mm(scores_grad, q_h)
                    for c in range(b + 1):
                        v_grad[c] += dv[c * block : (c + 1) * block]
                        k_grad[c] += dk[c * block : (c + 1) * block]
                grad[mine, at[0]] = (q_grad * 0.125).astype(BF)
            for c in range(blocks):
                mine = pl.ds(c * block, block)
                grad[mine, at[1]] = k_grad[c].astype(BF)
                grad[mine, at[2]] = v_grad[c].astype(BF)
            return carry

        lax.fori_loop(0, pairs, pair, 0)

    args = [attn_grad, projected, lse, segments.reshape(count, 1), segments]
    spaces = "v" * len(args) + "a" * n_out
    scratch = weight_out.scratch() + [pltpu.VMEM((count, count), F32), pltpu.VMEM((count, width), BF)]
    return call(
        kernel, [jax.ShapeDtypeStruct((count, 3 * width), BF)], args + weight_out.arrays, spaces, scratch,
        "attend_back", 2 * count * width * (width + 5 * count) * 2, 12 * count * width * 4, after,
    )[0]


def project_back(links, projected_grad, first_in, after):
    width = first_in.shape[1]
    size = 3 * width // links.n

    def kernel(grad, first, *refs):
        whole = refs[-1]
        whole[...] = t_mm(grad[...], first[...]).astype(BF)
        links.write_sum(refs[:-1], whole, 0, size)

    return call(
        kernel, links.sum_shapes(size, width), [projected_grad, first_in], "vv",
        [pltpu.VMEM((3 * width, width), BF)], "project_back", 6 * width**3, 12 * width * width, after,
    )


def tokens_back(links, projected_grad, tokens, after_grad, small, smalls, centroid_grad, weight_in, after):
    count, width = tokens.shape
    n, n_in = links.n, len(weight_in.arrays)
    cols, rows = width // n, small.shape[0]

    def kernel(grad, tok, after_ref, small_ref, small_2, small_3, centroids, *refs):
        in_refs, refs = refs[:n_in], refs[n_in:]
        out, *sums = refs[:-2]
        w_in, sems = refs[-2:]
        copies = weight_in.start(in_refs, w_in, sems)
        normal, inverse = normalize(tok[...].astype(F32))
        for copy in copies:
            copy.wait()
        first_grad = mm(grad[...], w_in[...])
        back, gain_grad, shift_grad = normalize_back(first_grad, normal, inverse, small_ref[0:1])
        out[...] = after_ref[...] + back
        parts = [gain_grad, small_2[0:1], small_3[0:1], shift_grad, small_2[1:2], small_3[1:2]]
        parts += [centroids[...], jnp.zeros((rows - 6 - n, width), F32)]
        both = jnp.concatenate(parts, axis=0).astype(BF)
        me = lax.axis_index("expert") if links.cube else 0
        source = lax.broadcasted_iota(I32, (128, width), 0)
        place = lax.broadcasted_iota(I32, (128, width), 1)
        for k in range(n):
            mine = (place == source + (me ^ k) * cols) & (source < cols)
            block = mm_t(both, jnp.where(mine, 1.0, 0.0).astype(BF)).astype(BF)
            ref, i = (sums[k % 2], k // 2) if links.cube else (sums[0], k)
            ref[i] = jnp.zeros((rows, width), BF)
            ref[i, :, :128] = block

    outs = [jax.ShapeDtypeStruct((count, width), F32)] + links.sum_shapes(rows, width)
    args = [projected_grad, tokens, after_grad, small, *smalls, centroid_grad]
    out, *sums = call(
        kernel, outs, args + weight_in.arrays, "v" * len(args) + "a" * n_in, weight_in.scratch(),
        "tokens_back", 6 * count * width * width, 20 * count * width, after,
    )
    return out, sums


def on_device(
    n, m, tokens, segments, routes, norm_gains, norm_shifts, project_in, project_out,
    dense_up, dense_down, centroids, expert_up, expert_down, cotangent,
):
    count, width = tokens.shape
    BEFORE.clear()
    capacity = 2 * count // n
    total = n * capacity
    own_hidden = expert_up.shape[2]
    links = Links(n, m)
    cols = width // n

    def chunk(start, wide):
        part = slice(start, start + wide)
        return jnp.concatenate([expert_up[0][:, part], expert_down[0][:, part]], axis=0)

    chunks = [512, 256] if own_hidden == 768 and m == 4 else [own_hidden]
    gathered, start = [], 0
    for wide in chunks:
        whole = lax.all_gather(chunk(start, wide), "dp", axis=0, tiled=True)
        gathered.append(whole.reshape(m, 2, width, wide))
        start += wide

    pad = -(6 + n) % 16
    small = jnp.concatenate([norm_gains, norm_shifts, centroids], axis=0)
    small = jnp.pad(small, ((0, pad), (0, width - cols)))
    group = [project_in.T, project_out.T, small]
    started = links.start(jnp.concatenate(group, axis=0))
    weight_in, weight_out, weight_small = links.by_rows([a.shape[0] for a in group], started)
    started_up = links.start(dense_up, links.second)
    started_down = links.start(dense_down.T, links.second)

    row_slots, slots, cots = prepare(links, routes, cotangent, capacity)
    first_in, projected, mixed, lse, after_attn, second_in, small = attend(
        n, tokens, segments, weight_small, weight_in, weight_out, []
    )
    weight_up = links.by_columns(started_up, [small])
    (weight_down,) = links.by_rows([cols], started_down, [small])
    cots = links.exchange(cots, links.second)
    activated, slope = widen(second_in, weight_up, [])
    hidden, gates, sent = dispatch(
        links, activated, after_attn, small, row_slots, routes, weight_down, total, [cots]
    )
    rows, grads, *across = expert_rows(links.exchange(sent), cots, width, [])

    sums, expert_sums = None, []
    for c, whole in enumerate(gathered):
        if c < len(chunks) - 1:
            w_grads, *sums = expert(rows, grads, across, whole, sums, None)
            expert_sums.append(w_grads)
        else:
            back, results, acts, pre_grads = expert(rows, grads, across, whole, sums, cots)
    back = links.exchange(back)
    expert_sums.append(expert_grads(across, acts, pre_grads))

    def own_sum(grads):
        sums = lax.psum_scatter(grads.reshape(-1, grads.shape[-1]), "dp", scatter_dimension=0, tiled=True)
        return sums.reshape(grads.shape[1:])

    summed = [own_sum(expert_sums[0])]
    returned = links.exchange(results, [back])

    hidden_grad, down_in, small_3, centroid_grad, sums_down = gate_back(
        links, back, slots, routes, hidden, gates, small, cotangent, activated
    )
    twin_down = links.twins(sums_down)
    widened_grad, sums_up = widen_back(links, down_in, slope, second_in, weight_down)
    twin_up = links.twins(sums_up)
    down = links.fold([sums_down], twin_down, [returned])
    down_got = links.across(down)
    after_grad, attn_grad, small_2, sums_out = second_back(
        links, widened_grad, after_attn, hidden_grad, mixed, small, weight_up, []
    )
    twin_out = links.twins(sums_out)
    projected_grad = attend_back(attn_grad, projected, lse, segments, weight_out, [])
    up = links.fold([sums_up, sums_out], twin_up + twin_out)
    up_got = links.across(up)
    down = links.fold_again(down, down_got)
    down_got = links.across_again(down)
    tokens_grad, sums_small = tokens_back(
        links, projected_grad, tokens, after_grad, small, [small_2, small_3], centroid_grad, weight_in, []
    )
    twin_small = links.twins(sums_small)
    for grads in expert_sums[1:]:
        summed.append(own_sum(links.gated(grads, summed + [sums_small[0]])))
    sums_in = project_back(links, projected_grad, first_in, [])
    twin_in = links.twins(sums_in)
    up = links.fold_again(up, up_got, "fold_wait")
    up_got = links.across_again(up)
    inner = links.fold([sums_in, sums_small], twin_in + twin_small)
    inner_got = links.across(inner)
    down = links.fold_last(down, down_got)
    down_got = links.inward(down)
    inner = links.fold_again(inner, inner_got)
    inner_got = links.across_again(inner)
    up = links.fold_last(up, up_got)
    up_got = links.inward(up)
    inner = links.fold_last(inner, inner_got)
    inner_got = links.inward(inner)
    output = combine(returned, slots, hidden, gates)
    down = links.joined(down, down_got)
    down_got = links.middle(down)
    down = links.joined(down, down_got)
    down_got = links.outward(down)
    up = links.joined(up, up_got)
    up_got = links.middle(up)
    inner = links.joined(inner, inner_got)
    inner_got = links.middle(inner)
    up = links.joined(up, up_got)
    up_got = links.outward(up)
    inner = links.joined(inner, inner_got)
    inner_got = links.outward(inner)
    expert_sums = finish(summed)
    units, columns = dense_up.shape[1], project_in.shape[1]
    down_sum = links.settled(down, down_got)
    up_sum, out_sum = links.settled_across(up, up_got, units)
    inner_sum = links.settled(inner, inner_got)
    small_sum = inner_sum[columns:, :cols]

    return (
        output, tokens_grad, small_sum[:3], small_sum[3:6], inner_sum[:columns].T, out_sum.T, up_sum,
        down_sum.T, small_sum[6 : 6 + n], expert_sums[0][None], expert_sums[1][None],
    )


def solution(mesh):
    sizes = dict(mesh.shape)
    both, over = P(("dp", "expert"), None), P(None, "expert")
    expert_place = P("expert", None, "dp")
    return jax.shard_map(
        functools.partial(on_device, sizes["expert"], sizes["dp"]),
        mesh=mesh,
        in_specs=(both,) * 3 + (over,) * 7 + (expert_place,) * 2 + (both,),
        out_specs=(both,) * 2 + (over,) * 7 + (expert_place,) * 2,
        check_vma=False,
    )
```

```python
import functools

import jax
import jax.numpy as jnp
from jax import lax
from jax.experimental import pallas as pl
from jax.experimental.pallas import tpu as pltpu
from jax.sharding import PartitionSpec as P

HEAD_DIM = 64
EXTRA = 128
BF = jnp.bfloat16
F32 = jnp.float32
I32 = jnp.int32
ROOT = 0.7978845608028654
COST = dict(
    prepare=3, attend=16, widen=9, dispatch=10, expert_rows=4, expert=20, expert_last=10, expert_grads=6, gate_back=10, widen_back=12, fold=1,
    second_back=17, attend_back=2, fold_again=1, fold_wait=12, project_back=2, tokens_back=2, fold_last=1, joined=6,
    combine=1, finish=1, settle=1,
)
WIDE = ("attend", "widen", "dispatch", "expert", "expert_last", "expert_grads", "widen_back", "settle")
VMEM_LIMIT = 60 * 1024 * 1024


def mm(left, right):
    return lax.dot_general(left, right, (((1,), (0,)), ((), ())), preferred_element_type=F32)


def mm_t(left, right):
    return lax.dot_general(left, right, (((1,), (1,)), ((), ())), preferred_element_type=F32)


def t_mm(left, right):
    return lax.dot_general(left, right, (((0,), (0,)), ((), ())), preferred_element_type=F32)


def normalize(rows):
    share = 1.0 / rows.shape[-1]
    centred = rows - jnp.sum(rows, axis=-1, keepdims=True) * share
    spread = jnp.sum(centred * centred, axis=-1, keepdims=True) * share
    inverse = lax.rsqrt(spread + 1e-05)
    return centred * inverse, inverse


def normalize_back(grad, normal, inverse, gain):
    share = 1.0 / grad.shape[-1]
    scaled = grad * gain
    first = jnp.sum(scaled, axis=-1, keepdims=True) * share
    second = jnp.sum(scaled * normal, axis=-1, keepdims=True) * share
    rows = inverse * (scaled - first - normal * second)
    return rows, jnp.sum(grad * normal, axis=0, keepdims=True), jnp.sum(grad, axis=0, keepdims=True)


def smooth_and_slope(v):
    square = v * v
    bend = jnp.tanh(v * (ROOT + ROOT * 0.044715 * square))
    half = 0.5 + 0.5 * bend
    slope = half + 0.5 * v * (1.0 - bend * bend) * (ROOT + 3.0 * ROOT * 0.044715 * square)
    return v * half, slope


def split3(v):
    hi = v.astype(BF)
    rest = v - hi.astype(F32)
    mid = rest.astype(BF)
    return hi, mid, (rest - mid.astype(F32)).astype(BF)


def scalar_columns(v):
    hi, mid, low = split3(v)
    lane = lax.broadcasted_iota(I32, (v.shape[0], EXTRA), 1)
    out = jnp.where(lane == 0, hi.astype(F32), 0.0)
    out = jnp.where(lane == 1, mid.astype(F32), out)
    return jnp.where(lane == 2, low.astype(F32), out).astype(BF)


def columns_scalar(columns):
    return jnp.sum(columns.astype(F32), axis=-1, keepdims=True)


def bias_of(by_row, by_column):
    count = by_row.shape[0]
    row = lax.broadcasted_iota(I32, (count, count), 0)
    column = lax.broadcasted_iota(I32, (count, count), 1)
    allowed = (by_row == by_column) & (row >= column)
    return jnp.where(allowed, 0.0, -1000000000.0)


def half_masks():
    lane = lax.broadcasted_iota(I32, (1, 2 * HEAD_DIM), 1)
    first = jnp.where(lane < HEAD_DIM, 1.0, 0.0)
    return first.astype(BF), (1.0 - first).astype(BF)


BEFORE = []


def smallest(outs):
    return min(outs, key=lambda a: a.size * a.dtype.itemsize)


def call(kernel, outs, args, spaces, scratch, name, flops, moved, after=(), results=None):
    where = {"v": pltpu.VMEM, "a": pl.ANY}
    after = list(after) + BEFORE
    read, waited = len(args), len(after)
    args, spaces = list(args) + list(after), spaces + "a" * waited

    def body(*refs):
        kernel(*refs[:read], *refs[read + waited :])

    got = pl.pallas_call(
        body,
        out_shape=outs,
        in_specs=[pl.BlockSpec(memory_space=where[s]) for s in spaces],
        out_specs=[pl.BlockSpec(memory_space=where[s]) for s in results or "v" * len(outs)],
        scratch_shapes=scratch,
        compiler_params=pltpu.CompilerParams(vmem_limit_bytes=VMEM_LIMIT if name in WIDE else VMEM_LIMIT // 2),
        cost_estimate=pl.CostEstimate(flops=COST[name] * 1150000000, bytes_accessed=1000, transcendentals=0),
        name=name,
    )(*args)
    BEFORE[:] = [smallest(got)]
    return got


class Weight:
    def __init__(self, arrays, copies, shape):
        self.arrays, self.copies, self.shape = arrays, copies, shape

    def scratch(self):
        return [pltpu.VMEM(self.shape, BF), pltpu.SemaphoreType.DMA((len(self.copies),))]

    def start(self, refs, whole, sems):
        me = lax.axis_index("expert")
        running = []
        for i, (index, source, place) in enumerate(self.copies):
            copy = pltpu.make_async_copy(
                refs[index].at[source], whole.at[place(me)], sems.at[i]
            )
            copy.start()
            running.append(copy)
        return running


def row_place(k, size, offset, rows, step):
    def place(me):
        if k is None:
            return (pl.ds(offset, rows),)
        return (pl.ds(pl.multiple_of((me ^ k) * size + offset, step), rows),)

    return place


def column_place(k, size, offset, rows):
    def place(me):
        if k is None:
            return (pl.ds(0, rows),)
        start = pl.multiple_of((me ^ k) * size, 128)
        return (pl.ds(offset, rows), pl.ds(start, size))

    return place


class Links:
    def __init__(self, n, m):
        self.n, self.m = n, m
        self.cube = n == 8
        self.line = m == 4
        self.second = ()

    def hop(self, value, bit):
        return lax.ppermute(value, "expert", [(i, i ^ bit) for i in range(self.n)])

    def gated(self, value, gate):
        return lax.optimization_barrier((value, *gate))[0] if gate else value

    def start(self, shard, gate=()):
        if not self.cube:
            return [shard]
        shard = self.gated(shard, gate)
        return [shard, self.hop(shard, 2), self.hop(shard, 4)]

    def pieces(self, started, gate=()):
        shard, by_x, by_y = lax.optimization_barrier((*started, *gate))[:3] if gate else started
        half = shard.shape[0] // 2 // 16 * 16
        far_a = self.hop(by_y[:half], 2)
        far_b = self.hop(by_x[half:], 4)
        self.second = (far_a, far_b)
        return [
            (0, 0, shard), (1, 0, self.hop(shard, 1)), (2, 0, by_x), (3, 0, self.hop(by_x, 1)),
            (4, 0, by_y), (5, 0, self.hop(by_y, 1)), (6, 0, far_a), (6, half, far_b),
            (7, 0, self.hop(far_a, 1)), (7, half, self.hop(far_b, 1)),
        ]

    def by_rows(self, sizes, started, gate=()):
        group = started[0]
        weights, first = [], 0
        if not self.cube:
            whole = lax.all_gather(group, "expert", axis=0, tiled=False)
            for size in sizes:
                part = whole[:, first : first + size].reshape(-1, group.shape[1])
                copies = [(0, (pl.ds(0, part.shape[0]),), row_place(None, 0, 0, part.shape[0], 8))]
                weights.append(Weight([part], copies, part.shape))
                first += size
            return weights
        pieces = self.pieces(started, gate)
        for size in sizes:
            arrays, copies = [], []
            for k, row, array in pieces:
                low, high = max(first, row), min(first + size, row + array.shape[0])
                if low < high:
                    source = (pl.ds(low - row, high - low),)
                    place = row_place(k, size, low - first, high - low, 16 if size % 16 == 0 else 8)
                    copies.append((len(arrays), source, place))
                    arrays.append(array)
            weights.append(Weight(arrays, copies, (self.n * size, group.shape[1])))
            first += size
        return weights

    def by_columns(self, started, gate=()):
        shard = started[0]
        rows, size = shard.shape
        if not self.cube:
            whole = lax.all_gather(shard, "expert", axis=1, tiled=True)
            return Weight([whole], [(0, (pl.ds(0, rows),), column_place(None, 0, 0, rows))], whole.shape)
        arrays, copies = [], []
        for k, row, array in self.pieces(started, gate):
            source = (pl.ds(0, array.shape[0]),)
            copies.append((len(arrays), source, column_place(k, size, row, array.shape[0])))
            arrays.append(array)
        return Weight(arrays, copies, (rows, self.n * size))

    def exchange(self, rows, gate=()):
        blocks = self.gated(rows, gate).reshape(self.n, -1, rows.shape[1])
        got = lax.all_to_all(blocks, "expert", split_axis=0, concat_axis=0, tiled=True)
        return got.reshape(rows.shape)

    def sum_shapes(self, rows, width):
        if not self.cube:
            return [jax.ShapeDtypeStruct((self.n, rows, width), BF)]
        return [jax.ShapeDtypeStruct((self.n // 2, rows, width), BF)] * 2

    def write_sum(self, refs, whole, first, size):
        for k in range(self.n):
            if self.cube:
                me = lax.axis_index("expert")
                step = 16 if size % 16 == 0 else 8
                start = pl.multiple_of((me ^ k) * size, step)
                refs[k % 2][k // 2, first : first + size] = whole[pl.ds(start, size)]
            else:
                refs[0][k, first : first + size] = whole[k * size : (k + 1) * size]

    def twins(self, blocks):
        return [self.hop(blocks[1], 1)] if self.cube else []

    def fold(self, groups, twins, after=()):
        if not self.cube:
            return [jnp.concatenate([g[0] for g in groups], axis=1)]
        rows = [g[0].shape[1] for g in groups]
        total, columns = sum(rows), groups[0][0].shape[2]
        half = total // 2 // 16 * 16

        def kernel(*refs):
            count = len(groups)
            outs = refs[2 * count :]
            first = 0
            for even, odd in zip(refs[:count], refs[count : 2 * count]):
                for m in range(4):
                    value = (even[m].astype(F32) + odd[m].astype(F32)).astype(BF)
                    low, high = first, first + even.shape[1]
                    cut = min(max(half, low), high)
                    if low < cut:
                        outs[m % 2][m // 2, low:cut] = value[: cut - low]
                    if cut < high:
                        outs[2 + m // 2][m % 2, cut - half : high - half] = value[cut - low :]
                first += even.shape[1]

        outs = [jax.ShapeDtypeStruct((2, half, columns), BF)] * 2
        outs += [jax.ShapeDtypeStruct((2, total - half, columns), BF)] * 2
        args = [g[0] for g in groups] + list(twins)
        return list(call(kernel, outs, args, "v" * len(args), [], "fold", 0, 0, after))

    def across(self, kept):
        return [self.hop(kept[1], 2), self.hop(kept[3], 4)] if self.cube else []

    def fold_again(self, kept, got, name="fold_again"):
        if not self.cube:
            return kept

        def kernel(first, got_first, second, got_second, *outs):
            for i, (mine, other) in enumerate(((first, got_first), (second, got_second))):
                for j in range(2):
                    outs[2 * i + j][...] = (mine[j].astype(F32) + other[j].astype(F32)).astype(BF)

        outs = [jax.ShapeDtypeStruct(a.shape[1:], BF) for a in (kept[0], kept[0], kept[2], kept[2])]
        args = [kept[0], got[0], kept[2], got[1]]
        return list(call(kernel, outs, args, "vvvv", [], name, 0, 0))

    def across_again(self, kept):
        return [self.hop(kept[1], 4), self.hop(kept[3], 2)] if self.cube else []

    def fold_last(self, kept, got):
        if not self.cube:
            return lax.psum_scatter(kept[0], "expert", scatter_dimension=0, tiled=True)[0]
        half = kept[0].shape[0]

        def kernel(first, got_first, second, got_second, out):
            out[:half] = (first[...].astype(F32) + got_first[...].astype(F32)).astype(BF)
            out[half:] = (second[...].astype(F32) + got_second[...].astype(F32)).astype(BF)

        rows = half + kept[2].shape[0]
        outs = [jax.ShapeDtypeStruct((rows, kept[0].shape[1]), BF)]
        return call(kernel, outs, [kept[0], got[0], kept[2], got[1]], "vvvv", [], "fold_last", 0, 0)[0]

    def along(self, value, pairs):
        return lax.ppermute(value, "dp", pairs)

    def inward(self, value):
        return [self.along(value, [(0, 1), (3, 2)])] if self.line else []

    def middle(self, value):
        return [self.along(value, [(1, 2), (2, 1)])] if self.line else []

    def outward(self, value):
        return [self.along(value, [(1, 0), (2, 3)])] if self.line else []

    def joined(self, value, got):
        if not self.line:
            return value

        def kernel(mine, other, out):
            out[...] = (mine[...].astype(F32) + other[...].astype(F32)).astype(BF)

        outs = [jax.ShapeDtypeStruct(value.shape, BF)]
        return call(kernel, outs, [value, got[0]], "vv", [], "joined", 0, 0)[0]

    def settled(self, value, got):
        if not self.line:
            return lax.psum(value, "dp").astype(F32)

        def kernel(mine, other, out):
            place = lax.axis_index("dp")

            def write(ref):
                out[...] = ref[...].astype(F32)

            middle = (place == 1) | (place == 2)
            pl.when(middle)(lambda: write(mine))
            pl.when(jnp.logical_not(middle))(lambda: write(other))

        outs = [jax.ShapeDtypeStruct(value.shape, F32)]
        return call(kernel, outs, [value, got[0]], "vv", [], "settle", 0, 0)[0]

    def settled_across(self, value, got, units):
        if not self.line:
            value = lax.psum(value, "dp").astype(F32)
            return value[:units].T, value[units:]

        def kernel(mine, other, up, out):
            place = lax.axis_index("dp")

            def write(ref):
                up[...] = ref[:units].astype(F32).T
                out[...] = ref[units:].astype(F32)

            middle = (place == 1) | (place == 2)
            pl.when(middle)(lambda: write(mine))
            pl.when(jnp.logical_not(middle))(lambda: write(other))

        rows, width = value.shape
        outs = [jax.ShapeDtypeStruct((width, units), F32), jax.ShapeDtypeStruct((rows - units, width), F32)]
        return call(kernel, outs, [value, got[0]], "vv", [], "settle", 0, 0)


def finish(parts):
    width = parts[0].shape[1]

    def kernel(*refs):
        ups, downs = refs[-2:]
        first = 0
        for ref in refs[:-2]:
            for i, out in enumerate((ups, downs)):
                out[:, first : first + ref.shape[2]] = ref[i].astype(F32)
            first += ref.shape[2]

    outs = [jax.ShapeDtypeStruct((width, sum(p.shape[2] for p in parts)), F32)] * 2
    return call(kernel, outs, parts, "v" * len(parts), [], "finish", 0, 0)


def prepare(links, routes, cotangent, capacity):
    count, width = cotangent.shape
    n = links.n
    total = n * capacity

    def kernel(by_row, by_column, cot, row_out, column_out, out):
        route_c, route_r = by_row[...], by_column[...]
        token = lax.broadcasted_iota(I32, (count, count), 0)
        other = lax.broadcasted_iota(I32, (count, count), 1)
        same = route_c == route_r
        rank_c = jnp.sum(jnp.where(same & (other < token), 1.0, 0.0), axis=1, keepdims=True)
        rank_r = jnp.sum(jnp.where(same & (token < other), 1.0, 0.0), axis=0, keepdims=True)
        slot_c = route_c * capacity + rank_c.astype(I32)
        slot_r = route_r * capacity + rank_r.astype(I32)
        column_out[...] = slot_c
        row_out[...] = slot_r
        place = lax.broadcasted_iota(I32, (total, count), 0)
        to_slots = jnp.where(place == slot_r, 1.0, 0.0).astype(BF)
        out[...] = mm(to_slots, cot[...]).astype(BF)

    outs = [jax.ShapeDtypeStruct((1, count), I32), jax.ShapeDtypeStruct((count, 1), I32)]
    outs.append(jax.ShapeDtypeStruct((total, width), BF))
    args = [routes, routes.reshape(1, count), cotangent]
    return call(
        kernel, outs, args, "vvv", [], "prepare", 2 * total * count * width, 4 * total * width
    )


def attend(n, tokens, segments, weight_small, weight_in, weight_out, after):
    count, width = tokens.shape
    pairs = width // (2 * HEAD_DIM)
    block = 128
    n_small, n_in, n_out = len(weight_small.arrays), len(weight_in.arrays), len(weight_out.arrays)
    small_rows, cols = weight_small.shape[0] // n, width // n

    def kernel(tok, seg_c, seg_r, *refs):
        small_refs, refs = refs[:n_small], refs[n_small:]
        in_refs, refs = refs[:n_in], refs[n_in:]
        out_refs, refs = refs[:n_out], refs[n_out:]
        first_ref, proj, mixed, lse, after_ref, second_ref, small_ref = refs[:7]
        w_small, small_sems, w_in, in_sems, w_out, out_sems, bias = refs[7:]
        small_copies = weight_small.start(small_refs, w_small, small_sems)
        in_copies = weight_in.start(in_refs, w_in, in_sems)
        out_copies = weight_out.start(out_refs, w_out, out_sems)
        rows = tok[...].astype(F32)
        normal, _ = normalize(rows)
        source = lax.broadcasted_iota(I32, (cols, width), 0)
        place = lax.broadcasted_iota(I32, (cols, width), 1)
        for copy in small_copies:
            copy.wait()
        small = jnp.zeros((small_rows, width), F32)
        for j in range(n):
            spread = jnp.where(place == source + j * cols, 1.0, 0.0).astype(BF)
            small += mm(w_small[j * small_rows : (j + 1) * small_rows, :cols], spread)
        small_ref[...] = small
        first = (normal * small_ref[0:1] + small_ref[3:4]).astype(BF)
        first_ref[...] = first
        bias[...] = bias_of(seg_c[...], seg_r[...])
        lse[...] = jnp.zeros_like(lse)
        for copy in in_copies:
            copy.wait()
        proj[...] = mm_t(first, w_in[...]).astype(BF)
        masks = half_masks()
        lane = lax.broadcasted_iota(I32, (block, 128), 1)

        def pair(i, carry):
            at = [pl.ds(pl.multiple_of(part * width + 128 * i, 128), 128) for part in range(3)]
            for b in range(count // block):
                mine, keys = pl.ds(b * block, block), pl.ds(0, (b + 1) * block)
                q, k, v = proj[mine, at[0]] * 0.125, proj[keys, at[1]], proj[keys, at[2]]
                got = jnp.zeros((block, 128), F32)
                kept = lse[mine]
                for h in range(2):
                    scores = mm_t(q * masks[h], k) + bias[mine, keys]
                    top = jnp.max(scores, axis=1, keepdims=True)
                    lifted = jnp.exp(scores - top)
                    totals = jnp.sum(lifted, axis=1, keepdims=True)
                    probs = (lifted * (1.0 / totals)).astype(BF)
                    got += mm(probs, v * masks[h])
                    kept = jnp.where(lane == 2 * i + h, top + jnp.log(totals), kept)
                lse[mine] = kept
                mixed[mine, at[0]] = got.astype(BF)
            return carry

        lax.fori_loop(0, pairs, pair, 0)
        for copy in out_copies:
            copy.wait()
        after = rows + mm_t(mixed[...], w_out[...])
        after_ref[...] = after
        normal, _ = normalize(after)
        second_ref[...] = (normal * small_ref[1:2] + small_ref[4:5]).astype(BF)

    shape = jax.ShapeDtypeStruct
    outs = [
        shape((count, width), BF), shape((count, 3 * width), BF), shape((count, width), BF),
        shape((count, 128), F32), shape((count, width), F32), shape((count, width), BF),
        shape((small_rows, width), F32),
    ]
    args = [tokens, segments.reshape(count, 1), segments]
    args += weight_small.arrays + weight_in.arrays + weight_out.arrays
    spaces = "vvv" + "a" * (n_small + n_in + n_out)
    scratch = weight_small.scratch() + weight_in.scratch() + weight_out.scratch() + [pltpu.VMEM((count, count), F32)]
    flops = 2 * count * width * (4 * width + 2 * count) * 2
    return call(kernel, outs, args, spaces, scratch, "attend", flops, 12 * count * width * 4, after)


def widen(second_in, weight_up, after):
    count = second_in.shape[0]
    hidden = weight_up.shape[1]
    pieces = len(weight_up.arrays)
    part = hidden // 4

    def kernel(second, *refs):
        up_refs, (act_ref, slope_ref, up, sems) = refs[:pieces], refs[pieces:]
        for copy in weight_up.start(up_refs, up, sems):
            copy.wait()
        rows = second[...]
        for i in range(4):
            at = pl.ds(i * part, part)
            value, slope = smooth_and_slope(mm(rows, up[:, at]))
            act_ref[:, at] = value.astype(BF)
            slope_ref[:, at] = slope.astype(BF)

    outs = [jax.ShapeDtypeStruct((count, hidden), BF)] * 2
    args = [second_in] + weight_up.arrays
    return call(
        kernel, outs, args, "v" + "a" * pieces, weight_up.scratch(), "widen",
        4 * count * hidden * second_in.shape[1], 8 * count * hidden, after,
    )


def dispatch(links, activated, after_attn, small, row_slots, routes, weight_down, total, after):
    count, width = after_attn.shape
    n = links.n
    pieces = len(weight_down.arrays)

    def kernel(act, after, small_ref, slot_r, route_c, *refs):
        down_refs, refs = refs[:pieces], refs[pieces:]
        hidden_ref, gates_ref, sent_ref = refs[:-2]
        down, sems = refs[-2:]
        for copy in weight_down.start(down_refs, down, sems):
            copy.wait()
        hidden = after[...] + mm_t(act[...], down[...])
        hidden_ref[...] = hidden
        normal, _ = normalize(hidden)
        moe_in = normal * small_ref[2:3] + small_ref[5:6]
        lane = lax.broadcasted_iota(I32, (count, n), 1)
        onehot = jnp.where(lane == route_c[...], 1.0, 0.0).astype(BF)
        chosen = mm(onehot, small_ref[6 : 6 + n].astype(BF))
        logit = jnp.sum(moe_in * chosen, axis=1, keepdims=True)
        gates = 1.0 / (1.0 + jnp.exp(-logit))
        gates_ref[...] = gates
        sent = jnp.concatenate([moe_in.astype(BF), scalar_columns(gates)], axis=1)
        place = lax.broadcasted_iota(I32, (total, count), 0)
        to_slots = jnp.where(place == slot_r[...], 1.0, 0.0).astype(BF)
        sent_ref[...] = mm(to_slots, sent).astype(BF)

    shape = jax.ShapeDtypeStruct
    outs = [shape((count, width), F32), shape((count, 1), F32)]
    outs.append(shape((total, width + EXTRA), BF))
    args = [activated, after_attn, small, row_slots, routes] + weight_down.arrays
    return call(
        kernel, outs, args, "vvvvv" + "a" * pieces, weight_down.scratch(), "dispatch",
        4 * count * width * 4 * width, 16 * count * width, after,
    )


def expert_rows(arrived, cots, width, after):
    total = arrived.shape[0]

    def kernel(arrived_ref, cot_ref, rows_ref, grads_ref, rows_across, grads_across):
        rows = arrived_ref[:, :width]
        rows_ref[...] = rows
        rows_across[...] = rows.T
        gates = columns_scalar(arrived_ref[:, width:])
        grads = (gates * cot_ref[...].astype(F32)).astype(BF)
        grads_ref[...] = grads
        grads_across[...] = grads.T

    outs = [jax.ShapeDtypeStruct((total, width), BF)] * 2 + [jax.ShapeDtypeStruct((width, total), BF)] * 2
    return call(kernel, outs, [arrived, cots], "vv", [], "expert_rows", 0, 0, after)


def expert(rows, grads, across, weights, sums, cot):
    total, width = rows.shape
    m, _, _, wide = weights.shape
    last, started = cot is not None, sums is not None

    def kernel(rows_ref, grads_ref, rows_across, grads_across, *refs):
        refs = list(refs)
        take = lambda k: [refs.pop(0) for _ in range(k)]
        carried = take(2) if started else None
        (cot_ref,) = take(1) if last else (None,)
        (weight_ref,) = take(1)
        if last:
            outs, (acts, pre_grads) = take(2), take(2)
            held, sems, out_sum, row_sum = refs
        else:
            (w_grads,), outs = take(1), take(2)
            held, sems, out_sum, row_sum, grad_held, out_sems = refs
        entering = [pltpu.make_async_copy(weight_ref.at[i], held.at[i], sems.at[i]) for i in range(m)]
        for copy in entering:
            copy.start()
        r, g = rows_ref[...], grads_ref[...]
        leaving = []
        for i in range(m):
            entering[i].wait()
            up, down = held[i, 0], held[i, 1]
            value, slope = smooth_and_slope(mm(r, up))
            act = value.astype(BF)
            pre_grad = (mm(g, down) * slope).astype(BF)
            row_part, out_part = mm_t(pre_grad, up), mm_t(act, down)
            if i == 0 and started:
                row_part, out_part = row_part + carried[0][...], out_part + carried[1][...]
            if i > 0:
                row_part, out_part = row_part + row_sum[...], out_part + out_sum[...]
            row_sum[...] = row_part
            out_sum[...] = out_part
            if last:
                acts[i] = act
                pre_grads[i] = pre_grad
            else:
                grad_held[i, 0] = mm(rows_across[...], pre_grad).astype(BF)
                grad_held[i, 1] = mm(grads_across[...], act).astype(BF)
                copy = pltpu.make_async_copy(grad_held.at[i], w_grads.at[i], out_sems.at[i])
                copy.start()
                leaving.append(copy)
        if last:
            result = out_sum[...].astype(BF)
            gate_grad = jnp.sum(cot_ref[...].astype(F32) * result.astype(F32), axis=1, keepdims=True)
            outs[0][...] = jnp.concatenate([row_sum[...].astype(BF), scalar_columns(gate_grad)], axis=1)
            outs[1][...] = result
        else:
            outs[0][...] = row_sum[...]
            outs[1][...] = out_sum[...]
        for copy in leaving:
            copy.wait()

    shape = jax.ShapeDtypeStruct
    args = [rows, grads, *across] + (sums if started else []) + ([cot] if last else [])
    spaces = "v" * len(args) + "a"
    scratch = [
        pltpu.VMEM((m, 2, width, wide), BF), pltpu.SemaphoreType.DMA((m,)),
        pltpu.VMEM((total, width), F32), pltpu.VMEM((total, width), F32),
    ]
    if last:
        outs = [shape((total, width + EXTRA), BF), shape((total, width), BF)] + [shape((m, total, wide), BF)] * 2
        return call(kernel, outs, args + [weights], spaces, scratch, "expert_last", 0, 0)
    outs = [shape((m, 2, width, wide), BF)] + [shape((total, width), F32)] * 2
    scratch += [pltpu.VMEM((m, 2, width, wide), BF), pltpu.SemaphoreType.DMA((m,))]
    return call(kernel, outs, args + [weights], spaces, scratch, "expert", 0, 0, [], "avv")


def expert_grads(across, acts, pre_grads):
    m, _, wide = acts.shape
    width = across[0].shape[0]

    def kernel(rows_across, grads_across, acts_ref, pre_ref, out):
        for i in range(m):
            out[i, 0] = mm(rows_across[...], pre_ref[i]).astype(BF)
            out[i, 1] = mm(grads_across[...], acts_ref[i]).astype(BF)

    outs = [jax.ShapeDtypeStruct((m, 2, width, wide), BF)]
    return call(kernel, outs, [*across, acts, pre_grads], "vvvv", [], "expert_grads", 0, 0)[0]


def combine(returned, slots, hidden, gates):
    count, width = hidden.shape

    def kernel(slot_c, hidden_ref, gates_ref, got_ref, out):
        got = got_ref[...]
        place = lax.broadcasted_iota(I32, (count, got.shape[0]), 1)
        pick = jnp.where(place == slot_c[...], 1.0, 0.0).astype(BF)
        out[...] = (hidden_ref[...] + gates_ref[...] * mm(pick, got)).astype(BF)

    return call(
        kernel, [jax.ShapeDtypeStruct((count, width), BF)], [slots, hidden, gates, returned],
        "vvvv", [], "combine", 4 * count * count * width, 10 * count * width,
    )[0]


def gate_back(links, back, slots, routes, hidden, gates, small, cotangent, activated):
    count, width = hidden.shape
    n = links.n
    size = width // n
    units = activated.shape[1]

    def kernel(slot_c, route_c, hidden_ref, gates_ref, small_ref, cot, act, back_ref, *refs):
        got = back_ref[...]
        hidden_grad_ref, down_in_ref, small_out, centroid_out, *sums = refs[:-1]
        whole = refs[-1]
        place = lax.broadcasted_iota(I32, (count, got.shape[0]), 1)
        pick = jnp.where(place == slot_c[...], 1.0, 0.0).astype(BF)
        got = mm(pick, got)
        gates = gates_ref[...]
        logit_grad = columns_scalar(got[:, width:]) * gates * (1.0 - gates)
        lane = lax.broadcasted_iota(I32, (count, n), 1)
        onehot = jnp.where(lane == route_c[...], 1.0, 0.0).astype(BF)
        chosen = mm(onehot, small_ref[6 : 6 + n].astype(BF))
        normal, inverse = normalize(hidden_ref[...])
        gain = small_ref[2:3]
        moe_in = normal * gain + small_ref[5:6]
        terms = split3(logit_grad * moe_in)
        centroid_out[...] = t_mm(onehot, terms[0]) + t_mm(onehot, terms[1]) + t_mm(onehot, terms[2])
        moe_grad = got[:, :width] + logit_grad * chosen
        part, gain_grad, shift_grad = normalize_back(moe_grad, normal, inverse, gain)
        small_out[...] = jnp.concatenate([gain_grad, shift_grad], axis=0)
        hidden_grad = cot[...].astype(F32) + part
        hidden_grad_ref[...] = hidden_grad
        down_in = hidden_grad.astype(BF)
        down_in_ref[...] = down_in
        whole[...] = t_mm(down_in, act[...]).astype(BF)
        links.write_sum(sums, whole, 0, size)

    shape = jax.ShapeDtypeStruct
    outs = [
        shape((count, width), F32), shape((count, width), BF), shape((2, width), F32), shape((n, width), F32),
    ] + links.sum_shapes(size, units)
    args = [slots, routes, hidden, gates, small, cotangent, activated, back]
    hidden_grad, down_in, small_out, centroid_out, *sums = call(
        kernel, outs, args, "v" * len(args), [pltpu.VMEM((width, units), BF)], "gate_back",
        2 * count * width * units * 2, 8 * count * units,
    )
    return hidden_grad, down_in, small_out, centroid_out, sums


def widen_back(links, down_in, slope, second_in, weight_down):
    count, width = down_in.shape
    units = slope.shape[1]
    size = units // links.n
    pieces = len(weight_down.arrays)

    def kernel(down_in_ref, slope_ref, second, *refs):
        down_refs, refs = refs[:pieces], refs[pieces:]
        grad, *sums = refs[:-3]
        down, sems, whole = refs[-3:]
        for copy in weight_down.start(down_refs, down, sems):
            copy.wait()
        rows = down_in_ref[...]
        part = units // 4
        for i in range(4):
            at = pl.ds(i * part, part)
            piece = (mm(rows, down[:, at]) * slope_ref[:, at].astype(F32)).astype(BF)
            grad[:, at] = piece
            whole[at] = t_mm(piece, second[...]).astype(BF)
        links.write_sum(sums, whole, 0, size)

    outs = [jax.ShapeDtypeStruct((count, units), BF)] + links.sum_shapes(size, width)
    args = [down_in, slope, second_in]
    spaces = "vvv" + "a" * pieces
    scratch = weight_down.scratch() + [pltpu.VMEM((units, width), BF)]
    grad, *sums = call(
        kernel, outs, args + weight_down.arrays, spaces, scratch, "widen_back",
        4 * count * width * units, 8 * width * units,
    )
    return grad, sums


def second_back(links, widened_grad, after_attn, hidden_grad, mixed, small, weight_up, after):
    count, width = after_attn.shape
    n = links.n
    size = width // n
    pieces = len(weight_up.arrays)

    def kernel(grad, after_ref, hidden_grad_ref, mixed_ref, small_ref, *refs):
        up_refs, refs = refs[:pieces], refs[pieces:]
        after_grad_ref, attn_grad_ref, small_out, *sums = refs[:-3]
        up, sems, whole = refs[-3:]
        copies = weight_up.start(up_refs, up, sems)
        normal, inverse = normalize(after_ref[...])
        for copy in copies:
            copy.wait()
        second_grad = mm_t(grad[...], up[...])
        back, gain_grad, shift_grad = normalize_back(second_grad, normal, inverse, small_ref[1:2])
        small_out[...] = jnp.concatenate([gain_grad, shift_grad], axis=0)
        after_grad = hidden_grad_ref[...] + back
        after_grad_ref[...] = after_grad
        attn_grad = after_grad.astype(BF)
        attn_grad_ref[...] = attn_grad
        whole[...] = t_mm(attn_grad, mixed_ref[...]).astype(BF)
        links.write_sum(sums, whole, 0, size)

    shape = jax.ShapeDtypeStruct
    outs = [shape((count, width), F32), shape((count, width), BF), shape((2, width), F32)]
    outs += links.sum_shapes(size, width)
    args = [widened_grad, after_attn, hidden_grad, mixed, small]
    spaces = "vvvvv" + "a" * pieces
    scratch = weight_up.scratch() + [pltpu.VMEM((width, width), BF)]
    after_grad, attn_grad, small_out, *sums = call(
        kernel, outs, args + weight_up.arrays, spaces, scratch, "second_back",
        2 * count * width * 4 * width, 8 * width * 4 * width, after,
    )
    return after_grad, attn_grad, small_out, sums


def attend_back(attn_grad, projected, lse, segments, weight_out, after):
    count, width = attn_grad.shape
    pairs = width // (2 * HEAD_DIM)
    block = 128
    blocks = count // block
    n_out = len(weight_out.arrays)

    def kernel(attn_ref, proj, lse, seg_c, seg_r, *refs):
        out_refs, refs = refs[:n_out], refs[n_out:]
        grad, w_out, out_sems, bias, mixed_grad = refs
        copies = weight_out.start(out_refs, w_out, out_sems)
        bias[...] = bias_of(seg_c[...], seg_r[...])
        for copy in copies:
            copy.wait()
        mixed_grad[...] = mm(attn_ref[...], w_out[...]).astype(BF)
        masks = half_masks()
        lane = lax.broadcasted_iota(I32, (block, 128), 1)

        def pair(i, carry):
            at = [pl.ds(pl.multiple_of(part * width + 128 * i, 128), 128) for part in range(3)]
            k_grad = [jnp.zeros((block, 128), F32) for _ in range(blocks)]
            v_grad = [jnp.zeros((block, 128), F32) for _ in range(blocks)]
            for b in range(blocks):
                mine, keys = pl.ds(b * block, block), pl.ds(0, (b + 1) * block)
                q, k, v = proj[mine, at[0]] * 0.125, proj[keys, at[1]], proj[keys, at[2]]
                upper = mixed_grad[mine, at[0]]
                kept = lse[mine]
                q_grad = jnp.zeros((block, 128), F32)
                for h in range(2):
                    q_h, upper_h = q * masks[h], upper * masks[h]
                    log_total = jnp.sum(jnp.where(lane == 2 * i + h, kept, 0.0), axis=1, keepdims=True)
                    probs = jnp.exp(mm_t(q_h, k) + bias[mine, keys] - log_total)
                    probs_grad = mm_t(upper_h, v)
                    mean = jnp.sum(probs * probs_grad, axis=1, keepdims=True)
                    scores_grad = (probs * (probs_grad - mean)).astype(BF)
                    q_grad += mm(scores_grad, k * masks[h])
                    dv = t_mm(probs.astype(BF), upper_h)
                    dk = t_mm(scores_grad, q_h)
                    for c in range(b + 1):
                        v_grad[c] += dv[c * block : (c + 1) * block]
                        k_grad[c] += dk[c * block : (c + 1) * block]
                grad[mine, at[0]] = (q_grad * 0.125).astype(BF)
            for c in range(blocks):
                mine = pl.ds(c * block, block)
                grad[mine, at[1]] = k_grad[c].astype(BF)
                grad[mine, at[2]] = v_grad[c].astype(BF)
            return carry

        lax.fori_loop(0, pairs, pair, 0)

    args = [attn_grad, projected, lse, segments.reshape(count, 1), segments]
    spaces = "v" * len(args) + "a" * n_out
    scratch = weight_out.scratch() + [pltpu.VMEM((count, count), F32), pltpu.VMEM((count, width), BF)]
    return call(
        kernel, [jax.ShapeDtypeStruct((count, 3 * width), BF)], args + weight_out.arrays, spaces, scratch,
        "attend_back", 2 * count * width * (width + 5 * count) * 2, 12 * count * width * 4, after,
    )[0]


def project_back(links, projected_grad, first_in, after):
    width = first_in.shape[1]
    size = 3 * width // links.n

    def kernel(grad, first, *refs):
        whole = refs[-1]
        whole[...] = t_mm(grad[...], first[...]).astype(BF)
        links.write_sum(refs[:-1], whole, 0, size)

    return call(
        kernel, links.sum_shapes(size, width), [projected_grad, first_in], "vv",
        [pltpu.VMEM((3 * width, width), BF)], "project_back", 6 * width**3, 12 * width * width, after,
    )


def tokens_back(links, projected_grad, tokens, after_grad, small, smalls, centroid_grad, weight_in, after):
    count, width = tokens.shape
    n, n_in = links.n, len(weight_in.arrays)
    cols, rows = width // n, small.shape[0]

    def kernel(grad, tok, after_ref, small_ref, small_2, small_3, centroids, *refs):
        in_refs, refs = refs[:n_in], refs[n_in:]
        out, *sums = refs[:-2]
        w_in, sems = refs[-2:]
        copies = weight_in.start(in_refs, w_in, sems)
        normal, inverse = normalize(tok[...].astype(F32))
        for copy in copies:
            copy.wait()
        first_grad = mm(grad[...], w_in[...])
        back, gain_grad, shift_grad = normalize_back(first_grad, normal, inverse, small_ref[0:1])
        out[...] = after_ref[...] + back
        parts = [gain_grad, small_2[0:1], small_3[0:1], shift_grad, small_2[1:2], small_3[1:2]]
        parts += [centroids[...], jnp.zeros((rows - 6 - n, width), F32)]
        both = jnp.concatenate(parts, axis=0).astype(BF)
        me = lax.axis_index("expert") if links.cube else 0
        source = lax.broadcasted_iota(I32, (128, width), 0)
        place = lax.broadcasted_iota(I32, (128, width), 1)
        for k in range(n):
            mine = (place == source + (me ^ k) * cols) & (source < cols)
            block = mm_t(both, jnp.where(mine, 1.0, 0.0).astype(BF)).astype(BF)
            ref, i = (sums[k % 2], k // 2) if links.cube else (sums[0], k)
            ref[i] = jnp.zeros((rows, width), BF)
            ref[i, :, :128] = block

    outs = [jax.ShapeDtypeStruct((count, width), F32)] + links.sum_shapes(rows, width)
    args = [projected_grad, tokens, after_grad, small, *smalls, centroid_grad]
    out, *sums = call(
        kernel, outs, args + weight_in.arrays, "v" * len(args) + "a" * n_in, weight_in.scratch(),
        "tokens_back", 6 * count * width * width, 20 * count * width, after,
    )
    return out, sums


def on_device(
    n, m, tokens, segments, routes, norm_gains, norm_shifts, project_in, project_out,
    dense_up, dense_down, centroids, expert_up, expert_down, cotangent,
):
    count, width = tokens.shape
    BEFORE.clear()
    capacity = 2 * count // n
    total = n * capacity
    own_hidden = expert_up.shape[2]
    links = Links(n, m)
    cols = width // n

    def chunk(start, wide):
        part = slice(start, start + wide)
        return jnp.concatenate([expert_up[0][:, part], expert_down[0][:, part]], axis=0)

    chunks = [640, 128] if own_hidden == 768 and m == 4 else [own_hidden]
    gathered, start = [], 0
    for wide in chunks:
        whole = lax.all_gather(chunk(start, wide), "dp", axis=0, tiled=True)
        gathered.append(whole.reshape(m, 2, width, wide))
        start += wide

    pad = -(6 + n) % 16
    small = jnp.concatenate([norm_gains, norm_shifts, centroids], axis=0)
    small = jnp.pad(small, ((0, pad), (0, width - cols)))
    group = [project_in.T, project_out.T, small]
    started = links.start(jnp.concatenate(group, axis=0))
    weight_in, weight_out, weight_small = links.by_rows([a.shape[0] for a in group], started)
    started_up = links.start(dense_up, links.second)
    started_down = links.start(dense_down.T, links.second)

    row_slots, slots, cots = prepare(links, routes, cotangent, capacity)
    first_in, projected, mixed, lse, after_attn, second_in, small = attend(
        n, tokens, segments, weight_small, weight_in, weight_out, []
    )
    weight_up = links.by_columns(started_up, [small])
    (weight_down,) = links.by_rows([cols], started_down, [small])
    cots = links.exchange(cots, links.second)
    activated, slope = widen(second_in, weight_up, [])
    hidden, gates, sent = dispatch(
        links, activated, after_attn, small, row_slots, routes, weight_down, total, [cots]
    )
    rows, grads, *across = expert_rows(links.exchange(sent), cots, width, [])

    sums, expert_sums = None, []
    for c, whole in enumerate(gathered):
        if c < len(chunks) - 1:
            w_grads, *sums = expert(rows, grads, across, whole, sums, None)
            expert_sums.append(w_grads)
        else:
            back, results, acts, pre_grads = expert(rows, grads, across, whole, sums, cots)
    back = links.exchange(back)
    expert_sums.append(expert_grads(across, acts, pre_grads))

    def own_sum(grads):
        sums = lax.psum_scatter(grads.reshape(-1, grads.shape[-1]), "dp", scatter_dimension=0, tiled=True)
        return sums.reshape(grads.shape[1:])

    summed = [own_sum(expert_sums[0])]
    returned = links.exchange(results, [back])

    hidden_grad, down_in, small_3, centroid_grad, sums_down = gate_back(
        links, back, slots, routes, hidden, gates, small, cotangent, activated
    )
    twin_down = links.twins(sums_down)
    widened_grad, sums_up = widen_back(links, down_in, slope, second_in, weight_down)
    twin_up = links.twins(sums_up)
    down = links.fold([sums_down], twin_down, [returned])
    down_got = links.across(down)
    after_grad, attn_grad, small_2, sums_out = second_back(
        links, widened_grad, after_attn, hidden_grad, mixed, small, weight_up, []
    )
    twin_out = links.twins(sums_out)
    projected_grad = attend_back(attn_grad, projected, lse, segments, weight_out, [])
    up = links.fold([sums_up, sums_out], twin_up + twin_out)
    up_got = links.across(up)
    down = links.fold_again(down, down_got)
    down_got = links.across_again(down)
    tokens_grad, sums_small = tokens_back(
        links, projected_grad, tokens, after_grad, small, [small_2, small_3], centroid_grad, weight_in, []
    )
    twin_small = links.twins(sums_small)
    for grads in expert_sums[1:]:
        summed.append(own_sum(links.gated(grads, summed + [sums_small[0]])))
    sums_in = project_back(links, projected_grad, first_in, [])
    twin_in = links.twins(sums_in)
    up = links.fold_again(up, up_got, "fold_wait")
    up_got = links.across_again(up)
    inner = links.fold([sums_in, sums_small], twin_in + twin_small)
    inner_got = links.across(inner)
    down = links.fold_last(down, down_got)
    down_got = links.inward(down)
    inner = links.fold_again(inner, inner_got)
    inner_got = links.across_again(inner)
    up = links.fold_last(up, up_got)
    up_got = links.inward(up)
    inner = links.fold_last(inner, inner_got)
    inner_got = links.inward(inner)
    output = combine(returned, slots, hidden, gates)
    down = links.joined(down, down_got)
    down_got = links.middle(down)
    up = links.joined(up, up_got)
    up_got = links.middle(up)
    inner = links.joined(inner, inner_got)
    inner_got = links.middle(inner)
    down = links.joined(down, down_got)
    down_got = links.outward(down)
    up = links.joined(up, up_got)
    up_got = links.outward(up)
    inner = links.joined(inner, inner_got)
    inner_got = links.outward(inner)
    expert_sums = finish(summed)
    down_sum = links.settled(down, down_got)
    units, columns = dense_up.shape[1], project_in.shape[1]
    up_sum, out_sum = links.settled_across(up, up_got, units)
    inner_sum = links.settled(inner, inner_got)
    small_sum = inner_sum[columns:, :cols]

    return (
        output, tokens_grad, small_sum[:3], small_sum[3:6], inner_sum[:columns].T, out_sum.T, up_sum,
        down_sum.T, small_sum[6 : 6 + n], expert_sums[0][None], expert_sums[1][None],
    )


def solution(mesh):
    sizes = dict(mesh.shape)
    both, over = P(("dp", "expert"), None), P(None, "expert")
    expert_place = P("expert", None, "dp")
    return jax.shard_map(
        functools.partial(on_device, sizes["expert"], sizes["dp"]),
        mesh=mesh,
        in_specs=(both,) * 3 + (over,) * 7 + (expert_place,) * 2 + (both,),
        out_specs=(both,) * 2 + (over,) * 7 + (expert_place,) * 2,
        check_vma=False,
    )
```

```python
import functools

import jax
import jax.numpy as jnp
from jax import lax
from jax.experimental import pallas as pl
from jax.experimental.pallas import tpu as pltpu
from jax.sharding import PartitionSpec as P

HEAD_DIM = 64
EXTRA = 128
BF = jnp.bfloat16
F32 = jnp.float32
I32 = jnp.int32
ROOT = 0.7978845608028654
COST = dict(
    prepare=3, attend=16, widen=9, dispatch=10, expert_rows=4, expert=20, expert_last=10, expert_grads=6, gate_back=10, widen_back=12, fold=1, fold_wide=1,
    second_back=17, attend_back=2, fold_again=1, fold_wait=12, project_back=2, tokens_back=2, fold_last=1, joined=6,
    combine=1, finish=1, settle=1,
)
WIDE = ("attend", "widen", "dispatch", "expert", "expert_last", "expert_grads", "gate_back", "fold_wide", "widen_back", "settle")
VMEM_LIMIT = 60 * 1024 * 1024


def mm(left, right):
    return lax.dot_general(left, right, (((1,), (0,)), ((), ())), preferred_element_type=F32)


def mm_t(left, right):
    return lax.dot_general(left, right, (((1,), (1,)), ((), ())), preferred_element_type=F32)


def t_mm(left, right):
    return lax.dot_general(left, right, (((0,), (0,)), ((), ())), preferred_element_type=F32)


def normalize(rows):
    share = 1.0 / rows.shape[-1]
    centred = rows - jnp.sum(rows, axis=-1, keepdims=True) * share
    spread = jnp.sum(centred * centred, axis=-1, keepdims=True) * share
    inverse = lax.rsqrt(spread + 1e-05)
    return centred * inverse, inverse


def normalize_back(grad, normal, inverse, gain):
    share = 1.0 / grad.shape[-1]
    scaled = grad * gain
    first = jnp.sum(scaled, axis=-1, keepdims=True) * share
    second = jnp.sum(scaled * normal, axis=-1, keepdims=True) * share
    rows = inverse * (scaled - first - normal * second)
    return rows, jnp.sum(grad * normal, axis=0, keepdims=True), jnp.sum(grad, axis=0, keepdims=True)


def smooth_and_slope(v):
    square = v * v
    bend = jnp.tanh(v * (ROOT + ROOT * 0.044715 * square))
    half = 0.5 + 0.5 * bend
    slope = half + 0.5 * v * (1.0 - bend * bend) * (ROOT + 3.0 * ROOT * 0.044715 * square)
    return v * half, slope


def split3(v):
    hi = v.astype(BF)
    rest = v - hi.astype(F32)
    mid = rest.astype(BF)
    return hi, mid, (rest - mid.astype(F32)).astype(BF)


def scalar_columns(v):
    hi, mid, low = split3(v)
    lane = lax.broadcasted_iota(I32, (v.shape[0], EXTRA), 1)
    out = jnp.where(lane == 0, hi.astype(F32), 0.0)
    out = jnp.where(lane == 1, mid.astype(F32), out)
    return jnp.where(lane == 2, low.astype(F32), out).astype(BF)


def columns_scalar(columns):
    return jnp.sum(columns.astype(F32), axis=-1, keepdims=True)


def bias_of(by_row, by_column):
    count = by_row.shape[0]
    row = lax.broadcasted_iota(I32, (count, count), 0)
    column = lax.broadcasted_iota(I32, (count, count), 1)
    allowed = (by_row == by_column) & (row >= column)
    return jnp.where(allowed, 0.0, -1000000000.0)


def half_masks():
    lane = lax.broadcasted_iota(I32, (1, 2 * HEAD_DIM), 1)
    first = jnp.where(lane < HEAD_DIM, 1.0, 0.0)
    return first.astype(BF), (1.0 - first).astype(BF)


BEFORE = []


def smallest(outs):
    return min(outs, key=lambda a: a.size * a.dtype.itemsize)


def call(kernel, outs, args, spaces, scratch, name, flops, moved, after=(), results=None):
    where = {"v": pltpu.VMEM, "a": pl.ANY}
    after = list(after) + BEFORE
    read, waited = len(args), len(after)
    args, spaces = list(args) + list(after), spaces + "a" * waited

    def body(*refs):
        kernel(*refs[:read], *refs[read + waited :])

    got = pl.pallas_call(
        body,
        out_shape=outs,
        in_specs=[pl.BlockSpec(memory_space=where[s]) for s in spaces],
        out_specs=[pl.BlockSpec(memory_space=where[s]) for s in results or "v" * len(outs)],
        scratch_shapes=scratch,
        compiler_params=pltpu.CompilerParams(vmem_limit_bytes=VMEM_LIMIT if name in WIDE else VMEM_LIMIT // 2),
        cost_estimate=pl.CostEstimate(flops=COST[name] * 1150000000, bytes_accessed=1000, transcendentals=0),
        name=name,
    )(*args)
    BEFORE[:] = [smallest(got)]
    return got


class Weight:
    def __init__(self, arrays, copies, shape):
        self.arrays, self.copies, self.shape = arrays, copies, shape

    def scratch(self):
        return [pltpu.VMEM(self.shape, BF), pltpu.SemaphoreType.DMA((len(self.copies),))]

    def start(self, refs, whole, sems):
        me = lax.axis_index("expert")
        running = []
        for i, (index, source, place) in enumerate(self.copies):
            copy = pltpu.make_async_copy(
                refs[index].at[source], whole.at[place(me)], sems.at[i]
            )
            copy.start()
            running.append(copy)
        return running


def row_place(k, size, offset, rows, step):
    def place(me):
        if k is None:
            return (pl.ds(offset, rows),)
        return (pl.ds(pl.multiple_of((me ^ k) * size + offset, step), rows),)

    return place


def column_place(k, size, offset, rows):
    def place(me):
        if k is None:
            return (pl.ds(0, rows),)
        start = pl.multiple_of((me ^ k) * size, 128)
        return (pl.ds(offset, rows), pl.ds(start, size))

    return place


class Links:
    def __init__(self, n, m):
        self.n, self.m = n, m
        self.cube = n == 8
        self.line = m == 4
        self.second = ()

    def hop(self, value, bit):
        return lax.ppermute(value, "expert", [(i, i ^ bit) for i in range(self.n)])

    def gated(self, value, gate):
        return lax.optimization_barrier((value, *gate))[0] if gate else value

    def start(self, shard, gate=()):
        if not self.cube:
            return [shard]
        shard = self.gated(shard, gate)
        return [shard, self.hop(shard, 2), self.hop(shard, 4)]

    def pieces(self, started, gate=()):
        shard, by_x, by_y = lax.optimization_barrier((*started, *gate))[:3] if gate else started
        half = shard.shape[0] // 2 // 16 * 16
        far_a = self.hop(by_y[:half], 2)
        far_b = self.hop(by_x[half:], 4)
        self.second = (far_a, far_b)
        return [
            (0, 0, shard), (1, 0, self.hop(shard, 1)), (2, 0, by_x), (3, 0, self.hop(by_x, 1)),
            (4, 0, by_y), (5, 0, self.hop(by_y, 1)), (6, 0, far_a), (6, half, far_b),
            (7, 0, self.hop(far_a, 1)), (7, half, self.hop(far_b, 1)),
        ]

    def by_rows(self, sizes, started, gate=()):
        group = started[0]
        weights, first = [], 0
        if not self.cube:
            whole = lax.all_gather(group, "expert", axis=0, tiled=False)
            for size in sizes:
                part = whole[:, first : first + size].reshape(-1, group.shape[1])
                copies = [(0, (pl.ds(0, part.shape[0]),), row_place(None, 0, 0, part.shape[0], 8))]
                weights.append(Weight([part], copies, part.shape))
                first += size
            return weights
        pieces = self.pieces(started, gate)
        for size in sizes:
            arrays, copies = [], []
            for k, row, array in pieces:
                low, high = max(first, row), min(first + size, row + array.shape[0])
                if low < high:
                    source = (pl.ds(low - row, high - low),)
                    place = row_place(k, size, low - first, high - low, 16 if size % 16 == 0 else 8)
                    copies.append((len(arrays), source, place))
                    arrays.append(array)
            weights.append(Weight(arrays, copies, (self.n * size, group.shape[1])))
            first += size
        return weights

    def by_columns(self, started, gate=()):
        shard = started[0]
        rows, size = shard.shape
        if not self.cube:
            whole = lax.all_gather(shard, "expert", axis=1, tiled=True)
            return Weight([whole], [(0, (pl.ds(0, rows),), column_place(None, 0, 0, rows))], whole.shape)
        arrays, copies = [], []
        for k, row, array in self.pieces(started, gate):
            source = (pl.ds(0, array.shape[0]),)
            copies.append((len(arrays), source, column_place(k, size, row, array.shape[0])))
            arrays.append(array)
        return Weight(arrays, copies, (rows, self.n * size))

    def exchange(self, rows, gate=()):
        blocks = self.gated(rows, gate).reshape(self.n, -1, rows.shape[1])
        got = lax.all_to_all(blocks, "expert", split_axis=0, concat_axis=0, tiled=True)
        return got.reshape(rows.shape)

    def sum_shapes(self, rows, width):
        if not self.cube:
            return [jax.ShapeDtypeStruct((self.n, rows, width), BF)]
        return [jax.ShapeDtypeStruct((self.n // 2, rows, width), BF)] * 2

    def write_sum(self, refs, whole, first, size):
        for k in range(self.n):
            if self.cube:
                me = lax.axis_index("expert")
                step = 16 if size % 16 == 0 else 8
                start = pl.multiple_of((me ^ k) * size, step)
                refs[k % 2][k // 2, first : first + size] = whole[pl.ds(start, size)]
            else:
                refs[0][k, first : first + size] = whole[k * size : (k + 1) * size]

    def twins(self, blocks):
        return [self.hop(blocks[1], 1)] if self.cube else []

    def fold(self, groups, twins, name="fold"):
        if not self.cube:
            return [jnp.concatenate([g[0] for g in groups], axis=1)]
        rows = [g[0].shape[1] for g in groups]
        total, columns = sum(rows), groups[0][0].shape[2]
        half = total // 2 // 16 * 16

        def kernel(*refs):
            count = len(groups)
            outs = refs[2 * count :]
            first = 0
            for even, odd in zip(refs[:count], refs[count : 2 * count]):
                for m in range(4):
                    value = (even[m].astype(F32) + odd[m].astype(F32)).astype(BF)
                    low, high = first, first + even.shape[1]
                    cut = min(max(half, low), high)
                    if low < cut:
                        outs[m % 2][m // 2, low:cut] = value[: cut - low]
                    if cut < high:
                        outs[2 + m // 2][m % 2, cut - half : high - half] = value[cut - low :]
                first += even.shape[1]

        outs = [jax.ShapeDtypeStruct((2, half, columns), BF)] * 2
        outs += [jax.ShapeDtypeStruct((2, total - half, columns), BF)] * 2
        args = [g[0] for g in groups] + list(twins)
        return list(call(kernel, outs, args, "v" * len(args), [], name, 0, 0))

    def across(self, kept):
        return [self.hop(kept[1], 2), self.hop(kept[3], 4)] if self.cube else []

    def fold_again(self, kept, got, name="fold_again"):
        if not self.cube:
            return kept

        def kernel(first, got_first, second, got_second, *outs):
            for i, (mine, other) in enumerate(((first, got_first), (second, got_second))):
                for j in range(2):
                    outs[2 * i + j][...] = (mine[j].astype(F32) + other[j].astype(F32)).astype(BF)

        outs = [jax.ShapeDtypeStruct(a.shape[1:], BF) for a in (kept[0], kept[0], kept[2], kept[2])]
        args = [kept[0], got[0], kept[2], got[1]]
        return list(call(kernel, outs, args, "vvvv", [], name, 0, 0))

    def across_again(self, kept):
        return [self.hop(kept[1], 4), self.hop(kept[3], 2)] if self.cube else []

    def fold_last(self, kept, got):
        if not self.cube:
            return lax.psum_scatter(kept[0], "expert", scatter_dimension=0, tiled=True)[0]
        half = kept[0].shape[0]

        def kernel(first, got_first, second, got_second, out):
            out[:half] = (first[...].astype(F32) + got_first[...].astype(F32)).astype(BF)
            out[half:] = (second[...].astype(F32) + got_second[...].astype(F32)).astype(BF)

        rows = half + kept[2].shape[0]
        outs = [jax.ShapeDtypeStruct((rows, kept[0].shape[1]), BF)]
        return call(kernel, outs, [kept[0], got[0], kept[2], got[1]], "vvvv", [], "fold_last", 0, 0)[0]

    def along(self, value, pairs):
        return lax.ppermute(value, "dp", pairs)

    def inward(self, value):
        return [self.along(value, [(0, 1), (3, 2)])] if self.line else []

    def middle(self, value):
        return [self.along(value, [(1, 2), (2, 1)])] if self.line else []

    def outward(self, value):
        return [self.along(value, [(1, 0), (2, 3)])] if self.line else []

    def joined(self, value, got):
        if not self.line:
            return value

        def kernel(mine, other, out):
            out[...] = (mine[...].astype(F32) + other[...].astype(F32)).astype(BF)

        outs = [jax.ShapeDtypeStruct(value.shape, BF)]
        return call(kernel, outs, [value, got[0]], "vv", [], "joined", 0, 0)[0]

    def settled(self, value, got):
        if not self.line:
            return lax.psum(value, "dp").astype(F32)

        def kernel(mine, other, out):
            place = lax.axis_index("dp")

            def write(ref):
                out[...] = ref[...].astype(F32)

            middle = (place == 1) | (place == 2)
            pl.when(middle)(lambda: write(mine))
            pl.when(jnp.logical_not(middle))(lambda: write(other))

        outs = [jax.ShapeDtypeStruct(value.shape, F32)]
        return call(kernel, outs, [value, got[0]], "vv", [], "settle", 0, 0)[0]

    def settled_small(self, value, got, columns, cols):
        n = self.n
        rows = [(columns, 3), (columns + 3, 3), (columns + 6, n)]
        if not self.line:
            value = lax.psum(value, "dp").astype(F32)
            return [value[:columns]] + [value[i : i + size, :cols] for i, size in rows]

        def kernel(mine, other, out, *smalls):
            place = lax.axis_index("dp")

            def write(ref):
                out[...] = ref[:columns].astype(F32)
                rest = ref[columns:, :128].astype(F32)
                for (i, size), small in zip(rows, smalls):
                    small[...] = rest[i - columns : i - columns + size, :cols]

            middle = (place == 1) | (place == 2)
            pl.when(middle)(lambda: write(mine))
            pl.when(jnp.logical_not(middle))(lambda: write(other))

        outs = [jax.ShapeDtypeStruct((columns, value.shape[1]), F32)]
        outs += [jax.ShapeDtypeStruct((size, cols), F32) for _, size in rows]
        return call(kernel, outs, [value, got[0]], "vv", [], "settle", 0, 0)

    def settled_across(self, value, got, units):
        if not self.line:
            value = lax.psum(value, "dp").astype(F32)
            return value[:units].T, value[units:]

        def kernel(mine, other, up, out):
            place = lax.axis_index("dp")

            def write(ref):
                up[...] = ref[:units].astype(F32).T
                out[...] = ref[units:].astype(F32)

            middle = (place == 1) | (place == 2)
            pl.when(middle)(lambda: write(mine))
            pl.when(jnp.logical_not(middle))(lambda: write(other))

        rows, width = value.shape
        outs = [jax.ShapeDtypeStruct((width, units), F32), jax.ShapeDtypeStruct((rows - units, width), F32)]
        return call(kernel, outs, [value, got[0]], "vv", [], "settle", 0, 0)


def finish(parts):
    width = parts[0].shape[1]

    def kernel(*refs):
        ups, downs = refs[-2:]
        first = 0
        for ref in refs[:-2]:
            for i, out in enumerate((ups, downs)):
                out[:, first : first + ref.shape[2]] = ref[i].astype(F32)
            first += ref.shape[2]

    outs = [jax.ShapeDtypeStruct((width, sum(p.shape[2] for p in parts)), F32)] * 2
    return call(kernel, outs, parts, "v" * len(parts), [], "finish", 0, 0)


def prepare(links, routes, cotangent, capacity):
    count, width = cotangent.shape
    n = links.n
    total = n * capacity

    def kernel(by_row, by_column, cot, row_out, column_out, out):
        route_c, route_r = by_row[...], by_column[...]
        token = lax.broadcasted_iota(I32, (count, count), 0)
        other = lax.broadcasted_iota(I32, (count, count), 1)
        same = route_c == route_r
        rank_c = jnp.sum(jnp.where(same & (other < token), 1.0, 0.0), axis=1, keepdims=True)
        rank_r = jnp.sum(jnp.where(same & (token < other), 1.0, 0.0), axis=0, keepdims=True)
        slot_c = route_c * capacity + rank_c.astype(I32)
        slot_r = route_r * capacity + rank_r.astype(I32)
        column_out[...] = slot_c
        row_out[...] = slot_r
        place = lax.broadcasted_iota(I32, (total, count), 0)
        to_slots = jnp.where(place == slot_r, 1.0, 0.0).astype(BF)
        out[...] = mm(to_slots, cot[...]).astype(BF)

    outs = [jax.ShapeDtypeStruct((1, count), I32), jax.ShapeDtypeStruct((count, 1), I32)]
    outs.append(jax.ShapeDtypeStruct((total, width), BF))
    args = [routes, routes.reshape(1, count), cotangent]
    return call(
        kernel, outs, args, "vvv", [], "prepare", 2 * total * count * width, 4 * total * width
    )


def attend(n, tokens, segments, weight_small, weight_in, weight_out, after):
    count, width = tokens.shape
    pairs = width // (2 * HEAD_DIM)
    block = 128
    n_small, n_in, n_out = len(weight_small.arrays), len(weight_in.arrays), len(weight_out.arrays)
    small_rows, cols = weight_small.shape[0] // n, width // n

    def kernel(tok, seg_c, seg_r, *refs):
        small_refs, refs = refs[:n_small], refs[n_small:]
        in_refs, refs = refs[:n_in], refs[n_in:]
        out_refs, refs = refs[:n_out], refs[n_out:]
        first_ref, proj, mixed, lse, after_ref, second_ref, small_ref = refs[:7]
        w_small, small_sems, w_in, in_sems, w_out, out_sems, bias = refs[7:]
        small_copies = weight_small.start(small_refs, w_small, small_sems)
        in_copies = weight_in.start(in_refs, w_in, in_sems)
        out_copies = weight_out.start(out_refs, w_out, out_sems)
        rows = tok[...].astype(F32)
        normal, _ = normalize(rows)
        source = lax.broadcasted_iota(I32, (cols, width), 0)
        place = lax.broadcasted_iota(I32, (cols, width), 1)
        for copy in small_copies:
            copy.wait()
        small = jnp.zeros((small_rows, width), F32)
        for j in range(n):
            spread = jnp.where(place == source + j * cols, 1.0, 0.0).astype(BF)
            small += mm(w_small[j * small_rows : (j + 1) * small_rows, :cols], spread)
        small_ref[...] = small
        first = (normal * small_ref[0:1] + small_ref[3:4]).astype(BF)
        first_ref[...] = first
        bias[...] = bias_of(seg_c[...], seg_r[...])
        lse[...] = jnp.zeros_like(lse)
        for copy in in_copies:
            copy.wait()
        proj[...] = mm_t(first, w_in[...]).astype(BF)
        masks = half_masks()
        lane = lax.broadcasted_iota(I32, (block, 128), 1)

        def pair(i, carry):
            at = [pl.ds(pl.multiple_of(part * width + 128 * i, 128), 128) for part in range(3)]
            for b in range(count // block):
                mine, keys = pl.ds(b * block, block), pl.ds(0, (b + 1) * block)
                q, k, v = proj[mine, at[0]] * 0.125, proj[keys, at[1]], proj[keys, at[2]]
                got = jnp.zeros((block, 128), F32)
                kept = lse[mine]
                for h in range(2):
                    scores = mm_t(q * masks[h], k) + bias[mine, keys]
                    top = jnp.max(scores, axis=1, keepdims=True)
                    lifted = jnp.exp(scores - top)
                    totals = jnp.sum(lifted, axis=1, keepdims=True)
                    probs = (lifted * (1.0 / totals)).astype(BF)
                    got += mm(probs, v * masks[h])
                    kept = jnp.where(lane == 2 * i + h, top + jnp.log(totals), kept)
                lse[mine] = kept
                mixed[mine, at[0]] = got.astype(BF)
            return carry

        lax.fori_loop(0, pairs, pair, 0)
        for copy in out_copies:
            copy.wait()
        after = rows + mm_t(mixed[...], w_out[...])
        after_ref[...] = after
        normal, _ = normalize(after)
        second_ref[...] = (normal * small_ref[1:2] + small_ref[4:5]).astype(BF)

    shape = jax.ShapeDtypeStruct
    outs = [
        shape((count, width), BF), shape((count, 3 * width), BF), shape((count, width), BF),
        shape((count, 128), F32), shape((count, width), F32), shape((count, width), BF),
        shape((small_rows, width), F32),
    ]
    args = [tokens, segments.reshape(count, 1), segments]
    args += weight_small.arrays + weight_in.arrays + weight_out.arrays
    spaces = "vvv" + "a" * (n_small + n_in + n_out)
    scratch = weight_small.scratch() + weight_in.scratch() + weight_out.scratch() + [pltpu.VMEM((count, count), F32)]
    flops = 2 * count * width * (4 * width + 2 * count) * 2
    return call(kernel, outs, args, spaces, scratch, "attend", flops, 12 * count * width * 4, after)


def widen(second_in, weight_up, after):
    count = second_in.shape[0]
    hidden = weight_up.shape[1]
    pieces = len(weight_up.arrays)
    part = hidden // 4

    def kernel(second, *refs):
        up_refs, (act_ref, slope_ref, up, sems) = refs[:pieces], refs[pieces:]
        for copy in weight_up.start(up_refs, up, sems):
            copy.wait()
        rows = second[...]
        for i in range(4):
            at = pl.ds(i * part, part)
            value, slope = smooth_and_slope(mm(rows, up[:, at]))
            act_ref[:, at] = value.astype(BF)
            slope_ref[:, at] = slope.astype(BF)

    outs = [jax.ShapeDtypeStruct((count, hidden), BF)] * 2
    args = [second_in] + weight_up.arrays
    return call(
        kernel, outs, args, "v" + "a" * pieces, weight_up.scratch(), "widen",
        4 * count * hidden * second_in.shape[1], 8 * count * hidden, after,
    )


def dispatch(links, activated, after_attn, small, row_slots, routes, weight_down, total, after):
    count, width = after_attn.shape
    n = links.n
    pieces = len(weight_down.arrays)

    def kernel(act, after, small_ref, slot_r, route_c, *refs):
        down_refs, refs = refs[:pieces], refs[pieces:]
        hidden_ref, gates_ref, sent_ref = refs[:-2]
        down, sems = refs[-2:]
        for copy in weight_down.start(down_refs, down, sems):
            copy.wait()
        hidden = after[...] + mm_t(act[...], down[...])
        hidden_ref[...] = hidden
        normal, _ = normalize(hidden)
        moe_in = normal * small_ref[2:3] + small_ref[5:6]
        lane = lax.broadcasted_iota(I32, (count, n), 1)
        onehot = jnp.where(lane == route_c[...], 1.0, 0.0).astype(BF)
        chosen = mm(onehot, small_ref[6 : 6 + n].astype(BF))
        logit = jnp.sum(moe_in * chosen, axis=1, keepdims=True)
        gates = 1.0 / (1.0 + jnp.exp(-logit))
        gates_ref[...] = gates
        sent = jnp.concatenate([moe_in.astype(BF), scalar_columns(gates)], axis=1)
        place = lax.broadcasted_iota(I32, (total, count), 0)
        to_slots = jnp.where(place == slot_r[...], 1.0, 0.0).astype(BF)
        sent_ref[...] = mm(to_slots, sent).astype(BF)

    shape = jax.ShapeDtypeStruct
    outs = [shape((count, width), F32), shape((count, 1), F32)]
    outs.append(shape((total, width + EXTRA), BF))
    args = [activated, after_attn, small, row_slots, routes] + weight_down.arrays
    return call(
        kernel, outs, args, "vvvvv" + "a" * pieces, weight_down.scratch(), "dispatch",
        4 * count * width * 4 * width, 16 * count * width, after,
    )


def expert_rows(arrived, cots, width, after):
    total = arrived.shape[0]

    def kernel(arrived_ref, cot_ref, rows_ref, grads_ref, rows_across, grads_across):
        rows = arrived_ref[:, :width]
        rows_ref[...] = rows
        rows_across[...] = rows.T
        gates = columns_scalar(arrived_ref[:, width:])
        grads = (gates * cot_ref[...].astype(F32)).astype(BF)
        grads_ref[...] = grads
        grads_across[...] = grads.T

    outs = [jax.ShapeDtypeStruct((total, width), BF)] * 2 + [jax.ShapeDtypeStruct((width, total), BF)] * 2
    return call(kernel, outs, [arrived, cots], "vv", [], "expert_rows", 0, 0, after)


def expert(rows, grads, across, weights, sums, cot):
    total, width = rows.shape
    m, _, _, wide = weights.shape
    last, started = cot is not None, sums is not None
    group = m if last and m * wide <= 512 else 1
    steps, span = m // group, group * wide

    def kernel(rows_ref, grads_ref, rows_across, grads_across, *refs):
        refs = list(refs)
        take = lambda k: [refs.pop(0) for _ in range(k)]
        carried = take(2) if started else None
        (cot_ref,) = take(1) if last else (None,)
        (weight_ref,) = take(1)
        if last:
            outs, (acts, pre_grads) = take(2), take(2)
            held, sems, out_sum, row_sum = refs
        else:
            (w_grads,), outs = take(1), take(2)
            held, sems, out_sum, row_sum, grad_held, out_sems = refs
        entering = []
        for i in range(m):
            place = held.at[i // group, :, :, pl.ds(i % group * wide, wide)]
            entering.append(pltpu.make_async_copy(weight_ref.at[i], place, sems.at[i]))
        for copy in entering:
            copy.start()
        r, g = rows_ref[...], grads_ref[...]
        leaving = []
        for i in range(steps):
            for copy in entering[i * group : (i + 1) * group]:
                copy.wait()
            up, down = held[i, 0], held[i, 1]
            value, slope = smooth_and_slope(mm(r, up))
            act = value.astype(BF)
            pre_grad = (mm(g, down) * slope).astype(BF)
            row_part, out_part = mm_t(pre_grad, up), mm_t(act, down)
            if i == 0 and started:
                row_part, out_part = row_part + carried[0][...], out_part + carried[1][...]
            if i > 0:
                row_part, out_part = row_part + row_sum[...], out_part + out_sum[...]
            row_sum[...] = row_part
            out_sum[...] = out_part
            if last:
                acts[i] = act
                pre_grads[i] = pre_grad
            else:
                grad_held[i, 0] = mm(rows_across[...], pre_grad).astype(BF)
                grad_held[i, 1] = mm(grads_across[...], act).astype(BF)
                copy = pltpu.make_async_copy(grad_held.at[i], w_grads.at[i], out_sems.at[i])
                copy.start()
                leaving.append(copy)
        if last:
            result = out_sum[...].astype(BF)
            gate_grad = jnp.sum(cot_ref[...].astype(F32) * result.astype(F32), axis=1, keepdims=True)
            outs[0][...] = jnp.concatenate([row_sum[...].astype(BF), scalar_columns(gate_grad)], axis=1)
            outs[1][...] = result
        else:
            outs[0][...] = row_sum[...]
            outs[1][...] = out_sum[...]
        for copy in leaving:
            copy.wait()

    shape = jax.ShapeDtypeStruct
    args = [rows, grads, *across] + (sums if started else []) + ([cot] if last else [])
    spaces = "v" * len(args) + "a"
    scratch = [
        pltpu.VMEM((steps, 2, width, span), BF), pltpu.SemaphoreType.DMA((m,)),
        pltpu.VMEM((total, width), F32), pltpu.VMEM((total, width), F32),
    ]
    if last:
        outs = [shape((total, width + EXTRA), BF), shape((total, width), BF)] + [shape((steps, total, span), BF)] * 2
        return call(kernel, outs, args + [weights], spaces, scratch, "expert_last", 0, 0)
    outs = [shape((m, 2, width, wide), BF)] + [shape((total, width), F32)] * 2
    scratch += [pltpu.VMEM((m, 2, width, wide), BF), pltpu.SemaphoreType.DMA((m,))]
    return call(kernel, outs, args + [weights], spaces, scratch, "expert", 0, 0, [], "avv")


def expert_grads(m, across, acts, pre_grads):
    steps, _, span = acts.shape
    width = across[0].shape[0]
    group = m // steps
    wide = span // group

    def kernel(rows_across, grads_across, acts_ref, pre_ref, out):
        for i in range(steps):
            ups = mm(rows_across[...], pre_ref[i]).astype(BF)
            downs = mm(grads_across[...], acts_ref[i]).astype(BF)
            for j in range(group):
                out[i * group + j, 0] = ups[:, j * wide : (j + 1) * wide]
                out[i * group + j, 1] = downs[:, j * wide : (j + 1) * wide]

    outs = [jax.ShapeDtypeStruct((m, 2, width, wide), BF)]
    return call(kernel, outs, [*across, acts, pre_grads], "vvvv", [], "expert_grads", 0, 0)[0]


def combine(returned, slots, hidden, gates):
    count, width = hidden.shape

    def kernel(slot_c, hidden_ref, gates_ref, got_ref, out):
        got = got_ref[...]
        place = lax.broadcasted_iota(I32, (count, got.shape[0]), 1)
        pick = jnp.where(place == slot_c[...], 1.0, 0.0).astype(BF)
        out[...] = (hidden_ref[...] + gates_ref[...] * mm(pick, got)).astype(BF)

    return call(
        kernel, [jax.ShapeDtypeStruct((count, width), BF)], [slots, hidden, gates, returned],
        "vvvv", [], "combine", 4 * count * count * width, 10 * count * width,
    )[0]


def gate_back(links, back, slots, routes, hidden, gates, small, cotangent, activated):
    count, width = hidden.shape
    n = links.n
    size = width // n
    units = activated.shape[1]

    def kernel(slot_c, route_c, hidden_ref, gates_ref, small_ref, cot, act, back_ref, *refs):
        got = back_ref[...]
        hidden_grad_ref, down_in_ref, small_out, centroid_out, *sums = refs[:-1]
        whole = refs[-1]
        place = lax.broadcasted_iota(I32, (count, got.shape[0]), 1)
        pick = jnp.where(place == slot_c[...], 1.0, 0.0).astype(BF)
        got = mm(pick, got)
        gates = gates_ref[...]
        logit_grad = columns_scalar(got[:, width:]) * gates * (1.0 - gates)
        lane = lax.broadcasted_iota(I32, (count, n), 1)
        onehot = jnp.where(lane == route_c[...], 1.0, 0.0).astype(BF)
        chosen = mm(onehot, small_ref[6 : 6 + n].astype(BF))
        normal, inverse = normalize(hidden_ref[...])
        gain = small_ref[2:3]
        moe_in = normal * gain + small_ref[5:6]
        terms = split3(logit_grad * moe_in)
        centroid_out[...] = t_mm(onehot, terms[0]) + t_mm(onehot, terms[1]) + t_mm(onehot, terms[2])
        moe_grad = got[:, :width] + logit_grad * chosen
        part, gain_grad, shift_grad = normalize_back(moe_grad, normal, inverse, gain)
        small_out[...] = jnp.concatenate([gain_grad, shift_grad], axis=0)
        hidden_grad = cot[...].astype(F32) + part
        hidden_grad_ref[...] = hidden_grad
        down_in = hidden_grad.astype(BF)
        down_in_ref[...] = down_in
        whole[...] = t_mm(down_in, act[...]).astype(BF)
        links.write_sum(sums, whole, 0, size)

    shape = jax.ShapeDtypeStruct
    outs = [
        shape((count, width), F32), shape((count, width), BF), shape((2, width), F32), shape((n, width), F32),
    ] + links.sum_shapes(size, units)
    args = [slots, routes, hidden, gates, small, cotangent, activated, back]
    hidden_grad, down_in, small_out, centroid_out, *sums = call(
        kernel, outs, args, "v" * len(args), [pltpu.VMEM((width, units), BF)], "gate_back",
        2 * count * width * units * 2, 8 * count * units,
    )
    return hidden_grad, down_in, small_out, centroid_out, sums


def widen_back(links, down_in, slope, second_in, weight_down):
    count, width = down_in.shape
    units = slope.shape[1]
    size = units // links.n
    pieces = len(weight_down.arrays)

    def kernel(down_in_ref, slope_ref, second, *refs):
        down_refs, refs = refs[:pieces], refs[pieces:]
        grad, *sums = refs[:-3]
        down, sems, whole = refs[-3:]
        for copy in weight_down.start(down_refs, down, sems):
            copy.wait()
        rows = down_in_ref[...]
        part = units // 4
        for i in range(4):
            at = pl.ds(i * part, part)
            piece = (mm(rows, down[:, at]) * slope_ref[:, at].astype(F32)).astype(BF)
            grad[:, at] = piece
            whole[at] = t_mm(piece, second[...]).astype(BF)
        links.write_sum(sums, whole, 0, size)

    outs = [jax.ShapeDtypeStruct((count, units), BF)] + links.sum_shapes(size, width)
    args = [down_in, slope, second_in]
    spaces = "vvv" + "a" * pieces
    scratch = weight_down.scratch() + [pltpu.VMEM((units, width), BF)]
    grad, *sums = call(
        kernel, outs, args + weight_down.arrays, spaces, scratch, "widen_back",
        4 * count * width * units, 8 * width * units,
    )
    return grad, sums


def second_back(links, widened_grad, after_attn, hidden_grad, mixed, small, weight_up, after):
    count, width = after_attn.shape
    n = links.n
    size = width // n
    pieces = len(weight_up.arrays)

    def kernel(grad, after_ref, hidden_grad_ref, mixed_ref, small_ref, *refs):
        up_refs, refs = refs[:pieces], refs[pieces:]
        after_grad_ref, attn_grad_ref, small_out, *sums = refs[:-3]
        up, sems, whole = refs[-3:]
        copies = weight_up.start(up_refs, up, sems)
        normal, inverse = normalize(after_ref[...])
        for copy in copies:
            copy.wait()
        second_grad = mm_t(grad[...], up[...])
        back, gain_grad, shift_grad = normalize_back(second_grad, normal, inverse, small_ref[1:2])
        small_out[...] = jnp.concatenate([gain_grad, shift_grad], axis=0)
        after_grad = hidden_grad_ref[...] + back
        after_grad_ref[...] = after_grad
        attn_grad = after_grad.astype(BF)
        attn_grad_ref[...] = attn_grad
        whole[...] = t_mm(attn_grad, mixed_ref[...]).astype(BF)
        links.write_sum(sums, whole, 0, size)

    shape = jax.ShapeDtypeStruct
    outs = [shape((count, width), F32), shape((count, width), BF), shape((2, width), F32)]
    outs += links.sum_shapes(size, width)
    args = [widened_grad, after_attn, hidden_grad, mixed, small]
    spaces = "vvvvv" + "a" * pieces
    scratch = weight_up.scratch() + [pltpu.VMEM((width, width), BF)]
    after_grad, attn_grad, small_out, *sums = call(
        kernel, outs, args + weight_up.arrays, spaces, scratch, "second_back",
        2 * count * width * 4 * width, 8 * width * 4 * width, after,
    )
    return after_grad, attn_grad, small_out, sums


def attend_back(attn_grad, projected, lse, segments, weight_out, after):
    count, width = attn_grad.shape
    pairs = width // (2 * HEAD_DIM)
    block = 128
    blocks = count // block
    n_out = len(weight_out.arrays)

    def kernel(attn_ref, proj, lse, seg_c, seg_r, *refs):
        out_refs, refs = refs[:n_out], refs[n_out:]
        grad, w_out, out_sems, bias, mixed_grad = refs
        copies = weight_out.start(out_refs, w_out, out_sems)
        bias[...] = bias_of(seg_c[...], seg_r[...])
        for copy in copies:
            copy.wait()
        mixed_grad[...] = mm(attn_ref[...], w_out[...]).astype(BF)
        masks = half_masks()
        lane = lax.broadcasted_iota(I32, (block, 128), 1)

        def pair(i, carry):
            at = [pl.ds(pl.multiple_of(part * width + 128 * i, 128), 128) for part in range(3)]
            k_grad = [jnp.zeros((block, 128), F32) for _ in range(blocks)]
            v_grad = [jnp.zeros((block, 128), F32) for _ in range(blocks)]
            for b in range(blocks):
                mine, keys = pl.ds(b * block, block), pl.ds(0, (b + 1) * block)
                q, k, v = proj[mine, at[0]] * 0.125, proj[keys, at[1]], proj[keys, at[2]]
                upper = mixed_grad[mine, at[0]]
                kept = lse[mine]
                q_grad = jnp.zeros((block, 128), F32)
                for h in range(2):
                    q_h, upper_h = q * masks[h], upper * masks[h]
                    log_total = jnp.sum(jnp.where(lane == 2 * i + h, kept, 0.0), axis=1, keepdims=True)
                    probs = jnp.exp(mm_t(q_h, k) + bias[mine, keys] - log_total)
                    probs_grad = mm_t(upper_h, v)
                    mean = jnp.sum(probs * probs_grad, axis=1, keepdims=True)
                    scores_grad = (probs * (probs_grad - mean)).astype(BF)
                    q_grad += mm(scores_grad, k * masks[h])
                    dv = t_mm(probs.astype(BF), upper_h)
                    dk = t_mm(scores_grad, q_h)
                    for c in range(b + 1):
                        v_grad[c] += dv[c * block : (c + 1) * block]
                        k_grad[c] += dk[c * block : (c + 1) * block]
                grad[mine, at[0]] = (q_grad * 0.125).astype(BF)
            for c in range(blocks):
                mine = pl.ds(c * block, block)
                grad[mine, at[1]] = k_grad[c].astype(BF)
                grad[mine, at[2]] = v_grad[c].astype(BF)
            return carry

        lax.fori_loop(0, pairs, pair, 0)

    args = [attn_grad, projected, lse, segments.reshape(count, 1), segments]
    spaces = "v" * len(args) + "a" * n_out
    scratch = weight_out.scratch() + [pltpu.VMEM((count, count), F32), pltpu.VMEM((count, width), BF)]
    return call(
        kernel, [jax.ShapeDtypeStruct((count, 3 * width), BF)], args + weight_out.arrays, spaces, scratch,
        "attend_back", 2 * count * width * (width + 5 * count) * 2, 12 * count * width * 4, after,
    )[0]


def project_back(links, projected_grad, first_in, after):
    width = first_in.shape[1]
    size = 3 * width // links.n

    def kernel(grad, first, *refs):
        whole = refs[-1]
        whole[...] = t_mm(grad[...], first[...]).astype(BF)
        links.write_sum(refs[:-1], whole, 0, size)

    return call(
        kernel, links.sum_shapes(size, width), [projected_grad, first_in], "vv",
        [pltpu.VMEM((3 * width, width), BF)], "project_back", 6 * width**3, 12 * width * width, after,
    )


def tokens_back(links, projected_grad, tokens, after_grad, small, smalls, centroid_grad, weight_in, after):
    count, width = tokens.shape
    n, n_in = links.n, len(weight_in.arrays)
    cols, rows = width // n, small.shape[0]

    def kernel(grad, tok, after_ref, small_ref, small_2, small_3, centroids, *refs):
        in_refs, refs = refs[:n_in], refs[n_in:]
        out, *sums = refs[:-2]
        w_in, sems = refs[-2:]
        copies = weight_in.start(in_refs, w_in, sems)
        normal, inverse = normalize(tok[...].astype(F32))
        for copy in copies:
            copy.wait()
        first_grad = mm(grad[...], w_in[...])
        back, gain_grad, shift_grad = normalize_back(first_grad, normal, inverse, small_ref[0:1])
        out[...] = after_ref[...] + back
        parts = [gain_grad, small_2[0:1], small_3[0:1], shift_grad, small_2[1:2], small_3[1:2]]
        parts += [centroids[...], jnp.zeros((rows - 6 - n, width), F32)]
        both = jnp.concatenate(parts, axis=0).astype(BF)
        me = lax.axis_index("expert") if links.cube else 0
        source = lax.broadcasted_iota(I32, (128, width), 0)
        place = lax.broadcasted_iota(I32, (128, width), 1)
        for k in range(n):
            mine = (place == source + (me ^ k) * cols) & (source < cols)
            block = mm_t(both, jnp.where(mine, 1.0, 0.0).astype(BF)).astype(BF)
            ref, i = (sums[k % 2], k // 2) if links.cube else (sums[0], k)
            ref[i] = jnp.zeros((rows, width), BF)
            ref[i, :, :128] = block

    outs = [jax.ShapeDtypeStruct((count, width), F32)] + links.sum_shapes(rows, width)
    args = [projected_grad, tokens, after_grad, small, *smalls, centroid_grad]
    out, *sums = call(
        kernel, outs, args + weight_in.arrays, "v" * len(args) + "a" * n_in, weight_in.scratch(),
        "tokens_back", 6 * count * width * width, 20 * count * width, after,
    )
    return out, sums


def on_device(
    n, m, tokens, segments, routes, norm_gains, norm_shifts, project_in, project_out,
    dense_up, dense_down, centroids, expert_up, expert_down, cotangent,
):
    count, width = tokens.shape
    BEFORE.clear()
    capacity = 2 * count // n
    total = n * capacity
    own_hidden = expert_up.shape[2]
    links = Links(n, m)
    cols = width // n

    def chunk(start, wide):
        part = slice(start, start + wide)
        return jnp.concatenate([expert_up[0][:, part], expert_down[0][:, part]], axis=0)

    chunks = [640, 128] if own_hidden == 768 and m == 4 else [own_hidden]
    gathered, start = [], 0
    for wide in chunks:
        whole = lax.all_gather(chunk(start, wide), "dp", axis=0, tiled=True)
        gathered.append(whole.reshape(m, 2, width, wide))
        start += wide

    pad = -(6 + n) % 16
    small = jnp.concatenate([norm_gains, norm_shifts, centroids], axis=0)
    small = jnp.pad(small, ((0, pad), (0, width - cols)))
    group = [project_in.T, project_out.T, small]
    started = links.start(jnp.concatenate(group, axis=0))
    weight_in, weight_out, weight_small = links.by_rows([a.shape[0] for a in group], started)
    started_up = links.start(dense_up, links.second)
    started_down = links.start(dense_down.T, links.second)

    row_slots, slots, cots = prepare(links, routes, cotangent, capacity)
    first_in, projected, mixed, lse, after_attn, second_in, small = attend(
        n, tokens, segments, weight_small, weight_in, weight_out, []
    )
    weight_up = links.by_columns(started_up, [small])
    (weight_down,) = links.by_rows([cols], started_down, [small])
    cots = links.exchange(cots, links.second)
    activated, slope = widen(second_in, weight_up, [])
    hidden, gates, sent = dispatch(
        links, activated, after_attn, small, row_slots, routes, weight_down, total, [cots]
    )
    rows, grads, *across = expert_rows(links.exchange(sent), cots, width, [])

    sums, expert_sums = None, []
    for c, whole in enumerate(gathered):
        if c < len(chunks) - 1:
            w_grads, *sums = expert(rows, grads, across, whole, sums, None)
            expert_sums.append(w_grads)
        else:
            back, results, acts, pre_grads = expert(rows, grads, across, whole, sums, cots)
    back = links.exchange(back)
    expert_sums.append(expert_grads(m, across, acts, pre_grads))

    def own_sum(grads):
        sums = lax.psum_scatter(grads.reshape(-1, grads.shape[-1]), "dp", scatter_dimension=0, tiled=True)
        return sums.reshape(grads.shape[1:])

    summed = [own_sum(expert_sums[0])]
    returned = links.exchange(results, [back])

    hidden_grad, down_in, small_3, centroid_grad, sums_down = gate_back(
        links, back, slots, routes, hidden, gates, small, cotangent, activated
    )
    twin_down = links.twins(sums_down)
    widened_grad, sums_up = widen_back(links, down_in, slope, second_in, weight_down)
    twin_up = links.twins(sums_up)
    down = links.fold([sums_down], twin_down, "fold_wide")
    down_got = links.across(down)
    after_grad, attn_grad, small_2, sums_out = second_back(
        links, widened_grad, after_attn, hidden_grad, mixed, small, weight_up, [returned]
    )
    twin_out = links.twins(sums_out)
    projected_grad = attend_back(attn_grad, projected, lse, segments, weight_out, [])
    up = links.fold([sums_up, sums_out], twin_up + twin_out)
    up_got = links.across(up)
    down = links.fold_again(down, down_got)
    down_got = links.across_again(down)
    tokens_grad, sums_small = tokens_back(
        links, projected_grad, tokens, after_grad, small, [small_2, small_3], centroid_grad, weight_in, []
    )
    twin_small = links.twins(sums_small)
    for grads in expert_sums[1:]:
        summed.append(own_sum(links.gated(grads, summed + [sums_small[0]])))
    sums_in = project_back(links, projected_grad, first_in, [])
    twin_in = links.twins(sums_in)
    up = links.fold_again(up, up_got, "fold_wait")
    up_got = links.across_again(up)
    inner = links.fold([sums_in, sums_small], twin_in + twin_small)
    inner_got = links.across(inner)
    down = links.fold_last(down, down_got)
    down_got = links.inward(down)
    inner = links.fold_again(inner, inner_got)
    inner_got = links.across_again(inner)
    up = links.fold_last(up, up_got)
    up_got = links.inward(up)
    inner = links.fold_last(inner, inner_got)
    inner_got = links.inward(inner)
    output = combine(returned, slots, hidden, gates)
    down = links.joined(down, down_got)
    down_got = links.middle(down)
    up = links.joined(up, up_got)
    up_got = links.middle(up)
    inner = links.joined(inner, inner_got)
    inner_got = links.middle(inner)
    down = links.joined(down, down_got)
    down_got = links.outward(down)
    up = links.joined(up, up_got)
    up_got = links.outward(up)
    inner = links.joined(inner, inner_got)
    inner_got = links.outward(inner)
    expert_sums = finish(summed)
    down_sum = links.settled(down, down_got)
    units, columns = dense_up.shape[1], project_in.shape[1]
    up_sum, out_sum = links.settled_across(up, up_got, units)
    in_sum, gains_sum, shifts_sum, centroids_sum = links.settled_small(inner, inner_got, columns, cols)

    return (
        output, tokens_grad, gains_sum, shifts_sum, in_sum.T, out_sum.T, up_sum,
        down_sum.T, centroids_sum, expert_sums[0][None], expert_sums[1][None],
    )


def solution(mesh):
    sizes = dict(mesh.shape)
    both, over = P(("dp", "expert"), None), P(None, "expert")
    expert_place = P("expert", None, "dp")
    return jax.shard_map(
        functools.partial(on_device, sizes["expert"], sizes["dp"]),
        mesh=mesh,
        in_specs=(both,) * 3 + (over,) * 7 + (expert_place,) * 2 + (both,),
        out_specs=(both,) * 2 + (over,) * 7 + (expert_place,) * 2,
        check_vma=False,
    )
```

```python
import functools

import jax
import jax.numpy as jnp
from jax import lax
from jax.experimental import pallas as pl
from jax.experimental.pallas import tpu as pltpu
from jax.sharding import PartitionSpec as P

HEAD_DIM = 64
EXTRA = 128
BF = jnp.bfloat16
F32 = jnp.float32
I32 = jnp.int32
ROOT = 0.7978845608028654
COST = dict(
    prepare=3, attend=16, widen=9, dispatch=10, expert_rows=4, expert=20, expert_last=10, expert_grads=6, gate_back=10, widen_back=12, fold=1,
    second_back=17, attend_back=2, fold_again=1, fold_wait=20, project_back=2, tokens_back=2, fold_last=1, joined=6,
    combine=1, finish=1, settle=1,
)
WIDE = ("attend", "widen", "dispatch", "expert", "expert_last", "expert_grads", "gate_back", "widen_back", "settle")
VMEM_LIMIT = 60 * 1024 * 1024


def mm(left, right):
    return lax.dot_general(left, right, (((1,), (0,)), ((), ())), preferred_element_type=F32)


def mm_t(left, right):
    return lax.dot_general(left, right, (((1,), (1,)), ((), ())), preferred_element_type=F32)


def t_mm(left, right):
    return lax.dot_general(left, right, (((0,), (0,)), ((), ())), preferred_element_type=F32)


def normalize(rows):
    share = 1.0 / rows.shape[-1]
    centred = rows - jnp.sum(rows, axis=-1, keepdims=True) * share
    spread = jnp.sum(centred * centred, axis=-1, keepdims=True) * share
    inverse = lax.rsqrt(spread + 1e-05)
    return centred * inverse, inverse


def normalize_back(grad, normal, inverse, gain):
    share = 1.0 / grad.shape[-1]
    scaled = grad * gain
    first = jnp.sum(scaled, axis=-1, keepdims=True) * share
    second = jnp.sum(scaled * normal, axis=-1, keepdims=True) * share
    rows = inverse * (scaled - first - normal * second)
    return rows, jnp.sum(grad * normal, axis=0, keepdims=True), jnp.sum(grad, axis=0, keepdims=True)


def smooth_and_slope(v):
    square = v * v
    bend = jnp.tanh(v * (ROOT + ROOT * 0.044715 * square))
    half = 0.5 + 0.5 * bend
    slope = half + 0.5 * v * (1.0 - bend * bend) * (ROOT + 3.0 * ROOT * 0.044715 * square)
    return v * half, slope


def split3(v):
    hi = v.astype(BF)
    rest = v - hi.astype(F32)
    mid = rest.astype(BF)
    return hi, mid, (rest - mid.astype(F32)).astype(BF)


def scalar_columns(v):
    hi, mid, low = split3(v)
    lane = lax.broadcasted_iota(I32, (v.shape[0], EXTRA), 1)
    out = jnp.where(lane == 0, hi.astype(F32), 0.0)
    out = jnp.where(lane == 1, mid.astype(F32), out)
    return jnp.where(lane == 2, low.astype(F32), out).astype(BF)


def columns_scalar(columns):
    return jnp.sum(columns.astype(F32), axis=-1, keepdims=True)


def bias_of(by_row, by_column):
    count = by_row.shape[0]
    row = lax.broadcasted_iota(I32, (count, count), 0)
    column = lax.broadcasted_iota(I32, (count, count), 1)
    allowed = (by_row == by_column) & (row >= column)
    return jnp.where(allowed, 0.0, -1000000000.0)


def half_masks():
    lane = lax.broadcasted_iota(I32, (1, 2 * HEAD_DIM), 1)
    first = jnp.where(lane < HEAD_DIM, 1.0, 0.0)
    return first.astype(BF), (1.0 - first).astype(BF)


BEFORE = []


def smallest(outs):
    return min(outs, key=lambda a: a.size * a.dtype.itemsize)


def call(kernel, outs, args, spaces, scratch, name, flops, moved, after=(), results=None):
    where = {"v": pltpu.VMEM, "a": pl.ANY}
    after = list(after) + BEFORE
    read, waited = len(args), len(after)
    args, spaces = list(args) + list(after), spaces + "a" * waited

    def body(*refs):
        kernel(*refs[:read], *refs[read + waited :])

    got = pl.pallas_call(
        body,
        out_shape=outs,
        in_specs=[pl.BlockSpec(memory_space=where[s]) for s in spaces],
        out_specs=[pl.BlockSpec(memory_space=where[s]) for s in results or "v" * len(outs)],
        scratch_shapes=scratch,
        compiler_params=pltpu.CompilerParams(vmem_limit_bytes=VMEM_LIMIT if name in WIDE else VMEM_LIMIT // 2),
        cost_estimate=pl.CostEstimate(flops=COST[name] * 1150000000, bytes_accessed=1000, transcendentals=0),
        name=name,
    )(*args)
    BEFORE[:] = [smallest(got)]
    return got


class Weight:
    def __init__(self, arrays, copies, shape):
        self.arrays, self.copies, self.shape = arrays, copies, shape

    def scratch(self):
        return [pltpu.VMEM(self.shape, BF), pltpu.SemaphoreType.DMA((len(self.copies),))]

    def start(self, refs, whole, sems):
        me = lax.axis_index("expert")
        running = []
        for i, (index, source, place) in enumerate(self.copies):
            copy = pltpu.make_async_copy(
                refs[index].at[source], whole.at[place(me)], sems.at[i]
            )
            copy.start()
            running.append(copy)
        return running


def row_place(k, size, offset, rows, step):
    def place(me):
        if k is None:
            return (pl.ds(offset, rows),)
        return (pl.ds(pl.multiple_of((me ^ k) * size + offset, step), rows),)

    return place


def column_place(k, size, offset, rows):
    def place(me):
        if k is None:
            return (pl.ds(0, rows),)
        start = pl.multiple_of((me ^ k) * size, 128)
        return (pl.ds(offset, rows), pl.ds(start, size))

    return place


class Links:
    def __init__(self, n, m):
        self.n, self.m = n, m
        self.cube = n == 8
        self.line = m == 4
        self.second = ()

    def hop(self, value, bit):
        return lax.ppermute(value, "expert", [(i, i ^ bit) for i in range(self.n)])

    def gated(self, value, gate):
        return lax.optimization_barrier((value, *gate))[0] if gate else value

    def start(self, shard, gate=()):
        if not self.cube:
            return [shard]
        shard = self.gated(shard, gate)
        return [shard, self.hop(shard, 2), self.hop(shard, 4)]

    def pieces(self, started, gate=()):
        shard, by_x, by_y = lax.optimization_barrier((*started, *gate))[:3] if gate else started
        half = shard.shape[0] // 2 // 16 * 16
        far_a = self.hop(by_y[:half], 2)
        far_b = self.hop(by_x[half:], 4)
        self.second = (far_a, far_b)
        return [
            (0, 0, shard), (1, 0, self.hop(shard, 1)), (2, 0, by_x), (3, 0, self.hop(by_x, 1)),
            (4, 0, by_y), (5, 0, self.hop(by_y, 1)), (6, 0, far_a), (6, half, far_b),
            (7, 0, self.hop(far_a, 1)), (7, half, self.hop(far_b, 1)),
        ]

    def by_rows(self, sizes, started, gate=()):
        group = started[0]
        weights, first = [], 0
        if not self.cube:
            whole = lax.all_gather(group, "expert", axis=0, tiled=False)
            for size in sizes:
                part = whole[:, first : first + size].reshape(-1, group.shape[1])
                copies = [(0, (pl.ds(0, part.shape[0]),), row_place(None, 0, 0, part.shape[0], 8))]
                weights.append(Weight([part], copies, part.shape))
                first += size
            return weights
        pieces = self.pieces(started, gate)
        for size in sizes:
            arrays, copies = [], []
            for k, row, array in pieces:
                low, high = max(first, row), min(first + size, row + array.shape[0])
                if low < high:
                    source = (pl.ds(low - row, high - low),)
                    place = row_place(k, size, low - first, high - low, 16 if size % 16 == 0 else 8)
                    copies.append((len(arrays), source, place))
                    arrays.append(array)
            weights.append(Weight(arrays, copies, (self.n * size, group.shape[1])))
            first += size
        return weights

    def by_columns(self, started, gate=()):
        shard = started[0]
        rows, size = shard.shape
        if not self.cube:
            whole = lax.all_gather(shard, "expert", axis=1, tiled=True)
            return Weight([whole], [(0, (pl.ds(0, rows),), column_place(None, 0, 0, rows))], whole.shape)
        arrays, copies = [], []
        for k, row, array in self.pieces(started, gate):
            source = (pl.ds(0, array.shape[0]),)
            copies.append((len(arrays), source, column_place(k, size, row, array.shape[0])))
            arrays.append(array)
        return Weight(arrays, copies, (rows, self.n * size))

    def exchange(self, rows, gate=()):
        blocks = self.gated(rows, gate).reshape(self.n, -1, rows.shape[1])
        got = lax.all_to_all(blocks, "expert", split_axis=0, concat_axis=0, tiled=True)
        return got.reshape(rows.shape)

    def sum_shapes(self, rows, width):
        if not self.cube:
            return [jax.ShapeDtypeStruct((self.n, rows, width), BF)]
        return [jax.ShapeDtypeStruct((self.n // 2, rows, width), BF)] * 2

    def write_sum(self, refs, whole, first, size):
        for k in range(self.n):
            if self.cube:
                me = lax.axis_index("expert")
                step = 16 if size % 16 == 0 else 8
                start = pl.multiple_of((me ^ k) * size, step)
                refs[k % 2][k // 2, first : first + size] = whole[pl.ds(start, size)]
            else:
                refs[0][k, first : first + size] = whole[k * size : (k + 1) * size]

    def twins(self, blocks):
        return [self.hop(blocks[1], 1)] if self.cube else []

    def fold(self, groups, twins):
        if not self.cube:
            return [jnp.concatenate([g[0] for g in groups], axis=1)]
        rows = [g[0].shape[1] for g in groups]
        total, columns = sum(rows), groups[0][0].shape[2]
        half = total // 2 // 16 * 16

        def kernel(*refs):
            count = len(groups)
            outs = refs[2 * count :]
            first = 0
            for even, odd in zip(refs[:count], refs[count : 2 * count]):
                for m in range(4):
                    value = (even[m].astype(F32) + odd[m].astype(F32)).astype(BF)
                    low, high = first, first + even.shape[1]
                    cut = min(max(half, low), high)
                    if low < cut:
                        outs[m % 2][m // 2, low:cut] = value[: cut - low]
                    if cut < high:
                        outs[2 + m // 2][m % 2, cut - half : high - half] = value[cut - low :]
                first += even.shape[1]

        outs = [jax.ShapeDtypeStruct((2, half, columns), BF)] * 2
        outs += [jax.ShapeDtypeStruct((2, total - half, columns), BF)] * 2
        args = [g[0] for g in groups] + list(twins)
        return list(call(kernel, outs, args, "v" * len(args), [], "fold", 0, 0))

    def across(self, kept):
        return [self.hop(kept[1], 2), self.hop(kept[3], 4)] if self.cube else []

    def fold_again(self, kept, got, name="fold_again"):
        if not self.cube:
            return kept

        def kernel(first, got_first, second, got_second, *outs):
            for i, (mine, other) in enumerate(((first, got_first), (second, got_second))):
                for j in range(2):
                    outs[2 * i + j][...] = (mine[j].astype(F32) + other[j].astype(F32)).astype(BF)

        outs = [jax.ShapeDtypeStruct(a.shape[1:], BF) for a in (kept[0], kept[0], kept[2], kept[2])]
        args = [kept[0], got[0], kept[2], got[1]]
        return list(call(kernel, outs, args, "vvvv", [], name, 0, 0))

    def across_again(self, kept):
        return [self.hop(kept[1], 4), self.hop(kept[3], 2)] if self.cube else []

    def fold_last(self, kept, got):
        if not self.cube:
            return lax.psum_scatter(kept[0], "expert", scatter_dimension=0, tiled=True)[0]
        half = kept[0].shape[0]

        def kernel(first, got_first, second, got_second, out):
            out[:half] = (first[...].astype(F32) + got_first[...].astype(F32)).astype(BF)
            out[half:] = (second[...].astype(F32) + got_second[...].astype(F32)).astype(BF)

        rows = half + kept[2].shape[0]
        outs = [jax.ShapeDtypeStruct((rows, kept[0].shape[1]), BF)]
        return call(kernel, outs, [kept[0], got[0], kept[2], got[1]], "vvvv", [], "fold_last", 0, 0)[0]

    def along(self, value, pairs):
        return lax.ppermute(value, "dp", pairs)

    def inward(self, value):
        return [self.along(value, [(0, 1), (3, 2)])] if self.line else []

    def middle(self, value):
        return [self.along(value, [(1, 2), (2, 1)])] if self.line else []

    def outward(self, value):
        return [self.along(value, [(1, 0), (2, 3)])] if self.line else []

    def joined(self, value, got):
        if not self.line:
            return value

        def kernel(mine, other, out):
            out[...] = (mine[...].astype(F32) + other[...].astype(F32)).astype(BF)

        outs = [jax.ShapeDtypeStruct(value.shape, BF)]
        return call(kernel, outs, [value, got[0]], "vv", [], "joined", 0, 0)[0]

    def settled(self, value, got):
        if not self.line:
            return lax.psum(value, "dp").astype(F32)

        def kernel(mine, other, out):
            place = lax.axis_index("dp")

            def write(ref):
                out[...] = ref[...].astype(F32)

            middle = (place == 1) | (place == 2)
            pl.when(middle)(lambda: write(mine))
            pl.when(jnp.logical_not(middle))(lambda: write(other))

        outs = [jax.ShapeDtypeStruct(value.shape, F32)]
        return call(kernel, outs, [value, got[0]], "vv", [], "settle", 0, 0)[0]

    def settled_small(self, value, got, columns, cols):
        n = self.n
        rows = [(columns, 3), (columns + 3, 3), (columns + 6, n)]
        if not self.line:
            value = lax.psum(value, "dp").astype(F32)
            return [value[:columns]] + [value[i : i + size, :cols] for i, size in rows]

        def kernel(mine, other, out, *smalls):
            place = lax.axis_index("dp")

            def write(ref):
                out[...] = ref[:columns].astype(F32)
                rest = ref[columns:, :128].astype(F32)
                for (i, size), small in zip(rows, smalls):
                    small[...] = rest[i - columns : i - columns + size, :cols]

            middle = (place == 1) | (place == 2)
            pl.when(middle)(lambda: write(mine))
            pl.when(jnp.logical_not(middle))(lambda: write(other))

        outs = [jax.ShapeDtypeStruct((columns, value.shape[1]), F32)]
        outs += [jax.ShapeDtypeStruct((size, cols), F32) for _, size in rows]
        return call(kernel, outs, [value, got[0]], "vv", [], "settle", 0, 0)

    def settled_across(self, value, got, units):
        if not self.line:
            value = lax.psum(value, "dp").astype(F32)
            return value[:units].T, value[units:]

        def kernel(mine, other, up, out):
            place = lax.axis_index("dp")

            def write(ref):
                up[...] = ref[:units].astype(F32).T
                out[...] = ref[units:].astype(F32)

            middle = (place == 1) | (place == 2)
            pl.when(middle)(lambda: write(mine))
            pl.when(jnp.logical_not(middle))(lambda: write(other))

        rows, width = value.shape
        outs = [jax.ShapeDtypeStruct((width, units), F32), jax.ShapeDtypeStruct((rows - units, width), F32)]
        return call(kernel, outs, [value, got[0]], "vv", [], "settle", 0, 0)


def finish(parts):
    width = parts[0].shape[1]

    def kernel(*refs):
        ups, downs = refs[-2:]
        first = 0
        for ref in refs[:-2]:
            for i, out in enumerate((ups, downs)):
                out[:, first : first + ref.shape[2]] = ref[i].astype(F32)
            first += ref.shape[2]

    outs = [jax.ShapeDtypeStruct((width, sum(p.shape[2] for p in parts)), F32)] * 2
    return call(kernel, outs, parts, "v" * len(parts), [], "finish", 0, 0)


def prepare(links, routes, cotangent, capacity):
    count, width = cotangent.shape
    n = links.n
    total = n * capacity

    def kernel(by_row, by_column, cot, row_out, column_out, out):
        route_c, route_r = by_row[...], by_column[...]
        token = lax.broadcasted_iota(I32, (count, count), 0)
        other = lax.broadcasted_iota(I32, (count, count), 1)
        same = route_c == route_r
        rank_c = jnp.sum(jnp.where(same & (other < token), 1.0, 0.0), axis=1, keepdims=True)
        rank_r = jnp.sum(jnp.where(same & (token < other), 1.0, 0.0), axis=0, keepdims=True)
        slot_c = route_c * capacity + rank_c.astype(I32)
        slot_r = route_r * capacity + rank_r.astype(I32)
        column_out[...] = slot_c
        row_out[...] = slot_r
        place = lax.broadcasted_iota(I32, (total, count), 0)
        to_slots = jnp.where(place == slot_r, 1.0, 0.0).astype(BF)
        out[...] = mm(to_slots, cot[...]).astype(BF)

    outs = [jax.ShapeDtypeStruct((1, count), I32), jax.ShapeDtypeStruct((count, 1), I32)]
    outs.append(jax.ShapeDtypeStruct((total, width), BF))
    args = [routes, routes.reshape(1, count), cotangent]
    return call(
        kernel, outs, args, "vvv", [], "prepare", 2 * total * count * width, 4 * total * width
    )


def attend(n, tokens, segments, weight_small, weight_in, weight_out, after):
    count, width = tokens.shape
    pairs = width // (2 * HEAD_DIM)
    block = 128
    n_small, n_in, n_out = len(weight_small.arrays), len(weight_in.arrays), len(weight_out.arrays)
    small_rows, cols = weight_small.shape[0] // n, width // n

    def kernel(tok, seg_c, seg_r, *refs):
        small_refs, refs = refs[:n_small], refs[n_small:]
        in_refs, refs = refs[:n_in], refs[n_in:]
        out_refs, refs = refs[:n_out], refs[n_out:]
        first_ref, proj, mixed, lse, after_ref, second_ref, small_ref = refs[:7]
        w_small, small_sems, w_in, in_sems, w_out, out_sems, bias = refs[7:]
        small_copies = weight_small.start(small_refs, w_small, small_sems)
        in_copies = weight_in.start(in_refs, w_in, in_sems)
        out_copies = weight_out.start(out_refs, w_out, out_sems)
        rows = tok[...].astype(F32)
        normal, _ = normalize(rows)
        source = lax.broadcasted_iota(I32, (cols, width), 0)
        place = lax.broadcasted_iota(I32, (cols, width), 1)
        for copy in small_copies:
            copy.wait()
        small = jnp.zeros((small_rows, width), F32)
        for j in range(n):
            spread = jnp.where(place == source + j * cols, 1.0, 0.0).astype(BF)
            small += mm(w_small[j * small_rows : (j + 1) * small_rows, :cols], spread)
        small_ref[...] = small
        first = (normal * small_ref[0:1] + small_ref[3:4]).astype(BF)
        first_ref[...] = first
        bias[...] = bias_of(seg_c[...], seg_r[...])
        lse[...] = jnp.zeros_like(lse)
        for copy in in_copies:
            copy.wait()
        proj[...] = mm_t(first, w_in[...]).astype(BF)
        masks = half_masks()
        lane = lax.broadcasted_iota(I32, (block, 128), 1)

        def pair(i, carry):
            at = [pl.ds(pl.multiple_of(part * width + 128 * i, 128), 128) for part in range(3)]
            for b in range(count // block):
                mine, keys = pl.ds(b * block, block), pl.ds(0, (b + 1) * block)
                q, k, v = proj[mine, at[0]] * 0.125, proj[keys, at[1]], proj[keys, at[2]]
                got = jnp.zeros((block, 128), F32)
                kept = lse[mine]
                for h in range(2):
                    scores = mm_t(q * masks[h], k) + bias[mine, keys]
                    top = jnp.max(scores, axis=1, keepdims=True)
                    lifted = jnp.exp(scores - top)
                    totals = jnp.sum(lifted, axis=1, keepdims=True)
                    probs = (lifted * (1.0 / totals)).astype(BF)
                    got += mm(probs, v * masks[h])
                    kept = jnp.where(lane == 2 * i + h, top + jnp.log(totals), kept)
                lse[mine] = kept
                mixed[mine, at[0]] = got.astype(BF)
            return carry

        lax.fori_loop(0, pairs, pair, 0)
        for copy in out_copies:
            copy.wait()
        after = rows + mm_t(mixed[...], w_out[...])
        after_ref[...] = after
        normal, _ = normalize(after)
        second_ref[...] = (normal * small_ref[1:2] + small_ref[4:5]).astype(BF)

    shape = jax.ShapeDtypeStruct
    outs = [
        shape((count, width), BF), shape((count, 3 * width), BF), shape((count, width), BF),
        shape((count, 128), F32), shape((count, width), F32), shape((count, width), BF),
        shape((small_rows, width), F32),
    ]
    args = [tokens, segments.reshape(count, 1), segments]
    args += weight_small.arrays + weight_in.arrays + weight_out.arrays
    spaces = "vvv" + "a" * (n_small + n_in + n_out)
    scratch = weight_small.scratch() + weight_in.scratch() + weight_out.scratch() + [pltpu.VMEM((count, count), F32)]
    flops = 2 * count * width * (4 * width + 2 * count) * 2
    return call(kernel, outs, args, spaces, scratch, "attend", flops, 12 * count * width * 4, after)


def widen(second_in, weight_up, after):
    count = second_in.shape[0]
    hidden = weight_up.shape[1]
    pieces = len(weight_up.arrays)
    part = hidden // 4

    def kernel(second, *refs):
        up_refs, (act_ref, slope_ref, up, sems) = refs[:pieces], refs[pieces:]
        for copy in weight_up.start(up_refs, up, sems):
            copy.wait()
        rows = second[...]
        for i in range(4):
            at = pl.ds(i * part, part)
            value, slope = smooth_and_slope(mm(rows, up[:, at]))
            act_ref[:, at] = value.astype(BF)
            slope_ref[:, at] = slope.astype(BF)

    outs = [jax.ShapeDtypeStruct((count, hidden), BF)] * 2
    args = [second_in] + weight_up.arrays
    return call(
        kernel, outs, args, "v" + "a" * pieces, weight_up.scratch(), "widen",
        4 * count * hidden * second_in.shape[1], 8 * count * hidden, after,
    )


def dispatch(links, activated, after_attn, small, row_slots, routes, weight_down, total, after):
    count, width = after_attn.shape
    n = links.n
    pieces = len(weight_down.arrays)

    def kernel(act, after, small_ref, slot_r, route_c, *refs):
        down_refs, refs = refs[:pieces], refs[pieces:]
        hidden_ref, gates_ref, sent_ref = refs[:-2]
        down, sems = refs[-2:]
        for copy in weight_down.start(down_refs, down, sems):
            copy.wait()
        hidden = after[...] + mm_t(act[...], down[...])
        hidden_ref[...] = hidden
        normal, _ = normalize(hidden)
        moe_in = normal * small_ref[2:3] + small_ref[5:6]
        lane = lax.broadcasted_iota(I32, (count, n), 1)
        onehot = jnp.where(lane == route_c[...], 1.0, 0.0).astype(BF)
        chosen = mm(onehot, small_ref[6 : 6 + n].astype(BF))
        logit = jnp.sum(moe_in * chosen, axis=1, keepdims=True)
        gates = 1.0 / (1.0 + jnp.exp(-logit))
        gates_ref[...] = gates
        sent = jnp.concatenate([moe_in.astype(BF), scalar_columns(gates)], axis=1)
        place = lax.broadcasted_iota(I32, (total, count), 0)
        to_slots = jnp.where(place == slot_r[...], 1.0, 0.0).astype(BF)
        sent_ref[...] = mm(to_slots, sent).astype(BF)

    shape = jax.ShapeDtypeStruct
    outs = [shape((count, width), F32), shape((count, 1), F32)]
    outs.append(shape((total, width + EXTRA), BF))
    args = [activated, after_attn, small, row_slots, routes] + weight_down.arrays
    return call(
        kernel, outs, args, "vvvvv" + "a" * pieces, weight_down.scratch(), "dispatch",
        4 * count * width * 4 * width, 16 * count * width, after,
    )


def expert_rows(arrived, cots, width, after):
    total = arrived.shape[0]

    def kernel(arrived_ref, cot_ref, rows_ref, grads_ref, rows_across, grads_across):
        rows = arrived_ref[:, :width]
        rows_ref[...] = rows
        rows_across[...] = rows.T
        gates = columns_scalar(arrived_ref[:, width:])
        grads = (gates * cot_ref[...].astype(F32)).astype(BF)
        grads_ref[...] = grads
        grads_across[...] = grads.T

    outs = [jax.ShapeDtypeStruct((total, width), BF)] * 2 + [jax.ShapeDtypeStruct((width, total), BF)] * 2
    return call(kernel, outs, [arrived, cots], "vv", [], "expert_rows", 0, 0, after)


def expert(rows, grads, across, weights, sums, cot):
    total, width = rows.shape
    m, _, _, wide = weights.shape
    last, started = cot is not None, sums is not None
    group = m if last and m * wide <= 512 else 1
    steps, span = m // group, group * wide

    def kernel(rows_ref, grads_ref, rows_across, grads_across, *refs):
        refs = list(refs)
        take = lambda k: [refs.pop(0) for _ in range(k)]
        carried = take(2) if started else None
        (cot_ref,) = take(1) if last else (None,)
        (weight_ref,) = take(1)
        if last:
            outs, (acts, pre_grads) = take(2), take(2)
            held, sems, out_sum, row_sum = refs
        else:
            (w_grads,), outs = take(1), take(2)
            held, sems, out_sum, row_sum, grad_held, out_sems = refs
        entering = []
        for i in range(m):
            place = held.at[i // group, :, :, pl.ds(i % group * wide, wide)]
            entering.append(pltpu.make_async_copy(weight_ref.at[i], place, sems.at[i]))
        for copy in entering:
            copy.start()
        r, g = rows_ref[...], grads_ref[...]
        leaving = []
        for i in range(steps):
            for copy in entering[i * group : (i + 1) * group]:
                copy.wait()
            up, down = held[i, 0], held[i, 1]
            value, slope = smooth_and_slope(mm(r, up))
            act = value.astype(BF)
            pre_grad = (mm(g, down) * slope).astype(BF)
            row_part, out_part = mm_t(pre_grad, up), mm_t(act, down)
            if i == 0 and started:
                row_part, out_part = row_part + carried[0][...], out_part + carried[1][...]
            if i > 0:
                row_part, out_part = row_part + row_sum[...], out_part + out_sum[...]
            row_sum[...] = row_part
            out_sum[...] = out_part
            if last:
                acts[i] = act
                pre_grads[i] = pre_grad
            else:
                grad_held[i, 0] = mm(rows_across[...], pre_grad).astype(BF)
                grad_held[i, 1] = mm(grads_across[...], act).astype(BF)
                copy = pltpu.make_async_copy(grad_held.at[i], w_grads.at[i], out_sems.at[i])
                copy.start()
                leaving.append(copy)
        if last:
            result = out_sum[...].astype(BF)
            gate_grad = jnp.sum(cot_ref[...].astype(F32) * result.astype(F32), axis=1, keepdims=True)
            outs[0][...] = jnp.concatenate([row_sum[...].astype(BF), scalar_columns(gate_grad)], axis=1)
            outs[1][...] = result
        else:
            outs[0][...] = row_sum[...]
            outs[1][...] = out_sum[...]
        for copy in leaving:
            copy.wait()

    shape = jax.ShapeDtypeStruct
    args = [rows, grads, *across] + (sums if started else []) + ([cot] if last else [])
    spaces = "v" * len(args) + "a"
    scratch = [
        pltpu.VMEM((steps, 2, width, span), BF), pltpu.SemaphoreType.DMA((m,)),
        pltpu.VMEM((total, width), F32), pltpu.VMEM((total, width), F32),
    ]
    if last:
        outs = [shape((total, width + EXTRA), BF), shape((total, width), BF)] + [shape((steps, total, span), BF)] * 2
        return call(kernel, outs, args + [weights], spaces, scratch, "expert_last", 0, 0)
    outs = [shape((m, 2, width, wide), BF)] + [shape((total, width), F32)] * 2
    scratch += [pltpu.VMEM((m, 2, width, wide), BF), pltpu.SemaphoreType.DMA((m,))]
    return call(kernel, outs, args + [weights], spaces, scratch, "expert", 0, 0, [], "avv")


def expert_grads(m, across, acts, pre_grads):
    steps, _, span = acts.shape
    width = across[0].shape[0]
    group = m // steps
    wide = span // group

    def kernel(rows_across, grads_across, acts_ref, pre_ref, out):
        for i in range(steps):
            ups = mm(rows_across[...], pre_ref[i]).astype(BF)
            downs = mm(grads_across[...], acts_ref[i]).astype(BF)
            for j in range(group):
                out[i * group + j, 0] = ups[:, j * wide : (j + 1) * wide]
                out[i * group + j, 1] = downs[:, j * wide : (j + 1) * wide]

    outs = [jax.ShapeDtypeStruct((m, 2, width, wide), BF)]
    return call(kernel, outs, [*across, acts, pre_grads], "vvvv", [], "expert_grads", 0, 0)[0]


def combine(returned, slots, hidden, gates):
    count, width = hidden.shape

    def kernel(slot_c, hidden_ref, gates_ref, got_ref, out):
        got = got_ref[...]
        place = lax.broadcasted_iota(I32, (count, got.shape[0]), 1)
        pick = jnp.where(place == slot_c[...], 1.0, 0.0).astype(BF)
        out[...] = (hidden_ref[...] + gates_ref[...] * mm(pick, got)).astype(BF)

    return call(
        kernel, [jax.ShapeDtypeStruct((count, width), BF)], [slots, hidden, gates, returned],
        "vvvv", [], "combine", 4 * count * count * width, 10 * count * width,
    )[0]


def gate_back(links, back, slots, routes, hidden, gates, small, cotangent, activated):
    count, width = hidden.shape
    n = links.n
    size = width // n
    units = activated.shape[1]

    def kernel(slot_c, route_c, hidden_ref, gates_ref, small_ref, cot, act, back_ref, *refs):
        got = back_ref[...]
        hidden_grad_ref, down_in_ref, small_out, centroid_out, *sums = refs[:-1]
        whole = refs[-1]
        place = lax.broadcasted_iota(I32, (count, got.shape[0]), 1)
        pick = jnp.where(place == slot_c[...], 1.0, 0.0).astype(BF)
        got = mm(pick, got)
        gates = gates_ref[...]
        logit_grad = columns_scalar(got[:, width:]) * gates * (1.0 - gates)
        lane = lax.broadcasted_iota(I32, (count, n), 1)
        onehot = jnp.where(lane == route_c[...], 1.0, 0.0).astype(BF)
        chosen = mm(onehot, small_ref[6 : 6 + n].astype(BF))
        normal, inverse = normalize(hidden_ref[...])
        gain = small_ref[2:3]
        moe_in = normal * gain + small_ref[5:6]
        terms = split3(logit_grad * moe_in)
        centroid_out[...] = t_mm(onehot, terms[0]) + t_mm(onehot, terms[1]) + t_mm(onehot, terms[2])
        moe_grad = got[:, :width] + logit_grad * chosen
        part, gain_grad, shift_grad = normalize_back(moe_grad, normal, inverse, gain)
        small_out[...] = jnp.concatenate([gain_grad, shift_grad], axis=0)
        hidden_grad = cot[...].astype(F32) + part
        hidden_grad_ref[...] = hidden_grad
        down_in = hidden_grad.astype(BF)
        down_in_ref[...] = down_in
        whole[...] = t_mm(down_in, act[...]).astype(BF)
        links.write_sum(sums, whole, 0, size)

    shape = jax.ShapeDtypeStruct
    outs = [
        shape((count, width), F32), shape((count, width), BF), shape((2, width), F32), shape((n, width), F32),
    ] + links.sum_shapes(size, units)
    args = [slots, routes, hidden, gates, small, cotangent, activated, back]
    hidden_grad, down_in, small_out, centroid_out, *sums = call(
        kernel, outs, args, "v" * len(args), [pltpu.VMEM((width, units), BF)], "gate_back",
        2 * count * width * units * 2, 8 * count * units,
    )
    return hidden_grad, down_in, small_out, centroid_out, sums


def widen_back(links, down_in, slope, second_in, weight_down):
    count, width = down_in.shape
    units = slope.shape[1]
    size = units // links.n
    pieces = len(weight_down.arrays)

    def kernel(down_in_ref, slope_ref, second, *refs):
        down_refs, refs = refs[:pieces], refs[pieces:]
        grad, *sums = refs[:-3]
        down, sems, whole = refs[-3:]
        for copy in weight_down.start(down_refs, down, sems):
            copy.wait()
        rows = down_in_ref[...]
        part = units // 4
        for i in range(4):
            at = pl.ds(i * part, part)
            piece = (mm(rows, down[:, at]) * slope_ref[:, at].astype(F32)).astype(BF)
            grad[:, at] = piece
            whole[at] = t_mm(piece, second[...]).astype(BF)
        links.write_sum(sums, whole, 0, size)

    outs = [jax.ShapeDtypeStruct((count, units), BF)] + links.sum_shapes(size, width)
    args = [down_in, slope, second_in]
    spaces = "vvv" + "a" * pieces
    scratch = weight_down.scratch() + [pltpu.VMEM((units, width), BF)]
    grad, *sums = call(
        kernel, outs, args + weight_down.arrays, spaces, scratch, "widen_back",
        4 * count * width * units, 8 * width * units,
    )
    return grad, sums


def second_back(links, widened_grad, after_attn, hidden_grad, mixed, small, weight_up, after):
    count, width = after_attn.shape
    n = links.n
    size = width // n
    pieces = len(weight_up.arrays)

    def kernel(grad, after_ref, hidden_grad_ref, mixed_ref, small_ref, *refs):
        up_refs, refs = refs[:pieces], refs[pieces:]
        after_grad_ref, attn_grad_ref, small_out, *sums = refs[:-3]
        up, sems, whole = refs[-3:]
        copies = weight_up.start(up_refs, up, sems)
        normal, inverse = normalize(after_ref[...])
        for copy in copies:
            copy.wait()
        second_grad = mm_t(grad[...], up[...])
        back, gain_grad, shift_grad = normalize_back(second_grad, normal, inverse, small_ref[1:2])
        small_out[...] = jnp.concatenate([gain_grad, shift_grad], axis=0)
        after_grad = hidden_grad_ref[...] + back
        after_grad_ref[...] = after_grad
        attn_grad = after_grad.astype(BF)
        attn_grad_ref[...] = attn_grad
        whole[...] = t_mm(attn_grad, mixed_ref[...]).astype(BF)
        links.write_sum(sums, whole, 0, size)

    shape = jax.ShapeDtypeStruct
    outs = [shape((count, width), F32), shape((count, width), BF), shape((2, width), F32)]
    outs += links.sum_shapes(size, width)
    args = [widened_grad, after_attn, hidden_grad, mixed, small]
    spaces = "vvvvv" + "a" * pieces
    scratch = weight_up.scratch() + [pltpu.VMEM((width, width), BF)]
    after_grad, attn_grad, small_out, *sums = call(
        kernel, outs, args + weight_up.arrays, spaces, scratch, "second_back",
        2 * count * width * 4 * width, 8 * width * 4 * width, after,
    )
    return after_grad, attn_grad, small_out, sums


def attend_back(attn_grad, projected, lse, segments, weight_out, after):
    count, width = attn_grad.shape
    pairs = width // (2 * HEAD_DIM)
    block = 128
    blocks = count // block
    n_out = len(weight_out.arrays)

    def kernel(attn_ref, proj, lse, seg_c, seg_r, *refs):
        out_refs, refs = refs[:n_out], refs[n_out:]
        grad, w_out, out_sems, bias, mixed_grad = refs
        copies = weight_out.start(out_refs, w_out, out_sems)
        bias[...] = bias_of(seg_c[...], seg_r[...])
        for copy in copies:
            copy.wait()
        mixed_grad[...] = mm(attn_ref[...], w_out[...]).astype(BF)
        masks = half_masks()
        lane = lax.broadcasted_iota(I32, (block, 128), 1)

        def pair(i, carry):
            at = [pl.ds(pl.multiple_of(part * width + 128 * i, 128), 128) for part in range(3)]
            k_grad = [jnp.zeros((block, 128), F32) for _ in range(blocks)]
            v_grad = [jnp.zeros((block, 128), F32) for _ in range(blocks)]
            for b in range(blocks):
                mine, keys = pl.ds(b * block, block), pl.ds(0, (b + 1) * block)
                q, k, v = proj[mine, at[0]] * 0.125, proj[keys, at[1]], proj[keys, at[2]]
                upper = mixed_grad[mine, at[0]]
                kept = lse[mine]
                q_grad = jnp.zeros((block, 128), F32)
                for h in range(2):
                    q_h, upper_h = q * masks[h], upper * masks[h]
                    log_total = jnp.sum(jnp.where(lane == 2 * i + h, kept, 0.0), axis=1, keepdims=True)
                    probs = jnp.exp(mm_t(q_h, k) + bias[mine, keys] - log_total)
                    probs_grad = mm_t(upper_h, v)
                    mean = jnp.sum(probs * probs_grad, axis=1, keepdims=True)
                    scores_grad = (probs * (probs_grad - mean)).astype(BF)
                    q_grad += mm(scores_grad, k * masks[h])
                    dv = t_mm(probs.astype(BF), upper_h)
                    dk = t_mm(scores_grad, q_h)
                    for c in range(b + 1):
                        v_grad[c] += dv[c * block : (c + 1) * block]
                        k_grad[c] += dk[c * block : (c + 1) * block]
                grad[mine, at[0]] = (q_grad * 0.125).astype(BF)
            for c in range(blocks):
                mine = pl.ds(c * block, block)
                grad[mine, at[1]] = k_grad[c].astype(BF)
                grad[mine, at[2]] = v_grad[c].astype(BF)
            return carry

        lax.fori_loop(0, pairs, pair, 0)

    args = [attn_grad, projected, lse, segments.reshape(count, 1), segments]
    spaces = "v" * len(args) + "a" * n_out
    scratch = weight_out.scratch() + [pltpu.VMEM((count, count), F32), pltpu.VMEM((count, width), BF)]
    return call(
        kernel, [jax.ShapeDtypeStruct((count, 3 * width), BF)], args + weight_out.arrays, spaces, scratch,
        "attend_back", 2 * count * width * (width + 5 * count) * 2, 12 * count * width * 4, after,
    )[0]


def project_back(links, projected_grad, first_in, after):
    width = first_in.shape[1]
    size = 3 * width // links.n

    def kernel(grad, first, *refs):
        whole = refs[-1]
        whole[...] = t_mm(grad[...], first[...]).astype(BF)
        links.write_sum(refs[:-1], whole, 0, size)

    return call(
        kernel, links.sum_shapes(size, width), [projected_grad, first_in], "vv",
        [pltpu.VMEM((3 * width, width), BF)], "project_back", 6 * width**3, 12 * width * width, after,
    )


def tokens_back(links, projected_grad, tokens, after_grad, small, smalls, centroid_grad, weight_in, after):
    count, width = tokens.shape
    n, n_in = links.n, len(weight_in.arrays)
    cols, rows = width // n, small.shape[0]

    def kernel(grad, tok, after_ref, small_ref, small_2, small_3, centroids, *refs):
        in_refs, refs = refs[:n_in], refs[n_in:]
        out, *sums = refs[:-2]
        w_in, sems = refs[-2:]
        copies = weight_in.start(in_refs, w_in, sems)
        normal, inverse = normalize(tok[...].astype(F32))
        for copy in copies:
            copy.wait()
        first_grad = mm(grad[...], w_in[...])
        back, gain_grad, shift_grad = normalize_back(first_grad, normal, inverse, small_ref[0:1])
        out[...] = after_ref[...] + back
        parts = [gain_grad, small_2[0:1], small_3[0:1], shift_grad, small_2[1:2], small_3[1:2]]
        parts += [centroids[...], jnp.zeros((rows - 6 - n, width), F32)]
        both = jnp.concatenate(parts, axis=0).astype(BF)
        me = lax.axis_index("expert") if links.cube else 0
        source = lax.broadcasted_iota(I32, (128, width), 0)
        place = lax.broadcasted_iota(I32, (128, width), 1)
        for k in range(n):
            mine = (place == source + (me ^ k) * cols) & (source < cols)
            block = mm_t(both, jnp.where(mine, 1.0, 0.0).astype(BF)).astype(BF)
            ref, i = (sums[k % 2], k // 2) if links.cube else (sums[0], k)
            ref[i] = jnp.zeros((rows, width), BF)
            ref[i, :, :128] = block

    outs = [jax.ShapeDtypeStruct((count, width), F32)] + links.sum_shapes(rows, width)
    args = [projected_grad, tokens, after_grad, small, *smalls, centroid_grad]
    out, *sums = call(
        kernel, outs, args + weight_in.arrays, "v" * len(args) + "a" * n_in, weight_in.scratch(),
        "tokens_back", 6 * count * width * width, 20 * count * width, after,
    )
    return out, sums


def on_device(
    n, m, tokens, segments, routes, norm_gains, norm_shifts, project_in, project_out,
    dense_up, dense_down, centroids, expert_up, expert_down, cotangent,
):
    count, width = tokens.shape
    BEFORE.clear()
    capacity = 2 * count // n
    total = n * capacity
    own_hidden = expert_up.shape[2]
    links = Links(n, m)
    cols = width // n

    def chunk(start, wide):
        part = slice(start, start + wide)
        return jnp.concatenate([expert_up[0][:, part], expert_down[0][:, part]], axis=0)

    chunks = [640, 128] if own_hidden == 768 and m == 4 else [own_hidden]
    gathered, start = [], 0
    for wide in chunks:
        whole = lax.all_gather(chunk(start, wide), "dp", axis=0, tiled=True)
        gathered.append(whole.reshape(m, 2, width, wide))
        start += wide

    pad = -(6 + n) % 16
    small = jnp.concatenate([norm_gains, norm_shifts, centroids], axis=0)
    small = jnp.pad(small, ((0, pad), (0, width - cols)))
    group = [project_in.T, project_out.T, small]
    started = links.start(jnp.concatenate(group, axis=0))
    weight_in, weight_out, weight_small = links.by_rows([a.shape[0] for a in group], started)
    started_up = links.start(dense_up, links.second)
    started_down = links.start(dense_down.T, links.second)

    row_slots, slots, cots = prepare(links, routes, cotangent, capacity)
    first_in, projected, mixed, lse, after_attn, second_in, small = attend(
        n, tokens, segments, weight_small, weight_in, weight_out, []
    )
    weight_up = links.by_columns(started_up, [small])
    (weight_down,) = links.by_rows([cols], started_down, [small])
    cots = links.exchange(cots, links.second)
    activated, slope = widen(second_in, weight_up, [])
    hidden, gates, sent = dispatch(
        links, activated, after_attn, small, row_slots, routes, weight_down, total, [cots]
    )
    rows, grads, *across = expert_rows(links.exchange(sent), cots, width, [])

    sums, expert_sums = None, []
    for c, whole in enumerate(gathered):
        if c < len(chunks) - 1:
            w_grads, *sums = expert(rows, grads, across, whole, sums, None)
            expert_sums.append(w_grads)
        else:
            back, results, acts, pre_grads = expert(rows, grads, across, whole, sums, cots)
    back = links.exchange(back)
    expert_sums.append(expert_grads(m, across, acts, pre_grads))

    def own_sum(grads):
        sums = lax.psum_scatter(grads.reshape(-1, grads.shape[-1]), "dp", scatter_dimension=0, tiled=True)
        return sums.reshape(grads.shape[1:])

    summed = [own_sum(expert_sums[0])]
    returned = links.exchange(results, [back])

    hidden_grad, down_in, small_3, centroid_grad, sums_down = gate_back(
        links, back, slots, routes, hidden, gates, small, cotangent, activated
    )
    twin_down = links.twins(sums_down)
    widened_grad, sums_up = widen_back(links, down_in, slope, second_in, weight_down)
    twin_up = links.twins(sums_up)
    down = links.fold([sums_down], twin_down)
    down_got = links.across(down)
    after_grad, attn_grad, small_2, sums_out = second_back(
        links, widened_grad, after_attn, hidden_grad, mixed, small, weight_up, [returned]
    )
    twin_out = links.twins(sums_out)
    projected_grad = attend_back(attn_grad, projected, lse, segments, weight_out, [])
    up = links.fold([sums_up, sums_out], twin_up + twin_out)
    up_got = links.across(up)
    down = links.fold_again(down, down_got)
    down_got = links.across_again(down)
    tokens_grad, sums_small = tokens_back(
        links, projected_grad, tokens, after_grad, small, [small_2, small_3], centroid_grad, weight_in, []
    )
    twin_small = links.twins(sums_small)
    for grads in expert_sums[1:]:
        summed.append(own_sum(links.gated(grads, summed + [sums_small[0]])))
    sums_in = project_back(links, projected_grad, first_in, [])
    twin_in = links.twins(sums_in)
    down = links.fold_last(down, down_got)
    down_got = links.inward(down)
    up = links.fold_again(up, up_got, "fold_wait")
    up_got = links.across_again(up)
    inner = links.fold([sums_in, sums_small], twin_in + twin_small)
    inner_got = links.across(inner)
    inner = links.fold_again(inner, inner_got)
    inner_got = links.across_again(inner)
    up = links.fold_last(up, up_got)
    up_got = links.inward(up)
    inner = links.fold_last(inner, inner_got)
    inner_got = links.inward(inner)
    output = combine(returned, slots, hidden, gates)
    down = links.joined(down, down_got)
    down_got = links.middle(down)
    up = links.joined(up, up_got)
    up_got = links.middle(up)
    inner = links.joined(inner, inner_got)
    inner_got = links.middle(inner)
    down = links.joined(down, down_got)
    down_got = links.outward(down)
    up = links.joined(up, up_got)
    up_got = links.outward(up)
    inner = links.joined(inner, inner_got)
    inner_got = links.outward(inner)
    expert_sums = finish(summed)
    down_sum = links.settled(down, down_got)
    units, columns = dense_up.shape[1], project_in.shape[1]
    up_sum, out_sum = links.settled_across(up, up_got, units)
    in_sum, gains_sum, shifts_sum, centroids_sum = links.settled_small(inner, inner_got, columns, cols)

    return (
        output, tokens_grad, gains_sum, shifts_sum, in_sum.T, out_sum.T, up_sum,
        down_sum.T, centroids_sum, expert_sums[0][None], expert_sums[1][None],
    )


def solution(mesh):
    sizes = dict(mesh.shape)
    both, over = P(("dp", "expert"), None), P(None, "expert")
    expert_place = P("expert", None, "dp")
    return jax.shard_map(
        functools.partial(on_device, sizes["expert"], sizes["dp"]),
        mesh=mesh,
        in_specs=(both,) * 3 + (over,) * 7 + (expert_place,) * 2 + (both,),
        out_specs=(both,) * 2 + (over,) * 7 + (expert_place,) * 2,
        check_vma=False,
    )
```

```python
import functools

import jax
import jax.numpy as jnp
from jax import lax
from jax.experimental import pallas as pl
from jax.experimental.pallas import tpu as pltpu
from jax.sharding import PartitionSpec as P

HEAD_DIM = 64
EXTRA = 128
BF = jnp.bfloat16
F32 = jnp.float32
I32 = jnp.int32
ROOT = 0.7978845608028654
COST = dict(
    prepare=3, attend=16, widen=9, dispatch=10, expert_rows=4, expert=20, expert_last=10, expert_grads=6, gate_back=10, widen_back=12, fold=1, fold_wide=1,
    second_back=17, attend_back=2, fold_again=1, fold_wait=12, project_back=2, tokens_back=2, fold_last=1, joined=4,
    combine=1, finish=1, settle=1,
)
WIDE = ("attend", "widen", "dispatch", "expert", "expert_last", "expert_grads", "gate_back", "fold_wide", "widen_back", "settle")
VMEM_LIMIT = 60 * 1024 * 1024


def mm(left, right):
    return lax.dot_general(left, right, (((1,), (0,)), ((), ())), preferred_element_type=F32)


def mm_t(left, right):
    return lax.dot_general(left, right, (((1,), (1,)), ((), ())), preferred_element_type=F32)


def t_mm(left, right):
    return lax.dot_general(left, right, (((0,), (0,)), ((), ())), preferred_element_type=F32)


def normalize(rows):
    share = 1.0 / rows.shape[-1]
    centred = rows - jnp.sum(rows, axis=-1, keepdims=True) * share
    spread = jnp.sum(centred * centred, axis=-1, keepdims=True) * share
    inverse = lax.rsqrt(spread + 1e-05)
    return centred * inverse, inverse


def normalize_back(grad, normal, inverse, gain):
    share = 1.0 / grad.shape[-1]
    scaled = grad * gain
    first = jnp.sum(scaled, axis=-1, keepdims=True) * share
    second = jnp.sum(scaled * normal, axis=-1, keepdims=True) * share
    rows = inverse * (scaled - first - normal * second)
    return rows, jnp.sum(grad * normal, axis=0, keepdims=True), jnp.sum(grad, axis=0, keepdims=True)


def smooth_and_slope(v):
    square = v * v
    bend = jnp.tanh(v * (ROOT + ROOT * 0.044715 * square))
    half = 0.5 + 0.5 * bend
    slope = half + 0.5 * v * (1.0 - bend * bend) * (ROOT + 3.0 * ROOT * 0.044715 * square)
    return v * half, slope


def split3(v):
    hi = v.astype(BF)
    rest = v - hi.astype(F32)
    mid = rest.astype(BF)
    return hi, mid, (rest - mid.astype(F32)).astype(BF)


def scalar_columns(v):
    hi, mid, low = split3(v)
    lane = lax.broadcasted_iota(I32, (v.shape[0], EXTRA), 1)
    out = jnp.where(lane == 0, hi.astype(F32), 0.0)
    out = jnp.where(lane == 1, mid.astype(F32), out)
    return jnp.where(lane == 2, low.astype(F32), out).astype(BF)


def columns_scalar(columns):
    return jnp.sum(columns.astype(F32), axis=-1, keepdims=True)


def bias_of(by_row, by_column):
    count = by_row.shape[0]
    row = lax.broadcasted_iota(I32, (count, count), 0)
    column = lax.broadcasted_iota(I32, (count, count), 1)
    allowed = (by_row == by_column) & (row >= column)
    return jnp.where(allowed, 0.0, -1000000000.0)


def half_masks():
    lane = lax.broadcasted_iota(I32, (1, 2 * HEAD_DIM), 1)
    first = jnp.where(lane < HEAD_DIM, 1.0, 0.0)
    return first.astype(BF), (1.0 - first).astype(BF)


BEFORE = []


def smallest(outs):
    return min(outs, key=lambda a: a.size * a.dtype.itemsize)


def call(kernel, outs, args, spaces, scratch, name, flops, moved, after=(), results=None):
    where = {"v": pltpu.VMEM, "a": pl.ANY}
    after = list(after) + BEFORE
    read, waited = len(args), len(after)
    args, spaces = list(args) + list(after), spaces + "a" * waited

    def body(*refs):
        kernel(*refs[:read], *refs[read + waited :])

    got = pl.pallas_call(
        body,
        out_shape=outs,
        in_specs=[pl.BlockSpec(memory_space=where[s]) for s in spaces],
        out_specs=[pl.BlockSpec(memory_space=where[s]) for s in results or "v" * len(outs)],
        scratch_shapes=scratch,
        compiler_params=pltpu.CompilerParams(vmem_limit_bytes=VMEM_LIMIT if name in WIDE else VMEM_LIMIT // 2),
        cost_estimate=pl.CostEstimate(flops=COST[name] * 1150000000, bytes_accessed=1000, transcendentals=0),
        name=name,
    )(*args)
    BEFORE[:] = [smallest(got)]
    return got


class Weight:
    def __init__(self, arrays, copies, shape):
        self.arrays, self.copies, self.shape = arrays, copies, shape

    def scratch(self):
        return [pltpu.VMEM(self.shape, BF), pltpu.SemaphoreType.DMA((len(self.copies),))]

    def start(self, refs, whole, sems):
        me = lax.axis_index("expert")
        running = []
        for i, (index, source, place) in enumerate(self.copies):
            copy = pltpu.make_async_copy(
                refs[index].at[source], whole.at[place(me)], sems.at[i]
            )
            copy.start()
            running.append(copy)
        return running


def row_place(k, size, offset, rows, step):
    def place(me):
        if k is None:
            return (pl.ds(offset, rows),)
        return (pl.ds(pl.multiple_of((me ^ k) * size + offset, step), rows),)

    return place


def column_place(k, size, offset, rows):
    def place(me):
        if k is None:
            return (pl.ds(0, rows),)
        start = pl.multiple_of((me ^ k) * size, 128)
        return (pl.ds(offset, rows), pl.ds(start, size))

    return place


class Links:
    def __init__(self, n, m):
        self.n, self.m = n, m
        self.cube = n == 8
        self.line = m == 4
        self.second = ()

    def hop(self, value, bit):
        return lax.ppermute(value, "expert", [(i, i ^ bit) for i in range(self.n)])

    def gated(self, value, gate):
        return lax.optimization_barrier((value, *gate))[0] if gate else value

    def start(self, shard, gate=()):
        if not self.cube:
            return [shard]
        shard = self.gated(shard, gate)
        return [shard, self.hop(shard, 2), self.hop(shard, 4)]

    def pieces(self, started, gate=()):
        shard, by_x, by_y = lax.optimization_barrier((*started, *gate))[:3] if gate else started
        half = shard.shape[0] // 2 // 16 * 16
        far_a = self.hop(by_y[:half], 2)
        far_b = self.hop(by_x[half:], 4)
        self.second = (far_a, far_b)
        return [
            (0, 0, shard), (1, 0, self.hop(shard, 1)), (2, 0, by_x), (3, 0, self.hop(by_x, 1)),
            (4, 0, by_y), (5, 0, self.hop(by_y, 1)), (6, 0, far_a), (6, half, far_b),
            (7, 0, self.hop(far_a, 1)), (7, half, self.hop(far_b, 1)),
        ]

    def by_rows(self, sizes, started, gate=()):
        group = started[0]
        weights, first = [], 0
        if not self.cube:
            whole = lax.all_gather(group, "expert", axis=0, tiled=False)
            for size in sizes:
                part = whole[:, first : first + size].reshape(-1, group.shape[1])
                copies = [(0, (pl.ds(0, part.shape[0]),), row_place(None, 0, 0, part.shape[0], 8))]
                weights.append(Weight([part], copies, part.shape))
                first += size
            return weights
        pieces = self.pieces(started, gate)
        for size in sizes:
            arrays, copies = [], []
            for k, row, array in pieces:
                low, high = max(first, row), min(first + size, row + array.shape[0])
                if low < high:
                    source = (pl.ds(low - row, high - low),)
                    place = row_place(k, size, low - first, high - low, 16 if size % 16 == 0 else 8)
                    copies.append((len(arrays), source, place))
                    arrays.append(array)
            weights.append(Weight(arrays, copies, (self.n * size, group.shape[1])))
            first += size
        return weights

    def by_columns(self, started, gate=()):
        shard = started[0]
        rows, size = shard.shape
        if not self.cube:
            whole = lax.all_gather(shard, "expert", axis=1, tiled=True)
            return Weight([whole], [(0, (pl.ds(0, rows),), column_place(None, 0, 0, rows))], whole.shape)
        arrays, copies = [], []
        for k, row, array in self.pieces(started, gate):
            source = (pl.ds(0, array.shape[0]),)
            copies.append((len(arrays), source, column_place(k, size, row, array.shape[0])))
            arrays.append(array)
        return Weight(arrays, copies, (rows, self.n * size))

    def exchange(self, rows, gate=()):
        blocks = self.gated(rows, gate).reshape(self.n, -1, rows.shape[1])
        got = lax.all_to_all(blocks, "expert", split_axis=0, concat_axis=0, tiled=True)
        return got.reshape(rows.shape)

    def sum_shapes(self, rows, width):
        if not self.cube:
            return [jax.ShapeDtypeStruct((self.n, rows, width), BF)]
        return [jax.ShapeDtypeStruct((self.n // 2, rows, width), BF)] * 2

    def write_sum(self, refs, whole, first, size):
        for k in range(self.n):
            if self.cube:
                me = lax.axis_index("expert")
                step = 16 if size % 16 == 0 else 8
                start = pl.multiple_of((me ^ k) * size, step)
                refs[k % 2][k // 2, first : first + size] = whole[pl.ds(start, size)]
            else:
                refs[0][k, first : first + size] = whole[k * size : (k + 1) * size]

    def twins(self, blocks):
        return [self.hop(blocks[1], 1)] if self.cube else []

    def fold(self, groups, twins, name="fold"):
        if not self.cube:
            return [jnp.concatenate([g[0] for g in groups], axis=1)]
        rows = [g[0].shape[1] for g in groups]
        total, columns = sum(rows), groups[0][0].shape[2]
        half = total // 2 // 16 * 16

        def kernel(*refs):
            count = len(groups)
            outs = refs[2 * count :]
            first = 0
            for even, odd in zip(refs[:count], refs[count : 2 * count]):
                for m in range(4):
                    value = (even[m].astype(F32) + odd[m].astype(F32)).astype(BF)
                    low, high = first, first + even.shape[1]
                    cut = min(max(half, low), high)
                    if low < cut:
                        outs[m % 2][m // 2, low:cut] = value[: cut - low]
                    if cut < high:
                        outs[2 + m // 2][m % 2, cut - half : high - half] = value[cut - low :]
                first += even.shape[1]

        outs = [jax.ShapeDtypeStruct((2, half, columns), BF)] * 2
        outs += [jax.ShapeDtypeStruct((2, total - half, columns), BF)] * 2
        args = [g[0] for g in groups] + list(twins)
        return list(call(kernel, outs, args, "v" * len(args), [], name, 0, 0))

    def across(self, kept):
        return [self.hop(kept[1], 2), self.hop(kept[3], 4)] if self.cube else []

    def fold_again(self, kept, got, name="fold_again"):
        if not self.cube:
            return kept

        def kernel(first, got_first, second, got_second, *outs):
            for i, (mine, other) in enumerate(((first, got_first), (second, got_second))):
                for j in range(2):
                    outs[2 * i + j][...] = (mine[j].astype(F32) + other[j].astype(F32)).astype(BF)

        outs = [jax.ShapeDtypeStruct(a.shape[1:], BF) for a in (kept[0], kept[0], kept[2], kept[2])]
        args = [kept[0], got[0], kept[2], got[1]]
        return list(call(kernel, outs, args, "vvvv", [], name, 0, 0))

    def across_again(self, kept):
        return [self.hop(kept[1], 4), self.hop(kept[3], 2)] if self.cube else []

    def fold_last(self, kept, got):
        if not self.cube:
            return lax.psum_scatter(kept[0], "expert", scatter_dimension=0, tiled=True)[0]
        half = kept[0].shape[0]

        def kernel(first, got_first, second, got_second, out):
            out[:half] = (first[...].astype(F32) + got_first[...].astype(F32)).astype(BF)
            out[half:] = (second[...].astype(F32) + got_second[...].astype(F32)).astype(BF)

        rows = half + kept[2].shape[0]
        outs = [jax.ShapeDtypeStruct((rows, kept[0].shape[1]), BF)]
        return call(kernel, outs, [kept[0], got[0], kept[2], got[1]], "vvvv", [], "fold_last", 0, 0)[0]

    def along(self, value, pairs):
        return lax.ppermute(value, "dp", pairs)

    def inward(self, value):
        return [self.along(value, [(0, 1), (3, 2)])] if self.line else []

    def middle(self, value):
        return [self.along(value, [(1, 2), (2, 1)])] if self.line else []

    def outward(self, value):
        return [self.along(value, [(1, 0), (2, 3)])] if self.line else []

    def joined(self, value, got):
        if not self.line:
            return value

        def kernel(mine, other, out):
            out[...] = (mine[...].astype(F32) + other[...].astype(F32)).astype(BF)

        outs = [jax.ShapeDtypeStruct(value.shape, BF)]
        return call(kernel, outs, [value, got[0]], "vv", [], "joined", 0, 0)[0]

    def settled(self, value, got):
        if not self.line:
            return lax.psum(value, "dp").astype(F32)

        def kernel(mine, other, out):
            place = lax.axis_index("dp")

            def write(ref):
                out[...] = ref[...].astype(F32)

            middle = (place == 1) | (place == 2)
            pl.when(middle)(lambda: write(mine))
            pl.when(jnp.logical_not(middle))(lambda: write(other))

        outs = [jax.ShapeDtypeStruct(value.shape, F32)]
        return call(kernel, outs, [value, got[0]], "vv", [], "settle", 0, 0)[0]

    def settled_small(self, value, got, columns, cols):
        n = self.n
        rows = [(columns, 3), (columns + 3, 3), (columns + 6, n)]
        if not self.line:
            value = lax.psum(value, "dp").astype(F32)
            return [value[:columns]] + [value[i : i + size, :cols] for i, size in rows]

        def kernel(mine, other, out, *smalls):
            place = lax.axis_index("dp")

            def write(ref):
                out[...] = ref[:columns].astype(F32)
                rest = ref[columns:, :128].astype(F32)
                for (i, size), small in zip(rows, smalls):
                    small[...] = rest[i - columns : i - columns + size, :cols]

            middle = (place == 1) | (place == 2)
            pl.when(middle)(lambda: write(mine))
            pl.when(jnp.logical_not(middle))(lambda: write(other))

        outs = [jax.ShapeDtypeStruct((columns, value.shape[1]), F32)]
        outs += [jax.ShapeDtypeStruct((size, cols), F32) for _, size in rows]
        return call(kernel, outs, [value, got[0]], "vv", [], "settle", 0, 0)

    def settled_across(self, value, got, units):
        if not self.line:
            value = lax.psum(value, "dp").astype(F32)
            return value[:units].T, value[units:]

        def kernel(mine, other, up, out):
            place = lax.axis_index("dp")

            def write(ref):
                up[...] = ref[:units].astype(F32).T
                out[...] = ref[units:].astype(F32)

            middle = (place == 1) | (place == 2)
            pl.when(middle)(lambda: write(mine))
            pl.when(jnp.logical_not(middle))(lambda: write(other))

        rows, width = value.shape
        outs = [jax.ShapeDtypeStruct((width, units), F32), jax.ShapeDtypeStruct((rows - units, width), F32)]
        return call(kernel, outs, [value, got[0]], "vv", [], "settle", 0, 0)


def finish(parts):
    width = parts[0].shape[1]

    def kernel(*refs):
        ups, downs = refs[-2:]
        first = 0
        for ref in refs[:-2]:
            for i, out in enumerate((ups, downs)):
                out[:, first : first + ref.shape[2]] = ref[i].astype(F32)
            first += ref.shape[2]

    outs = [jax.ShapeDtypeStruct((width, sum(p.shape[2] for p in parts)), F32)] * 2
    return call(kernel, outs, parts, "v" * len(parts), [], "finish", 0, 0)


def prepare(links, routes, cotangent, capacity):
    count, width = cotangent.shape
    n = links.n
    total = n * capacity

    def kernel(by_row, by_column, cot, row_out, column_out, out):
        route_c, route_r = by_row[...], by_column[...]
        token = lax.broadcasted_iota(I32, (count, count), 0)
        other = lax.broadcasted_iota(I32, (count, count), 1)
        same = route_c == route_r
        rank_c = jnp.sum(jnp.where(same & (other < token), 1.0, 0.0), axis=1, keepdims=True)
        rank_r = jnp.sum(jnp.where(same & (token < other), 1.0, 0.0), axis=0, keepdims=True)
        slot_c = route_c * capacity + rank_c.astype(I32)
        slot_r = route_r * capacity + rank_r.astype(I32)
        column_out[...] = slot_c
        row_out[...] = slot_r
        place = lax.broadcasted_iota(I32, (total, count), 0)
        to_slots = jnp.where(place == slot_r, 1.0, 0.0).astype(BF)
        out[...] = mm(to_slots, cot[...]).astype(BF)

    outs = [jax.ShapeDtypeStruct((1, count), I32), jax.ShapeDtypeStruct((count, 1), I32)]
    outs.append(jax.ShapeDtypeStruct((total, width), BF))
    args = [routes, routes.reshape(1, count), cotangent]
    return call(
        kernel, outs, args, "vvv", [], "prepare", 2 * total * count * width, 4 * total * width
    )


def attend(n, tokens, segments, weight_small, weight_in, weight_out, after):
    count, width = tokens.shape
    pairs = width // (2 * HEAD_DIM)
    block = 128
    n_small, n_in, n_out = len(weight_small.arrays), len(weight_in.arrays), len(weight_out.arrays)
    small_rows, cols = weight_small.shape[0] // n, width // n

    def kernel(tok, seg_c, seg_r, *refs):
        small_refs, refs = refs[:n_small], refs[n_small:]
        in_refs, refs = refs[:n_in], refs[n_in:]
        out_refs, refs = refs[:n_out], refs[n_out:]
        first_ref, proj, mixed, lse, after_ref, second_ref, small_ref = refs[:7]
        w_small, small_sems, w_in, in_sems, w_out, out_sems, bias = refs[7:]
        small_copies = weight_small.start(small_refs, w_small, small_sems)
        in_copies = weight_in.start(in_refs, w_in, in_sems)
        out_copies = weight_out.start(out_refs, w_out, out_sems)
        rows = tok[...].astype(F32)
        normal, _ = normalize(rows)
        source = lax.broadcasted_iota(I32, (cols, width), 0)
        place = lax.broadcasted_iota(I32, (cols, width), 1)
        for copy in small_copies:
            copy.wait()
        small = jnp.zeros((small_rows, width), F32)
        for j in range(n):
            spread = jnp.where(place == source + j * cols, 1.0, 0.0).astype(BF)
            small += mm(w_small[j * small_rows : (j + 1) * small_rows, :cols], spread)
        small_ref[...] = small
        first = (normal * small_ref[0:1] + small_ref[3:4]).astype(BF)
        first_ref[...] = first
        bias[...] = bias_of(seg_c[...], seg_r[...])
        lse[...] = jnp.zeros_like(lse)
        for copy in in_copies:
            copy.wait()
        proj[...] = mm_t(first, w_in[...]).astype(BF)
        masks = half_masks()
        lane = lax.broadcasted_iota(I32, (block, 128), 1)

        def pair(i, carry):
            at = [pl.ds(pl.multiple_of(part * width + 128 * i, 128), 128) for part in range(3)]
            for b in range(count // block):
                mine, keys = pl.ds(b * block, block), pl.ds(0, (b + 1) * block)
                q, k, v = proj[mine, at[0]] * 0.125, proj[keys, at[1]], proj[keys, at[2]]
                got = jnp.zeros((block, 128), F32)
                kept = lse[mine]
                for h in range(2):
                    scores = mm_t(q * masks[h], k) + bias[mine, keys]
                    top = jnp.max(scores, axis=1, keepdims=True)
                    lifted = jnp.exp(scores - top)
                    totals = jnp.sum(lifted, axis=1, keepdims=True)
                    probs = (lifted * (1.0 / totals)).astype(BF)
                    got += mm(probs, v * masks[h])
                    kept = jnp.where(lane == 2 * i + h, top + jnp.log(totals), kept)
                lse[mine] = kept
                mixed[mine, at[0]] = got.astype(BF)
            return carry

        lax.fori_loop(0, pairs, pair, 0)
        for copy in out_copies:
            copy.wait()
        after = rows + mm_t(mixed[...], w_out[...])
        after_ref[...] = after
        normal, _ = normalize(after)
        second_ref[...] = (normal * small_ref[1:2] + small_ref[4:5]).astype(BF)

    shape = jax.ShapeDtypeStruct
    outs = [
        shape((count, width), BF), shape((count, 3 * width), BF), shape((count, width), BF),
        shape((count, 128), F32), shape((count, width), F32), shape((count, width), BF),
        shape((small_rows, width), F32),
    ]
    args = [tokens, segments.reshape(count, 1), segments]
    args += weight_small.arrays + weight_in.arrays + weight_out.arrays
    spaces = "vvv" + "a" * (n_small + n_in + n_out)
    scratch = weight_small.scratch() + weight_in.scratch() + weight_out.scratch() + [pltpu.VMEM((count, count), F32)]
    flops = 2 * count * width * (4 * width + 2 * count) * 2
    return call(kernel, outs, args, spaces, scratch, "attend", flops, 12 * count * width * 4, after)


def widen(second_in, weight_up, after):
    count = second_in.shape[0]
    hidden = weight_up.shape[1]
    pieces = len(weight_up.arrays)
    part = hidden // 4

    def kernel(second, *refs):
        up_refs, (act_ref, slope_ref, up, sems) = refs[:pieces], refs[pieces:]
        for copy in weight_up.start(up_refs, up, sems):
            copy.wait()
        rows = second[...]
        for i in range(4):
            at = pl.ds(i * part, part)
            value, slope = smooth_and_slope(mm(rows, up[:, at]))
            act_ref[:, at] = value.astype(BF)
            slope_ref[:, at] = slope.astype(BF)

    outs = [jax.ShapeDtypeStruct((count, hidden), BF)] * 2
    args = [second_in] + weight_up.arrays
    return call(
        kernel, outs, args, "v" + "a" * pieces, weight_up.scratch(), "widen",
        4 * count * hidden * second_in.shape[1], 8 * count * hidden, after,
    )


def dispatch(links, activated, after_attn, small, row_slots, routes, weight_down, total, after):
    count, width = after_attn.shape
    n = links.n
    pieces = len(weight_down.arrays)

    def kernel(act, after, small_ref, slot_r, route_c, *refs):
        down_refs, refs = refs[:pieces], refs[pieces:]
        hidden_ref, gates_ref, sent_ref = refs[:-2]
        down, sems = refs[-2:]
        for copy in weight_down.start(down_refs, down, sems):
            copy.wait()
        hidden = after[...] + mm_t(act[...], down[...])
        hidden_ref[...] = hidden
        normal, _ = normalize(hidden)
        moe_in = normal * small_ref[2:3] + small_ref[5:6]
        lane = lax.broadcasted_iota(I32, (count, n), 1)
        onehot = jnp.where(lane == route_c[...], 1.0, 0.0).astype(BF)
        chosen = mm(onehot, small_ref[6 : 6 + n].astype(BF))
        logit = jnp.sum(moe_in * chosen, axis=1, keepdims=True)
        gates = 1.0 / (1.0 + jnp.exp(-logit))
        gates_ref[...] = gates
        sent = jnp.concatenate([moe_in.astype(BF), scalar_columns(gates)], axis=1)
        place = lax.broadcasted_iota(I32, (total, count), 0)
        to_slots = jnp.where(place == slot_r[...], 1.0, 0.0).astype(BF)
        sent_ref[...] = mm(to_slots, sent).astype(BF)

    shape = jax.ShapeDtypeStruct
    outs = [shape((count, width), F32), shape((count, 1), F32)]
    outs.append(shape((total, width + EXTRA), BF))
    args = [activated, after_attn, small, row_slots, routes] + weight_down.arrays
    return call(
        kernel, outs, args, "vvvvv" + "a" * pieces, weight_down.scratch(), "dispatch",
        4 * count * width * 4 * width, 16 * count * width, after,
    )


def expert_rows(arrived, cots, width, after):
    total = arrived.shape[0]

    def kernel(arrived_ref, cot_ref, rows_ref, grads_ref, rows_across, grads_across):
        rows = arrived_ref[:, :width]
        rows_ref[...] = rows
        rows_across[...] = rows.T
        gates = columns_scalar(arrived_ref[:, width:])
        grads = (gates * cot_ref[...].astype(F32)).astype(BF)
        grads_ref[...] = grads
        grads_across[...] = grads.T

    outs = [jax.ShapeDtypeStruct((total, width), BF)] * 2 + [jax.ShapeDtypeStruct((width, total), BF)] * 2
    return call(kernel, outs, [arrived, cots], "vv", [], "expert_rows", 0, 0, after)


def expert(rows, grads, across, weights, sums, cot):
    total, width = rows.shape
    m, _, _, wide = weights.shape
    last, started = cot is not None, sums is not None
    group = m if last and m * wide <= 512 else 1
    steps, span = m // group, group * wide

    def kernel(rows_ref, grads_ref, rows_across, grads_across, *refs):
        refs = list(refs)
        take = lambda k: [refs.pop(0) for _ in range(k)]
        carried = take(2) if started else None
        (cot_ref,) = take(1) if last else (None,)
        (weight_ref,) = take(1)
        if last:
            outs, (acts, pre_grads) = take(2), take(2)
            held, sems, out_sum, row_sum = refs
        else:
            (w_grads,), outs = take(1), take(2)
            held, sems, out_sum, row_sum, grad_held, out_sems = refs
        entering = []
        for i in range(m):
            place = held.at[i // group, :, :, pl.ds(i % group * wide, wide)]
            entering.append(pltpu.make_async_copy(weight_ref.at[i], place, sems.at[i]))
        for copy in entering:
            copy.start()
        r, g = rows_ref[...], grads_ref[...]
        leaving = []
        for i in range(steps):
            for copy in entering[i * group : (i + 1) * group]:
                copy.wait()
            up, down = held[i, 0], held[i, 1]
            value, slope = smooth_and_slope(mm(r, up))
            act = value.astype(BF)
            pre_grad = (mm(g, down) * slope).astype(BF)
            row_part, out_part = mm_t(pre_grad, up), mm_t(act, down)
            if i == 0 and started:
                row_part, out_part = row_part + carried[0][...], out_part + carried[1][...]
            if i > 0:
                row_part, out_part = row_part + row_sum[...], out_part + out_sum[...]
            row_sum[...] = row_part
            out_sum[...] = out_part
            if last:
                acts[i] = act
                pre_grads[i] = pre_grad
            else:
                grad_held[i, 0] = mm(rows_across[...], pre_grad).astype(BF)
                grad_held[i, 1] = mm(grads_across[...], act).astype(BF)
                copy = pltpu.make_async_copy(grad_held.at[i], w_grads.at[i], out_sems.at[i])
                copy.start()
                leaving.append(copy)
        if last:
            result = out_sum[...].astype(BF)
            gate_grad = jnp.sum(cot_ref[...].astype(F32) * result.astype(F32), axis=1, keepdims=True)
            outs[0][...] = jnp.concatenate([row_sum[...].astype(BF), scalar_columns(gate_grad)], axis=1)
            outs[1][...] = result
        else:
            outs[0][...] = row_sum[...]
            outs[1][...] = out_sum[...]
        for copy in leaving:
            copy.wait()

    shape = jax.ShapeDtypeStruct
    args = [rows, grads, *across] + (sums if started else []) + ([cot] if last else [])
    spaces = "v" * len(args) + "a"
    scratch = [
        pltpu.VMEM((steps, 2, width, span), BF), pltpu.SemaphoreType.DMA((m,)),
        pltpu.VMEM((total, width), F32), pltpu.VMEM((total, width), F32),
    ]
    if last:
        outs = [shape((total, width + EXTRA), BF), shape((total, width), BF)] + [shape((steps, total, span), BF)] * 2
        return call(kernel, outs, args + [weights], spaces, scratch, "expert_last", 0, 0)
    outs = [shape((m, 2, width, wide), BF)] + [shape((total, width), F32)] * 2
    scratch += [pltpu.VMEM((m, 2, width, wide), BF), pltpu.SemaphoreType.DMA((m,))]
    return call(kernel, outs, args + [weights], spaces, scratch, "expert", 0, 0, [], "avv")


def expert_grads(m, across, acts, pre_grads):
    steps, _, span = acts.shape
    width = across[0].shape[0]
    group = m // steps
    wide = span // group

    def kernel(rows_across, grads_across, acts_ref, pre_ref, out):
        for i in range(steps):
            ups = mm(rows_across[...], pre_ref[i]).astype(BF)
            downs = mm(grads_across[...], acts_ref[i]).astype(BF)
            for j in range(group):
                out[i * group + j, 0] = ups[:, j * wide : (j + 1) * wide]
                out[i * group + j, 1] = downs[:, j * wide : (j + 1) * wide]

    outs = [jax.ShapeDtypeStruct((m, 2, width, wide), BF)]
    return call(kernel, outs, [*across, acts, pre_grads], "vvvv", [], "expert_grads", 0, 0)[0]


def combine(returned, slots, hidden, gates):
    count, width = hidden.shape

    def kernel(slot_c, hidden_ref, gates_ref, got_ref, out):
        got = got_ref[...]
        place = lax.broadcasted_iota(I32, (count, got.shape[0]), 1)
        pick = jnp.where(place == slot_c[...], 1.0, 0.0).astype(BF)
        out[...] = (hidden_ref[...] + gates_ref[...] * mm(pick, got)).astype(BF)

    return call(
        kernel, [jax.ShapeDtypeStruct((count, width), BF)], [slots, hidden, gates, returned],
        "vvvv", [], "combine", 4 * count * count * width, 10 * count * width,
    )[0]


def gate_back(links, back, slots, routes, hidden, gates, small, cotangent, activated):
    count, width = hidden.shape
    n = links.n
    size = width // n
    units = activated.shape[1]

    def kernel(slot_c, route_c, hidden_ref, gates_ref, small_ref, cot, act, back_ref, *refs):
        got = back_ref[...]
        hidden_grad_ref, down_in_ref, small_out, centroid_out, *sums = refs[:-1]
        whole = refs[-1]
        place = lax.broadcasted_iota(I32, (count, got.shape[0]), 1)
        pick = jnp.where(place == slot_c[...], 1.0, 0.0).astype(BF)
        got = mm(pick, got)
        gates = gates_ref[...]
        logit_grad = columns_scalar(got[:, width:]) * gates * (1.0 - gates)
        lane = lax.broadcasted_iota(I32, (count, n), 1)
        onehot = jnp.where(lane == route_c[...], 1.0, 0.0).astype(BF)
        chosen = mm(onehot, small_ref[6 : 6 + n].astype(BF))
        normal, inverse = normalize(hidden_ref[...])
        gain = small_ref[2:3]
        moe_in = normal * gain + small_ref[5:6]
        terms = split3(logit_grad * moe_in)
        centroid_out[...] = t_mm(onehot, terms[0]) + t_mm(onehot, terms[1]) + t_mm(onehot, terms[2])
        moe_grad = got[:, :width] + logit_grad * chosen
        part, gain_grad, shift_grad = normalize_back(moe_grad, normal, inverse, gain)
        small_out[...] = jnp.concatenate([gain_grad, shift_grad], axis=0)
        hidden_grad = cot[...].astype(F32) + part
        hidden_grad_ref[...] = hidden_grad
        down_in = hidden_grad.astype(BF)
        down_in_ref[...] = down_in
        whole[...] = t_mm(down_in, act[...]).astype(BF)
        links.write_sum(sums, whole, 0, size)

    shape = jax.ShapeDtypeStruct
    outs = [
        shape((count, width), F32), shape((count, width), BF), shape((2, width), F32), shape((n, width), F32),
    ] + links.sum_shapes(size, units)
    args = [slots, routes, hidden, gates, small, cotangent, activated, back]
    hidden_grad, down_in, small_out, centroid_out, *sums = call(
        kernel, outs, args, "v" * len(args), [pltpu.VMEM((width, units), BF)], "gate_back",
        2 * count * width * units * 2, 8 * count * units,
    )
    return hidden_grad, down_in, small_out, centroid_out, sums


def widen_back(links, down_in, slope, second_in, weight_down):
    count, width = down_in.shape
    units = slope.shape[1]
    size = units // links.n
    pieces = len(weight_down.arrays)

    def kernel(down_in_ref, slope_ref, second, *refs):
        down_refs, refs = refs[:pieces], refs[pieces:]
        grad, *sums = refs[:-3]
        down, sems, whole = refs[-3:]
        for copy in weight_down.start(down_refs, down, sems):
            copy.wait()
        rows = down_in_ref[...]
        part = units // 4
        for i in range(4):
            at = pl.ds(i * part, part)
            piece = (mm(rows, down[:, at]) * slope_ref[:, at].astype(F32)).astype(BF)
            grad[:, at] = piece
            whole[at] = t_mm(piece, second[...]).astype(BF)
        links.write_sum(sums, whole, 0, size)

    outs = [jax.ShapeDtypeStruct((count, units), BF)] + links.sum_shapes(size, width)
    args = [down_in, slope, second_in]
    spaces = "vvv" + "a" * pieces
    scratch = weight_down.scratch() + [pltpu.VMEM((units, width), BF)]
    grad, *sums = call(
        kernel, outs, args + weight_down.arrays, spaces, scratch, "widen_back",
        4 * count * width * units, 8 * width * units,
    )
    return grad, sums


def second_back(links, widened_grad, after_attn, hidden_grad, mixed, small, weight_up, after):
    count, width = after_attn.shape
    n = links.n
    size = width // n
    pieces = len(weight_up.arrays)

    def kernel(grad, after_ref, hidden_grad_ref, mixed_ref, small_ref, *refs):
        up_refs, refs = refs[:pieces], refs[pieces:]
        after_grad_ref, attn_grad_ref, small_out, *sums = refs[:-3]
        up, sems, whole = refs[-3:]
        copies = weight_up.start(up_refs, up, sems)
        normal, inverse = normalize(after_ref[...])
        for copy in copies:
            copy.wait()
        second_grad = mm_t(grad[...], up[...])
        back, gain_grad, shift_grad = normalize_back(second_grad, normal, inverse, small_ref[1:2])
        small_out[...] = jnp.concatenate([gain_grad, shift_grad], axis=0)
        after_grad = hidden_grad_ref[...] + back
        after_grad_ref[...] = after_grad
        attn_grad = after_grad.astype(BF)
        attn_grad_ref[...] = attn_grad
        whole[...] = t_mm(attn_grad, mixed_ref[...]).astype(BF)
        links.write_sum(sums, whole, 0, size)

    shape = jax.ShapeDtypeStruct
    outs = [shape((count, width), F32), shape((count, width), BF), shape((2, width), F32)]
    outs += links.sum_shapes(size, width)
    args = [widened_grad, after_attn, hidden_grad, mixed, small]
    spaces = "vvvvv" + "a" * pieces
    scratch = weight_up.scratch() + [pltpu.VMEM((width, width), BF)]
    after_grad, attn_grad, small_out, *sums = call(
        kernel, outs, args + weight_up.arrays, spaces, scratch, "second_back",
        2 * count * width * 4 * width, 8 * width * 4 * width, after,
    )
    return after_grad, attn_grad, small_out, sums


def attend_back(attn_grad, projected, lse, segments, weight_out, after):
    count, width = attn_grad.shape
    pairs = width // (2 * HEAD_DIM)
    block = 128
    blocks = count // block
    n_out = len(weight_out.arrays)

    def kernel(attn_ref, proj, lse, seg_c, seg_r, *refs):
        out_refs, refs = refs[:n_out], refs[n_out:]
        grad, w_out, out_sems, bias, mixed_grad = refs
        copies = weight_out.start(out_refs, w_out, out_sems)
        bias[...] = bias_of(seg_c[...], seg_r[...])
        for copy in copies:
            copy.wait()
        mixed_grad[...] = mm(attn_ref[...], w_out[...]).astype(BF)
        masks = half_masks()
        lane = lax.broadcasted_iota(I32, (block, 128), 1)

        def pair(i, carry):
            at = [pl.ds(pl.multiple_of(part * width + 128 * i, 128), 128) for part in range(3)]
            k_grad = [jnp.zeros((block, 128), F32) for _ in range(blocks)]
            v_grad = [jnp.zeros((block, 128), F32) for _ in range(blocks)]
            for b in range(blocks):
                mine, keys = pl.ds(b * block, block), pl.ds(0, (b + 1) * block)
                q, k, v = proj[mine, at[0]] * 0.125, proj[keys, at[1]], proj[keys, at[2]]
                upper = mixed_grad[mine, at[0]]
                kept = lse[mine]
                q_grad = jnp.zeros((block, 128), F32)
                for h in range(2):
                    q_h, upper_h = q * masks[h], upper * masks[h]
                    log_total = jnp.sum(jnp.where(lane == 2 * i + h, kept, 0.0), axis=1, keepdims=True)
                    probs = jnp.exp(mm_t(q_h, k) + bias[mine, keys] - log_total)
                    probs_grad = mm_t(upper_h, v)
                    mean = jnp.sum(probs * probs_grad, axis=1, keepdims=True)
                    scores_grad = (probs * (probs_grad - mean)).astype(BF)
                    q_grad += mm(scores_grad, k * masks[h])
                    dv = t_mm(probs.astype(BF), upper_h)
                    dk = t_mm(scores_grad, q_h)
                    for c in range(b + 1):
                        v_grad[c] += dv[c * block : (c + 1) * block]
                        k_grad[c] += dk[c * block : (c + 1) * block]
                grad[mine, at[0]] = (q_grad * 0.125).astype(BF)
            for c in range(blocks):
                mine = pl.ds(c * block, block)
                grad[mine, at[1]] = k_grad[c].astype(BF)
                grad[mine, at[2]] = v_grad[c].astype(BF)
            return carry

        lax.fori_loop(0, pairs, pair, 0)

    args = [attn_grad, projected, lse, segments.reshape(count, 1), segments]
    spaces = "v" * len(args) + "a" * n_out
    scratch = weight_out.scratch() + [pltpu.VMEM((count, count), F32), pltpu.VMEM((count, width), BF)]
    return call(
        kernel, [jax.ShapeDtypeStruct((count, 3 * width), BF)], args + weight_out.arrays, spaces, scratch,
        "attend_back", 2 * count * width * (width + 5 * count) * 2, 12 * count * width * 4, after,
    )[0]


def project_back(links, projected_grad, first_in, after):
    width = first_in.shape[1]
    size = 3 * width // links.n

    def kernel(grad, first, *refs):
        whole = refs[-1]
        whole[...] = t_mm(grad[...], first[...]).astype(BF)
        links.write_sum(refs[:-1], whole, 0, size)

    return call(
        kernel, links.sum_shapes(size, width), [projected_grad, first_in], "vv",
        [pltpu.VMEM((3 * width, width), BF)], "project_back", 6 * width**3, 12 * width * width, after,
    )


def tokens_back(links, projected_grad, tokens, after_grad, small, smalls, centroid_grad, weight_in, after):
    count, width = tokens.shape
    n, n_in = links.n, len(weight_in.arrays)
    cols, rows = width // n, small.shape[0]

    def kernel(grad, tok, after_ref, small_ref, small_2, small_3, centroids, *refs):
        in_refs, refs = refs[:n_in], refs[n_in:]
        out, *sums = refs[:-2]
        w_in, sems = refs[-2:]
        copies = weight_in.start(in_refs, w_in, sems)
        normal, inverse = normalize(tok[...].astype(F32))
        for copy in copies:
            copy.wait()
        first_grad = mm(grad[...], w_in[...])
        back, gain_grad, shift_grad = normalize_back(first_grad, normal, inverse, small_ref[0:1])
        out[...] = after_ref[...] + back
        parts = [gain_grad, small_2[0:1], small_3[0:1], shift_grad, small_2[1:2], small_3[1:2]]
        parts += [centroids[...], jnp.zeros((rows - 6 - n, width), F32)]
        both = jnp.concatenate(parts, axis=0).astype(BF)
        me = lax.axis_index("expert") if links.cube else 0
        source = lax.broadcasted_iota(I32, (128, width), 0)
        place = lax.broadcasted_iota(I32, (128, width), 1)
        for k in range(n):
            mine = (place == source + (me ^ k) * cols) & (source < cols)
            block = mm_t(both, jnp.where(mine, 1.0, 0.0).astype(BF)).astype(BF)
            ref, i = (sums[k % 2], k // 2) if links.cube else (sums[0], k)
            ref[i] = jnp.zeros((rows, width), BF)
            ref[i, :, :128] = block

    outs = [jax.ShapeDtypeStruct((count, width), F32)] + links.sum_shapes(rows, width)
    args = [projected_grad, tokens, after_grad, small, *smalls, centroid_grad]
    out, *sums = call(
        kernel, outs, args + weight_in.arrays, "v" * len(args) + "a" * n_in, weight_in.scratch(),
        "tokens_back", 6 * count * width * width, 20 * count * width, after,
    )
    return out, sums


def on_device(
    n, m, tokens, segments, routes, norm_gains, norm_shifts, project_in, project_out,
    dense_up, dense_down, centroids, expert_up, expert_down, cotangent,
):
    count, width = tokens.shape
    BEFORE.clear()
    capacity = 2 * count // n
    total = n * capacity
    own_hidden = expert_up.shape[2]
    links = Links(n, m)
    cols = width // n

    def chunk(start, wide):
        part = slice(start, start + wide)
        return jnp.concatenate([expert_up[0][:, part], expert_down[0][:, part]], axis=0)

    chunks = [640, 128] if own_hidden == 768 and m == 4 else [own_hidden]
    gathered, start = [], 0
    for wide in chunks:
        whole = lax.all_gather(chunk(start, wide), "dp", axis=0, tiled=True)
        gathered.append(whole.reshape(m, 2, width, wide))
        start += wide

    pad = -(6 + n) % 16
    small = jnp.concatenate([norm_gains, norm_shifts, centroids], axis=0)
    small = jnp.pad(small, ((0, pad), (0, width - cols)))
    group = [project_in.T, project_out.T, small]
    started = links.start(jnp.concatenate(group, axis=0))
    weight_in, weight_out, weight_small = links.by_rows([a.shape[0] for a in group], started)
    started_up = links.start(dense_up, links.second)
    started_down = links.start(dense_down.T, links.second)

    row_slots, slots, cots = prepare(links, routes, cotangent, capacity)
    first_in, projected, mixed, lse, after_attn, second_in, small = attend(
        n, tokens, segments, weight_small, weight_in, weight_out, []
    )
    weight_up = links.by_columns(started_up, [small])
    (weight_down,) = links.by_rows([cols], started_down, [small])
    cots = links.exchange(cots, links.second)
    activated, slope = widen(second_in, weight_up, [])
    hidden, gates, sent = dispatch(
        links, activated, after_attn, small, row_slots, routes, weight_down, total, [cots]
    )
    rows, grads, *across = expert_rows(links.exchange(sent), cots, width, [])

    sums, expert_sums = None, []
    for c, whole in enumerate(gathered):
        if c < len(chunks) - 1:
            w_grads, *sums = expert(rows, grads, across, whole, sums, None)
            expert_sums.append(w_grads)
        else:
            back, results, acts, pre_grads = expert(rows, grads, across, whole, sums, cots)
    back = links.exchange(back)
    expert_sums.append(expert_grads(m, across, acts, pre_grads))

    def own_sum(grads):
        sums = lax.psum_scatter(grads.reshape(-1, grads.shape[-1]), "dp", scatter_dimension=0, tiled=True)
        return sums.reshape(grads.shape[1:])

    summed = [own_sum(expert_sums[0])]
    returned = links.exchange(results, [back])

    hidden_grad, down_in, small_3, centroid_grad, sums_down = gate_back(
        links, back, slots, routes, hidden, gates, small, cotangent, activated
    )
    twin_down = links.twins(sums_down)
    widened_grad, sums_up = widen_back(links, down_in, slope, second_in, weight_down)
    twin_up = links.twins(sums_up)
    down = links.fold([sums_down], twin_down, "fold_wide")
    down_got = links.across(down)
    after_grad, attn_grad, small_2, sums_out = second_back(
        links, widened_grad, after_attn, hidden_grad, mixed, small, weight_up, [returned]
    )
    twin_out = links.twins(sums_out)
    projected_grad = attend_back(attn_grad, projected, lse, segments, weight_out, [])
    up = links.fold([sums_up, sums_out], twin_up + twin_out)
    up_got = links.across(up)
    down = links.fold_again(down, down_got)
    down_got = links.across_again(down)
    tokens_grad, sums_small = tokens_back(
        links, projected_grad, tokens, after_grad, small, [small_2, small_3], centroid_grad, weight_in, []
    )
    twin_small = links.twins(sums_small)
    for grads in expert_sums[1:]:
        summed.append(own_sum(links.gated(grads, summed + [sums_small[0]])))
    sums_in = project_back(links, projected_grad, first_in, [])
    twin_in = links.twins(sums_in)
    up = links.fold_again(up, up_got, "fold_wait")
    up_got = links.across_again(up)
    inner = links.fold([sums_in, sums_small], twin_in + twin_small)
    inner_got = links.across(inner)
    down = links.fold_last(down, down_got)
    down_got = links.inward(down)
    inner = links.fold_again(inner, inner_got)
    inner_got = links.across_again(inner)
    up = links.fold_last(up, up_got)
    up_got = links.inward(up)
    inner = links.fold_last(inner, inner_got)
    inner_got = links.inward(inner)
    output = combine(returned, slots, hidden, gates)
    down = links.joined(down, down_got)
    down_got = links.middle(down)
    up = links.joined(up, up_got)
    up_got = links.middle(up)
    inner = links.joined(inner, inner_got)
    inner_got = links.middle(inner)
    down = links.joined(down, down_got)
    down_got = links.outward(down)
    up = links.joined(up, up_got)
    up_got = links.outward(up)
    inner = links.joined(inner, inner_got)
    inner_got = links.outward(inner)
    expert_sums = finish(summed)
    down_sum = links.settled(down, down_got)
    units, columns = dense_up.shape[1], project_in.shape[1]
    up_sum, out_sum = links.settled_across(up, up_got, units)
    in_sum, gains_sum, shifts_sum, centroids_sum = links.settled_small(inner, inner_got, columns, cols)

    return (
        output, tokens_grad, gains_sum, shifts_sum, in_sum.T, out_sum.T, up_sum,
        down_sum.T, centroids_sum, expert_sums[0][None], expert_sums[1][None],
    )


def solution(mesh):
    sizes = dict(mesh.shape)
    both, over = P(("dp", "expert"), None), P(None, "expert")
    expert_place = P("expert", None, "dp")
    return jax.shard_map(
        functools.partial(on_device, sizes["expert"], sizes["dp"]),
        mesh=mesh,
        in_specs=(both,) * 3 + (over,) * 7 + (expert_place,) * 2 + (both,),
        out_specs=(both,) * 2 + (over,) * 7 + (expert_place,) * 2,
        check_vma=False,
    )
```

```python
import functools

import jax
import jax.numpy as jnp
from jax import lax
from jax.experimental import pallas as pl
from jax.experimental.pallas import tpu as pltpu
from jax.sharding import PartitionSpec as P

HEAD_DIM = 64
EXTRA = 128
BF = jnp.bfloat16
F32 = jnp.float32
I32 = jnp.int32
ROOT = 0.7978845608028654
COST = dict(
    prepare=3, attend=16, widen=9, dispatch=10, expert_rows=4, expert=20, expert_last=10, expert_grads=6, gate_back=10, widen_back=12, fold=1, fold_wide=1,
    second_back=17, attend_back=2, fold_again=1, fold_wait=12, project_back=2, tokens_back=2, fold_last=1, joined=6,
    combine=1, finish=1, settle=1,
)
WIDE = ("attend", "widen", "dispatch", "expert", "expert_last", "expert_grads", "gate_back", "fold_wide", "widen_back", "second_back", "attend_back", "tokens_back", "settle")
VMEM_LIMIT = 60 * 1024 * 1024


def mm(left, right):
    return lax.dot_general(left, right, (((1,), (0,)), ((), ())), preferred_element_type=F32)


def mm_t(left, right):
    return lax.dot_general(left, right, (((1,), (1,)), ((), ())), preferred_element_type=F32)


def t_mm(left, right):
    return lax.dot_general(left, right, (((0,), (0,)), ((), ())), preferred_element_type=F32)


def normalize(rows):
    share = 1.0 / rows.shape[-1]
    centred = rows - jnp.sum(rows, axis=-1, keepdims=True) * share
    spread = jnp.sum(centred * centred, axis=-1, keepdims=True) * share
    inverse = lax.rsqrt(spread + 1e-05)
    return centred * inverse, inverse


def normalize_back(grad, normal, inverse, gain):
    share = 1.0 / grad.shape[-1]
    scaled = grad * gain
    first = jnp.sum(scaled, axis=-1, keepdims=True) * share
    second = jnp.sum(scaled * normal, axis=-1, keepdims=True) * share
    rows = inverse * (scaled - first - normal * second)
    return rows, jnp.sum(grad * normal, axis=0, keepdims=True), jnp.sum(grad, axis=0, keepdims=True)


def smooth_and_slope(v):
    square = v * v
    bend = jnp.tanh(v * (ROOT + ROOT * 0.044715 * square))
    half = 0.5 + 0.5 * bend
    slope = half + 0.5 * v * (1.0 - bend * bend) * (ROOT + 3.0 * ROOT * 0.044715 * square)
    return v * half, slope


def split3(v):
    hi = v.astype(BF)
    rest = v - hi.astype(F32)
    mid = rest.astype(BF)
    return hi, mid, (rest - mid.astype(F32)).astype(BF)


def scalar_columns(v):
    hi, mid, low = split3(v)
    lane = lax.broadcasted_iota(I32, (v.shape[0], EXTRA), 1)
    out = jnp.where(lane == 0, hi.astype(F32), 0.0)
    out = jnp.where(lane == 1, mid.astype(F32), out)
    return jnp.where(lane == 2, low.astype(F32), out).astype(BF)


def columns_scalar(columns):
    return jnp.sum(columns.astype(F32), axis=-1, keepdims=True)


def bias_of(by_row, by_column):
    count = by_row.shape[0]
    row = lax.broadcasted_iota(I32, (count, count), 0)
    column = lax.broadcasted_iota(I32, (count, count), 1)
    allowed = (by_row == by_column) & (row >= column)
    return jnp.where(allowed, 0.0, -1000000000.0)


def half_masks():
    lane = lax.broadcasted_iota(I32, (1, 2 * HEAD_DIM), 1)
    first = jnp.where(lane < HEAD_DIM, 1.0, 0.0)
    return first.astype(BF), (1.0 - first).astype(BF)


BEFORE = []


def smallest(outs):
    return min(outs, key=lambda a: a.size * a.dtype.itemsize)


def call(kernel, outs, args, spaces, scratch, name, flops, moved, after=(), results=None):
    where = {"v": pltpu.VMEM, "a": pl.ANY}
    after = list(after) + BEFORE
    read, waited = len(args), len(after)
    args, spaces = list(args) + list(after), spaces + "a" * waited

    def body(*refs):
        kernel(*refs[:read], *refs[read + waited :])

    got = pl.pallas_call(
        body,
        out_shape=outs,
        in_specs=[pl.BlockSpec(memory_space=where[s]) for s in spaces],
        out_specs=[pl.BlockSpec(memory_space=where[s]) for s in results or "v" * len(outs)],
        scratch_shapes=scratch,
        compiler_params=pltpu.CompilerParams(vmem_limit_bytes=VMEM_LIMIT if name in WIDE else VMEM_LIMIT // 2),
        cost_estimate=pl.CostEstimate(flops=COST[name] * 1150000000, bytes_accessed=1000, transcendentals=0),
        name=name,
    )(*args)
    BEFORE[:] = [smallest(got)]
    return got


class Weight:
    def __init__(self, arrays, copies, shape):
        self.arrays, self.copies, self.shape = arrays, copies, shape

    def scratch(self):
        return [pltpu.VMEM(self.shape, BF), pltpu.SemaphoreType.DMA((len(self.copies),))]

    def start(self, refs, whole, sems):
        me = lax.axis_index("expert")
        running = []
        for i, (index, source, place) in enumerate(self.copies):
            copy = pltpu.make_async_copy(
                refs[index].at[source], whole.at[place(me)], sems.at[i]
            )
            copy.start()
            running.append(copy)
        return running


def row_place(k, size, offset, rows, step):
    def place(me):
        if k is None:
            return (pl.ds(offset, rows),)
        return (pl.ds(pl.multiple_of((me ^ k) * size + offset, step), rows),)

    return place


def column_place(k, size, offset, rows):
    def place(me):
        if k is None:
            return (pl.ds(0, rows),)
        start = pl.multiple_of((me ^ k) * size, 128)
        return (pl.ds(offset, rows), pl.ds(start, size))

    return place


class Links:
    def __init__(self, n, m):
        self.n, self.m = n, m
        self.cube = n == 8
        self.line = m == 4
        self.second = ()

    def hop(self, value, bit):
        return lax.ppermute(value, "expert", [(i, i ^ bit) for i in range(self.n)])

    def gated(self, value, gate):
        return lax.optimization_barrier((value, *gate))[0] if gate else value

    def start(self, shard, gate=()):
        if not self.cube:
            return [shard]
        shard = self.gated(shard, gate)
        return [shard, self.hop(shard, 2), self.hop(shard, 4)]

    def pieces(self, started, gate=()):
        shard, by_x, by_y = lax.optimization_barrier((*started, *gate))[:3] if gate else started
        half = shard.shape[0] // 2 // 16 * 16
        far_a = self.hop(by_y[:half], 2)
        far_b = self.hop(by_x[half:], 4)
        self.second = (far_a, far_b)
        return [
            (0, 0, shard), (1, 0, self.hop(shard, 1)), (2, 0, by_x), (3, 0, self.hop(by_x, 1)),
            (4, 0, by_y), (5, 0, self.hop(by_y, 1)), (6, 0, far_a), (6, half, far_b),
            (7, 0, self.hop(far_a, 1)), (7, half, self.hop(far_b, 1)),
        ]

    def by_rows(self, sizes, started, gate=()):
        group = started[0]
        weights, first = [], 0
        if not self.cube:
            whole = lax.all_gather(group, "expert", axis=0, tiled=False)
            for size in sizes:
                part = whole[:, first : first + size].reshape(-1, group.shape[1])
                copies = [(0, (pl.ds(0, part.shape[0]),), row_place(None, 0, 0, part.shape[0], 8))]
                weights.append(Weight([part], copies, part.shape))
                first += size
            return weights
        pieces = self.pieces(started, gate)
        for size in sizes:
            arrays, copies = [], []
            for k, row, array in pieces:
                low, high = max(first, row), min(first + size, row + array.shape[0])
                if low < high:
                    source = (pl.ds(low - row, high - low),)
                    place = row_place(k, size, low - first, high - low, 16 if size % 16 == 0 else 8)
                    copies.append((len(arrays), source, place))
                    arrays.append(array)
            weights.append(Weight(arrays, copies, (self.n * size, group.shape[1])))
            first += size
        return weights

    def by_columns(self, started, gate=()):
        shard = started[0]
        rows, size = shard.shape
        if not self.cube:
            whole = lax.all_gather(shard, "expert", axis=1, tiled=True)
            return Weight([whole], [(0, (pl.ds(0, rows),), column_place(None, 0, 0, rows))], whole.shape)
        arrays, copies = [], []
        for k, row, array in self.pieces(started, gate):
            source = (pl.ds(0, array.shape[0]),)
            copies.append((len(arrays), source, column_place(k, size, row, array.shape[0])))
            arrays.append(array)
        return Weight(arrays, copies, (rows, self.n * size))

    def exchange(self, rows, gate=()):
        blocks = self.gated(rows, gate).reshape(self.n, -1, rows.shape[1])
        got = lax.all_to_all(blocks, "expert", split_axis=0, concat_axis=0, tiled=True)
        return got.reshape(rows.shape)

    def sum_shapes(self, rows, width):
        if not self.cube:
            return [jax.ShapeDtypeStruct((self.n, rows, width), BF)]
        return [jax.ShapeDtypeStruct((self.n // 2, rows, width), BF)] * 2

    def write_sum(self, refs, whole, first, size):
        for k in range(self.n):
            if self.cube:
                me = lax.axis_index("expert")
                step = 16 if size % 16 == 0 else 8
                start = pl.multiple_of((me ^ k) * size, step)
                refs[k % 2][k // 2, first : first + size] = whole[pl.ds(start, size)]
            else:
                refs[0][k, first : first + size] = whole[k * size : (k + 1) * size]

    def twins(self, blocks):
        return [self.hop(blocks[1], 1)] if self.cube else []

    def fold(self, groups, twins, name="fold"):
        if not self.cube:
            return [jnp.concatenate([g[0] for g in groups], axis=1)]
        rows = [g[0].shape[1] for g in groups]
        total, columns = sum(rows), groups[0][0].shape[2]
        half = total // 2 // 16 * 16

        def kernel(*refs):
            count = len(groups)
            outs = refs[2 * count :]
            first = 0
            for even, odd in zip(refs[:count], refs[count : 2 * count]):
                for m in range(4):
                    value = (even[m].astype(F32) + odd[m].astype(F32)).astype(BF)
                    low, high = first, first + even.shape[1]
                    cut = min(max(half, low), high)
                    if low < cut:
                        outs[m % 2][m // 2, low:cut] = value[: cut - low]
                    if cut < high:
                        outs[2 + m // 2][m % 2, cut - half : high - half] = value[cut - low :]
                first += even.shape[1]

        outs = [jax.ShapeDtypeStruct((2, half, columns), BF)] * 2
        outs += [jax.ShapeDtypeStruct((2, total - half, columns), BF)] * 2
        args = [g[0] for g in groups] + list(twins)
        return list(call(kernel, outs, args, "v" * len(args), [], name, 0, 0))

    def across(self, kept):
        return [self.hop(kept[1], 2), self.hop(kept[3], 4)] if self.cube else []

    def fold_again(self, kept, got, name="fold_again"):
        if not self.cube:
            return kept

        def kernel(first, got_first, second, got_second, *outs):
            for i, (mine, other) in enumerate(((first, got_first), (second, got_second))):
                for j in range(2):
                    outs[2 * i + j][...] = (mine[j].astype(F32) + other[j].astype(F32)).astype(BF)

        outs = [jax.ShapeDtypeStruct(a.shape[1:], BF) for a in (kept[0], kept[0], kept[2], kept[2])]
        args = [kept[0], got[0], kept[2], got[1]]
        return list(call(kernel, outs, args, "vvvv", [], name, 0, 0))

    def across_again(self, kept):
        return [self.hop(kept[1], 4), self.hop(kept[3], 2)] if self.cube else []

    def fold_last(self, kept, got):
        if not self.cube:
            return lax.psum_scatter(kept[0], "expert", scatter_dimension=0, tiled=True)[0]
        half = kept[0].shape[0]

        def kernel(first, got_first, second, got_second, out):
            out[:half] = (first[...].astype(F32) + got_first[...].astype(F32)).astype(BF)
            out[half:] = (second[...].astype(F32) + got_second[...].astype(F32)).astype(BF)

        rows = half + kept[2].shape[0]
        outs = [jax.ShapeDtypeStruct((rows, kept[0].shape[1]), BF)]
        return call(kernel, outs, [kept[0], got[0], kept[2], got[1]], "vvvv", [], "fold_last", 0, 0)[0]

    def along(self, value, pairs):
        return lax.ppermute(value, "dp", pairs)

    def inward(self, value):
        return [self.along(value, [(0, 1), (3, 2)])] if self.line else []

    def middle(self, value):
        return [self.along(value, [(1, 2), (2, 1)])] if self.line else []

    def outward(self, value):
        return [self.along(value, [(1, 0), (2, 3)])] if self.line else []

    def joined(self, value, got):
        if not self.line:
            return value

        def kernel(mine, other, out):
            out[...] = (mine[...].astype(F32) + other[...].astype(F32)).astype(BF)

        outs = [jax.ShapeDtypeStruct(value.shape, BF)]
        return call(kernel, outs, [value, got[0]], "vv", [], "joined", 0, 0)[0]

    def settled(self, value, got):
        if not self.line:
            return lax.psum(value, "dp").astype(F32)

        def kernel(mine, other, out):
            place = lax.axis_index("dp")

            def write(ref):
                out[...] = ref[...].astype(F32)

            middle = (place == 1) | (place == 2)
            pl.when(middle)(lambda: write(mine))
            pl.when(jnp.logical_not(middle))(lambda: write(other))

        outs = [jax.ShapeDtypeStruct(value.shape, F32)]
        return call(kernel, outs, [value, got[0]], "vv", [], "settle", 0, 0)[0]

    def settled_small(self, value, got, columns, cols):
        n = self.n
        rows = [(columns, 3), (columns + 3, 3), (columns + 6, n)]
        if not self.line:
            value = lax.psum(value, "dp").astype(F32)
            return [value[:columns]] + [value[i : i + size, :cols] for i, size in rows]

        def kernel(mine, other, out, *smalls):
            place = lax.axis_index("dp")

            def write(ref):
                out[...] = ref[:columns].astype(F32)
                rest = ref[columns:, :128].astype(F32)
                for (i, size), small in zip(rows, smalls):
                    small[...] = rest[i - columns : i - columns + size, :cols]

            middle = (place == 1) | (place == 2)
            pl.when(middle)(lambda: write(mine))
            pl.when(jnp.logical_not(middle))(lambda: write(other))

        outs = [jax.ShapeDtypeStruct((columns, value.shape[1]), F32)]
        outs += [jax.ShapeDtypeStruct((size, cols), F32) for _, size in rows]
        return call(kernel, outs, [value, got[0]], "vv", [], "settle", 0, 0)

    def settled_across(self, value, got, units):
        if not self.line:
            value = lax.psum(value, "dp").astype(F32)
            return value[:units].T, value[units:]

        def kernel(mine, other, up, out):
            place = lax.axis_index("dp")

            def write(ref):
                up[...] = ref[:units].astype(F32).T
                out[...] = ref[units:].astype(F32)

            middle = (place == 1) | (place == 2)
            pl.when(middle)(lambda: write(mine))
            pl.when(jnp.logical_not(middle))(lambda: write(other))

        rows, width = value.shape
        outs = [jax.ShapeDtypeStruct((width, units), F32), jax.ShapeDtypeStruct((rows - units, width), F32)]
        return call(kernel, outs, [value, got[0]], "vv", [], "settle", 0, 0)


def finish(parts):
    width = parts[0].shape[1]

    def kernel(*refs):
        ups, downs = refs[-2:]
        first = 0
        for ref in refs[:-2]:
            for i, out in enumerate((ups, downs)):
                out[:, first : first + ref.shape[2]] = ref[i].astype(F32)
            first += ref.shape[2]

    outs = [jax.ShapeDtypeStruct((width, sum(p.shape[2] for p in parts)), F32)] * 2
    return call(kernel, outs, parts, "v" * len(parts), [], "finish", 0, 0)


def prepare(links, routes, cotangent, capacity):
    count, width = cotangent.shape
    n = links.n
    total = n * capacity

    def kernel(by_row, by_column, cot, row_out, column_out, out):
        route_c, route_r = by_row[...], by_column[...]
        token = lax.broadcasted_iota(I32, (count, count), 0)
        other = lax.broadcasted_iota(I32, (count, count), 1)
        same = route_c == route_r
        rank_c = jnp.sum(jnp.where(same & (other < token), 1.0, 0.0), axis=1, keepdims=True)
        rank_r = jnp.sum(jnp.where(same & (token < other), 1.0, 0.0), axis=0, keepdims=True)
        slot_c = route_c * capacity + rank_c.astype(I32)
        slot_r = route_r * capacity + rank_r.astype(I32)
        column_out[...] = slot_c
        row_out[...] = slot_r
        place = lax.broadcasted_iota(I32, (total, count), 0)
        to_slots = jnp.where(place == slot_r, 1.0, 0.0).astype(BF)
        out[...] = mm(to_slots, cot[...]).astype(BF)

    outs = [jax.ShapeDtypeStruct((1, count), I32), jax.ShapeDtypeStruct((count, 1), I32)]
    outs.append(jax.ShapeDtypeStruct((total, width), BF))
    args = [routes, routes.reshape(1, count), cotangent]
    return call(
        kernel, outs, args, "vvv", [], "prepare", 2 * total * count * width, 4 * total * width
    )


def attend(n, tokens, segments, weight_small, weight_in, weight_out, after):
    count, width = tokens.shape
    pairs = width // (2 * HEAD_DIM)
    block = 128
    n_small, n_in, n_out = len(weight_small.arrays), len(weight_in.arrays), len(weight_out.arrays)
    small_rows, cols = weight_small.shape[0] // n, width // n

    def kernel(tok, seg_c, seg_r, *refs):
        small_refs, refs = refs[:n_small], refs[n_small:]
        in_refs, refs = refs[:n_in], refs[n_in:]
        out_refs, refs = refs[:n_out], refs[n_out:]
        first_ref, proj, mixed, lse, after_ref, second_ref, small_ref = refs[:7]
        w_small, small_sems, w_in, in_sems, w_out, out_sems, bias = refs[7:]
        small_copies = weight_small.start(small_refs, w_small, small_sems)
        in_copies = weight_in.start(in_refs, w_in, in_sems)
        out_copies = weight_out.start(out_refs, w_out, out_sems)
        rows = tok[...].astype(F32)
        normal, _ = normalize(rows)
        source = lax.broadcasted_iota(I32, (cols, width), 0)
        place = lax.broadcasted_iota(I32, (cols, width), 1)
        for copy in small_copies:
            copy.wait()
        small = jnp.zeros((small_rows, width), F32)
        for j in range(n):
            spread = jnp.where(place == source + j * cols, 1.0, 0.0).astype(BF)
            small += mm(w_small[j * small_rows : (j + 1) * small_rows, :cols], spread)
        small_ref[...] = small
        first = (normal * small_ref[0:1] + small_ref[3:4]).astype(BF)
        first_ref[...] = first
        bias[...] = bias_of(seg_c[...], seg_r[...])
        lse[...] = jnp.zeros_like(lse)
        for copy in in_copies:
            copy.wait()
        proj[...] = mm_t(first, w_in[...]).astype(BF)
        masks = half_masks()
        lane = lax.broadcasted_iota(I32, (block, 128), 1)

        def pair(i, carry):
            at = [pl.ds(pl.multiple_of(part * width + 128 * i, 128), 128) for part in range(3)]
            for b in range(count // block):
                mine, keys = pl.ds(b * block, block), pl.ds(0, (b + 1) * block)
                q, k, v = proj[mine, at[0]] * 0.125, proj[keys, at[1]], proj[keys, at[2]]
                got = jnp.zeros((block, 128), F32)
                kept = lse[mine]
                for h in range(2):
                    scores = mm_t(q * masks[h], k) + bias[mine, keys]
                    top = jnp.max(scores, axis=1, keepdims=True)
                    lifted = jnp.exp(scores - top)
                    totals = jnp.sum(lifted, axis=1, keepdims=True)
                    probs = (lifted * (1.0 / totals)).astype(BF)
                    got += mm(probs, v * masks[h])
                    kept = jnp.where(lane == 2 * i + h, top + jnp.log(totals), kept)
                lse[mine] = kept
                mixed[mine, at[0]] = got.astype(BF)
            return carry

        lax.fori_loop(0, pairs, pair, 0)
        for copy in out_copies:
            copy.wait()
        after = rows + mm_t(mixed[...], w_out[...])
        after_ref[...] = after
        normal, _ = normalize(after)
        second_ref[...] = (normal * small_ref[1:2] + small_ref[4:5]).astype(BF)

    shape = jax.ShapeDtypeStruct
    outs = [
        shape((count, width), BF), shape((count, 3 * width), BF), shape((count, width), BF),
        shape((count, 128), F32), shape((count, width), F32), shape((count, width), BF),
        shape((small_rows, width), F32),
    ]
    args = [tokens, segments.reshape(count, 1), segments]
    args += weight_small.arrays + weight_in.arrays + weight_out.arrays
    spaces = "vvv" + "a" * (n_small + n_in + n_out)
    scratch = weight_small.scratch() + weight_in.scratch() + weight_out.scratch() + [pltpu.VMEM((count, count), F32)]
    flops = 2 * count * width * (4 * width + 2 * count) * 2
    return call(kernel, outs, args, spaces, scratch, "attend", flops, 12 * count * width * 4, after)


def widen(second_in, weight_up, after):
    count = second_in.shape[0]
    hidden = weight_up.shape[1]
    pieces = len(weight_up.arrays)
    part = hidden // 4

    def kernel(second, *refs):
        up_refs, (act_ref, slope_ref, up, sems) = refs[:pieces], refs[pieces:]
        for copy in weight_up.start(up_refs, up, sems):
            copy.wait()
        rows = second[...]
        for i in range(4):
            at = pl.ds(i * part, part)
            value, slope = smooth_and_slope(mm(rows, up[:, at]))
            act_ref[:, at] = value.astype(BF)
            slope_ref[:, at] = slope.astype(BF)

    outs = [jax.ShapeDtypeStruct((count, hidden), BF)] * 2
    args = [second_in] + weight_up.arrays
    return call(
        kernel, outs, args, "v" + "a" * pieces, weight_up.scratch(), "widen",
        4 * count * hidden * second_in.shape[1], 8 * count * hidden, after,
    )


def dispatch(links, activated, after_attn, small, row_slots, routes, weight_down, total, after):
    count, width = after_attn.shape
    n = links.n
    pieces = len(weight_down.arrays)

    def kernel(act, after, small_ref, slot_r, route_c, *refs):
        down_refs, refs = refs[:pieces], refs[pieces:]
        hidden_ref, gates_ref, sent_ref = refs[:-2]
        down, sems = refs[-2:]
        for copy in weight_down.start(down_refs, down, sems):
            copy.wait()
        hidden = after[...] + mm_t(act[...], down[...])
        hidden_ref[...] = hidden
        normal, _ = normalize(hidden)
        moe_in = normal * small_ref[2:3] + small_ref[5:6]
        lane = lax.broadcasted_iota(I32, (count, n), 1)
        onehot = jnp.where(lane == route_c[...], 1.0, 0.0).astype(BF)
        chosen = mm(onehot, small_ref[6 : 6 + n].astype(BF))
        logit = jnp.sum(moe_in * chosen, axis=1, keepdims=True)
        gates = 1.0 / (1.0 + jnp.exp(-logit))
        gates_ref[...] = gates
        sent = jnp.concatenate([moe_in.astype(BF), scalar_columns(gates)], axis=1)
        place = lax.broadcasted_iota(I32, (total, count), 0)
        to_slots = jnp.where(place == slot_r[...], 1.0, 0.0).astype(BF)
        sent_ref[...] = mm(to_slots, sent).astype(BF)

    shape = jax.ShapeDtypeStruct
    outs = [shape((count, width), F32), shape((count, 1), F32)]
    outs.append(shape((total, width + EXTRA), BF))
    args = [activated, after_attn, small, row_slots, routes] + weight_down.arrays
    return call(
        kernel, outs, args, "vvvvv" + "a" * pieces, weight_down.scratch(), "dispatch",
        4 * count * width * 4 * width, 16 * count * width, after,
    )


def expert_rows(arrived, cots, width, after):
    total = arrived.shape[0]

    def kernel(arrived_ref, cot_ref, rows_ref, grads_ref, rows_across, grads_across):
        rows = arrived_ref[:, :width]
        rows_ref[...] = rows
        rows_across[...] = rows.T
        gates = columns_scalar(arrived_ref[:, width:])
        grads = (gates * cot_ref[...].astype(F32)).astype(BF)
        grads_ref[...] = grads
        grads_across[...] = grads.T

    outs = [jax.ShapeDtypeStruct((total, width), BF)] * 2 + [jax.ShapeDtypeStruct((width, total), BF)] * 2
    return call(kernel, outs, [arrived, cots], "vv", [], "expert_rows", 0, 0, after)


def expert(rows, grads, across, weights, sums, cot):
    total, width = rows.shape
    m, _, _, wide = weights.shape
    last, started = cot is not None, sums is not None
    group = m if last and m * wide <= 512 else 1
    steps, span = m // group, group * wide

    def kernel(rows_ref, grads_ref, rows_across, grads_across, *refs):
        refs = list(refs)
        take = lambda k: [refs.pop(0) for _ in range(k)]
        carried = take(2) if started else None
        (cot_ref,) = take(1) if last else (None,)
        (weight_ref,) = take(1)
        if last:
            outs, (acts, pre_grads) = take(2), take(2)
            held, sems, out_sum, row_sum = refs
        else:
            (w_grads,), outs = take(1), take(2)
            held, sems, out_sum, row_sum, grad_held, out_sems = refs
        entering = []
        for i in range(m):
            place = held.at[i // group, :, :, pl.ds(i % group * wide, wide)]
            entering.append(pltpu.make_async_copy(weight_ref.at[i], place, sems.at[i]))
        for copy in entering:
            copy.start()
        r, g = rows_ref[...], grads_ref[...]
        leaving = []
        for i in range(steps):
            for copy in entering[i * group : (i + 1) * group]:
                copy.wait()
            up, down = held[i, 0], held[i, 1]
            value, slope = smooth_and_slope(mm(r, up))
            act = value.astype(BF)
            pre_grad = (mm(g, down) * slope).astype(BF)
            row_part, out_part = mm_t(pre_grad, up), mm_t(act, down)
            if i == 0 and started:
                row_part, out_part = row_part + carried[0][...], out_part + carried[1][...]
            if i > 0:
                row_part, out_part = row_part + row_sum[...], out_part + out_sum[...]
            row_sum[...] = row_part
            out_sum[...] = out_part
            if last:
                acts[i] = act
                pre_grads[i] = pre_grad
            else:
                grad_held[i, 0] = mm(rows_across[...], pre_grad).astype(BF)
                grad_held[i, 1] = mm(grads_across[...], act).astype(BF)
                copy = pltpu.make_async_copy(grad_held.at[i], w_grads.at[i], out_sems.at[i])
                copy.start()
                leaving.append(copy)
        if last:
            result = out_sum[...].astype(BF)
            gate_grad = jnp.sum(cot_ref[...].astype(F32) * result.astype(F32), axis=1, keepdims=True)
            outs[0][...] = jnp.concatenate([row_sum[...].astype(BF), scalar_columns(gate_grad)], axis=1)
            outs[1][...] = result
        else:
            outs[0][...] = row_sum[...]
            outs[1][...] = out_sum[...]
        for copy in leaving:
            copy.wait()

    shape = jax.ShapeDtypeStruct
    args = [rows, grads, *across] + (sums if started else []) + ([cot] if last else [])
    spaces = "v" * len(args) + "a"
    scratch = [
        pltpu.VMEM((steps, 2, width, span), BF), pltpu.SemaphoreType.DMA((m,)),
        pltpu.VMEM((total, width), F32), pltpu.VMEM((total, width), F32),
    ]
    if last:
        outs = [shape((total, width + EXTRA), BF), shape((total, width), BF)] + [shape((steps, total, span), BF)] * 2
        return call(kernel, outs, args + [weights], spaces, scratch, "expert_last", 0, 0)
    outs = [shape((m, 2, width, wide), BF)] + [shape((total, width), F32)] * 2
    scratch += [pltpu.VMEM((m, 2, width, wide), BF), pltpu.SemaphoreType.DMA((m,))]
    return call(kernel, outs, args + [weights], spaces, scratch, "expert", 0, 0, [], "avv")


def expert_grads(m, across, acts, pre_grads):
    steps, _, span = acts.shape
    width = across[0].shape[0]
    group = m // steps
    wide = span // group

    def kernel(rows_across, grads_across, acts_ref, pre_ref, out):
        for i in range(steps):
            ups = mm(rows_across[...], pre_ref[i]).astype(BF)
            downs = mm(grads_across[...], acts_ref[i]).astype(BF)
            for j in range(group):
                out[i * group + j, 0] = ups[:, j * wide : (j + 1) * wide]
                out[i * group + j, 1] = downs[:, j * wide : (j + 1) * wide]

    outs = [jax.ShapeDtypeStruct((m, 2, width, wide), BF)]
    return call(kernel, outs, [*across, acts, pre_grads], "vvvv", [], "expert_grads", 0, 0)[0]


def combine(returned, slots, hidden, gates):
    count, width = hidden.shape

    def kernel(slot_c, hidden_ref, gates_ref, got_ref, out):
        got = got_ref[...]
        place = lax.broadcasted_iota(I32, (count, got.shape[0]), 1)
        pick = jnp.where(place == slot_c[...], 1.0, 0.0).astype(BF)
        out[...] = (hidden_ref[...] + gates_ref[...] * mm(pick, got)).astype(BF)

    return call(
        kernel, [jax.ShapeDtypeStruct((count, width), BF)], [slots, hidden, gates, returned],
        "vvvv", [], "combine", 4 * count * count * width, 10 * count * width,
    )[0]


def gate_back(links, back, slots, routes, hidden, gates, small, cotangent, activated):
    count, width = hidden.shape
    n = links.n
    size = width // n
    units = activated.shape[1]

    def kernel(slot_c, route_c, hidden_ref, gates_ref, small_ref, cot, act, back_ref, *refs):
        got = back_ref[...]
        hidden_grad_ref, down_in_ref, small_out, centroid_out, *sums = refs[:-1]
        whole = refs[-1]
        place = lax.broadcasted_iota(I32, (count, got.shape[0]), 1)
        pick = jnp.where(place == slot_c[...], 1.0, 0.0).astype(BF)
        got = mm(pick, got)
        gates = gates_ref[...]
        logit_grad = columns_scalar(got[:, width:]) * gates * (1.0 - gates)
        lane = lax.broadcasted_iota(I32, (count, n), 1)
        onehot = jnp.where(lane == route_c[...], 1.0, 0.0).astype(BF)
        chosen = mm(onehot, small_ref[6 : 6 + n].astype(BF))
        normal, inverse = normalize(hidden_ref[...])
        gain = small_ref[2:3]
        moe_in = normal * gain + small_ref[5:6]
        terms = split3(logit_grad * moe_in)
        centroid_out[...] = t_mm(onehot, terms[0]) + t_mm(onehot, terms[1]) + t_mm(onehot, terms[2])
        moe_grad = got[:, :width] + logit_grad * chosen
        part, gain_grad, shift_grad = normalize_back(moe_grad, normal, inverse, gain)
        small_out[...] = jnp.concatenate([gain_grad, shift_grad], axis=0)
        hidden_grad = cot[...].astype(F32) + part
        hidden_grad_ref[...] = hidden_grad
        down_in = hidden_grad.astype(BF)
        down_in_ref[...] = down_in
        whole[...] = t_mm(down_in, act[...]).astype(BF)
        links.write_sum(sums, whole, 0, size)

    shape = jax.ShapeDtypeStruct
    outs = [
        shape((count, width), F32), shape((count, width), BF), shape((2, width), F32), shape((n, width), F32),
    ] + links.sum_shapes(size, units)
    args = [slots, routes, hidden, gates, small, cotangent, activated, back]
    hidden_grad, down_in, small_out, centroid_out, *sums = call(
        kernel, outs, args, "v" * len(args), [pltpu.VMEM((width, units), BF)], "gate_back",
        2 * count * width * units * 2, 8 * count * units,
    )
    return hidden_grad, down_in, small_out, centroid_out, sums


def widen_back(links, down_in, slope, second_in, weight_down):
    count, width = down_in.shape
    units = slope.shape[1]
    size = units // links.n
    pieces = len(weight_down.arrays)

    def kernel(down_in_ref, slope_ref, second, *refs):
        down_refs, refs = refs[:pieces], refs[pieces:]
        grad, *sums = refs[:-3]
        down, sems, whole = refs[-3:]
        for copy in weight_down.start(down_refs, down, sems):
            copy.wait()
        rows = down_in_ref[...]
        part = units // 4
        for i in range(4):
            at = pl.ds(i * part, part)
            piece = (mm(rows, down[:, at]) * slope_ref[:, at].astype(F32)).astype(BF)
            grad[:, at] = piece
            whole[at] = t_mm(piece, second[...]).astype(BF)
        links.write_sum(sums, whole, 0, size)

    outs = [jax.ShapeDtypeStruct((count, units), BF)] + links.sum_shapes(size, width)
    args = [down_in, slope, second_in]
    spaces = "vvv" + "a" * pieces
    scratch = weight_down.scratch() + [pltpu.VMEM((units, width), BF)]
    grad, *sums = call(
        kernel, outs, args + weight_down.arrays, spaces, scratch, "widen_back",
        4 * count * width * units, 8 * width * units,
    )
    return grad, sums


def second_back(links, widened_grad, after_attn, hidden_grad, mixed, small, weight_up, after):
    count, width = after_attn.shape
    n = links.n
    size = width // n
    pieces = len(weight_up.arrays)

    def kernel(grad, after_ref, hidden_grad_ref, mixed_ref, small_ref, *refs):
        up_refs, refs = refs[:pieces], refs[pieces:]
        after_grad_ref, attn_grad_ref, small_out, *sums = refs[:-3]
        up, sems, whole = refs[-3:]
        copies = weight_up.start(up_refs, up, sems)
        normal, inverse = normalize(after_ref[...])
        for copy in copies:
            copy.wait()
        second_grad = mm_t(grad[...], up[...])
        back, gain_grad, shift_grad = normalize_back(second_grad, normal, inverse, small_ref[1:2])
        small_out[...] = jnp.concatenate([gain_grad, shift_grad], axis=0)
        after_grad = hidden_grad_ref[...] + back
        after_grad_ref[...] = after_grad
        attn_grad = after_grad.astype(BF)
        attn_grad_ref[...] = attn_grad
        whole[...] = t_mm(attn_grad, mixed_ref[...]).astype(BF)
        links.write_sum(sums, whole, 0, size)

    shape = jax.ShapeDtypeStruct
    outs = [shape((count, width), F32), shape((count, width), BF), shape((2, width), F32)]
    outs += links.sum_shapes(size, width)
    args = [widened_grad, after_attn, hidden_grad, mixed, small]
    spaces = "vvvvv" + "a" * pieces
    scratch = weight_up.scratch() + [pltpu.VMEM((width, width), BF)]
    after_grad, attn_grad, small_out, *sums = call(
        kernel, outs, args + weight_up.arrays, spaces, scratch, "second_back",
        2 * count * width * 4 * width, 8 * width * 4 * width, after,
    )
    return after_grad, attn_grad, small_out, sums


def attend_back(attn_grad, projected, lse, segments, weight_out, after):
    count, width = attn_grad.shape
    pairs = width // (2 * HEAD_DIM)
    block = 128
    blocks = count // block
    n_out = len(weight_out.arrays)

    def kernel(attn_ref, proj, lse, seg_c, seg_r, *refs):
        out_refs, refs = refs[:n_out], refs[n_out:]
        grad, w_out, out_sems, bias, mixed_grad = refs
        copies = weight_out.start(out_refs, w_out, out_sems)
        bias[...] = bias_of(seg_c[...], seg_r[...])
        for copy in copies:
            copy.wait()
        mixed_grad[...] = mm(attn_ref[...], w_out[...]).astype(BF)
        masks = half_masks()
        lane = lax.broadcasted_iota(I32, (block, 128), 1)

        def pair(i, carry):
            at = [pl.ds(pl.multiple_of(part * width + 128 * i, 128), 128) for part in range(3)]
            k_grad = [jnp.zeros((block, 128), F32) for _ in range(blocks)]
            v_grad = [jnp.zeros((block, 128), F32) for _ in range(blocks)]
            for b in range(blocks):
                mine, keys = pl.ds(b * block, block), pl.ds(0, (b + 1) * block)
                q, k, v = proj[mine, at[0]] * 0.125, proj[keys, at[1]], proj[keys, at[2]]
                upper = mixed_grad[mine, at[0]]
                kept = lse[mine]
                q_grad = jnp.zeros((block, 128), F32)
                for h in range(2):
                    q_h, upper_h = q * masks[h], upper * masks[h]
                    log_total = jnp.sum(jnp.where(lane == 2 * i + h, kept, 0.0), axis=1, keepdims=True)
                    probs = jnp.exp(mm_t(q_h, k) + bias[mine, keys] - log_total)
                    probs_grad = mm_t(upper_h, v)
                    mean = jnp.sum(probs * probs_grad, axis=1, keepdims=True)
                    scores_grad = (probs * (probs_grad - mean)).astype(BF)
                    q_grad += mm(scores_grad, k * masks[h])
                    dv = t_mm(probs.astype(BF), upper_h)
                    dk = t_mm(scores_grad, q_h)
                    for c in range(b + 1):
                        v_grad[c] += dv[c * block : (c + 1) * block]
                        k_grad[c] += dk[c * block : (c + 1) * block]
                grad[mine, at[0]] = (q_grad * 0.125).astype(BF)
            for c in range(blocks):
                mine = pl.ds(c * block, block)
                grad[mine, at[1]] = k_grad[c].astype(BF)
                grad[mine, at[2]] = v_grad[c].astype(BF)
            return carry

        lax.fori_loop(0, pairs, pair, 0)

    args = [attn_grad, projected, lse, segments.reshape(count, 1), segments]
    spaces = "v" * len(args) + "a" * n_out
    scratch = weight_out.scratch() + [pltpu.VMEM((count, count), F32), pltpu.VMEM((count, width), BF)]
    return call(
        kernel, [jax.ShapeDtypeStruct((count, 3 * width), BF)], args + weight_out.arrays, spaces, scratch,
        "attend_back", 2 * count * width * (width + 5 * count) * 2, 12 * count * width * 4, after,
    )[0]


def project_back(links, projected_grad, first_in, after):
    width = first_in.shape[1]
    size = 3 * width // links.n

    def kernel(grad, first, *refs):
        whole = refs[-1]
        whole[...] = t_mm(grad[...], first[...]).astype(BF)
        links.write_sum(refs[:-1], whole, 0, size)

    return call(
        kernel, links.sum_shapes(size, width), [projected_grad, first_in], "vv",
        [pltpu.VMEM((3 * width, width), BF)], "project_back", 6 * width**3, 12 * width * width, after,
    )


def tokens_back(links, projected_grad, tokens, after_grad, small, smalls, centroid_grad, weight_in, after):
    count, width = tokens.shape
    n, n_in = links.n, len(weight_in.arrays)
    cols, rows = width // n, small.shape[0]

    def kernel(grad, tok, after_ref, small_ref, small_2, small_3, centroids, *refs):
        in_refs, refs = refs[:n_in], refs[n_in:]
        out, *sums = refs[:-2]
        w_in, sems = refs[-2:]
        copies = weight_in.start(in_refs, w_in, sems)
        normal, inverse = normalize(tok[...].astype(F32))
        for copy in copies:
            copy.wait()
        first_grad = mm(grad[...], w_in[...])
        back, gain_grad, shift_grad = normalize_back(first_grad, normal, inverse, small_ref[0:1])
        out[...] = after_ref[...] + back
        parts = [gain_grad, small_2[0:1], small_3[0:1], shift_grad, small_2[1:2], small_3[1:2]]
        parts += [centroids[...], jnp.zeros((rows - 6 - n, width), F32)]
        both = jnp.concatenate(parts, axis=0).astype(BF)
        me = lax.axis_index("expert") if links.cube else 0
        source = lax.broadcasted_iota(I32, (128, width), 0)
        place = lax.broadcasted_iota(I32, (128, width), 1)
        for k in range(n):
            mine = (place == source + (me ^ k) * cols) & (source < cols)
            block = mm_t(both, jnp.where(mine, 1.0, 0.0).astype(BF)).astype(BF)
            ref, i = (sums[k % 2], k // 2) if links.cube else (sums[0], k)
            ref[i] = jnp.zeros((rows, width), BF)
            ref[i, :, :128] = block

    outs = [jax.ShapeDtypeStruct((count, width), F32)] + links.sum_shapes(rows, width)
    args = [projected_grad, tokens, after_grad, small, *smalls, centroid_grad]
    out, *sums = call(
        kernel, outs, args + weight_in.arrays, "v" * len(args) + "a" * n_in, weight_in.scratch(),
        "tokens_back", 6 * count * width * width, 20 * count * width, after,
    )
    return out, sums


def on_device(
    n, m, tokens, segments, routes, norm_gains, norm_shifts, project_in, project_out,
    dense_up, dense_down, centroids, expert_up, expert_down, cotangent,
):
    count, width = tokens.shape
    BEFORE.clear()
    capacity = 2 * count // n
    total = n * capacity
    own_hidden = expert_up.shape[2]
    links = Links(n, m)
    cols = width // n

    def chunk(start, wide):
        part = slice(start, start + wide)
        return jnp.concatenate([expert_up[0][:, part], expert_down[0][:, part]], axis=0)

    chunks = [640, 128] if own_hidden == 768 and m == 4 else [own_hidden]
    gathered, start = [], 0
    for wide in chunks:
        whole = lax.all_gather(chunk(start, wide), "dp", axis=0, tiled=True)
        gathered.append(whole.reshape(m, 2, width, wide))
        start += wide

    pad = -(6 + n) % 16
    small = jnp.concatenate([norm_gains, norm_shifts, centroids], axis=0)
    small = jnp.pad(small, ((0, pad), (0, width - cols)))
    group = [project_in.T, project_out.T, small]
    started = links.start(jnp.concatenate(group, axis=0))
    weight_in, weight_out, weight_small = links.by_rows([a.shape[0] for a in group], started)
    started_up = links.start(dense_up, links.second)
    started_down = links.start(dense_down.T, links.second)

    row_slots, slots, cots = prepare(links, routes, cotangent, capacity)
    first_in, projected, mixed, lse, after_attn, second_in, small = attend(
        n, tokens, segments, weight_small, weight_in, weight_out, []
    )
    weight_up = links.by_columns(started_up, [small])
    (weight_down,) = links.by_rows([cols], started_down, [small])
    cots = links.exchange(cots, links.second)
    activated, slope = widen(second_in, weight_up, [])
    hidden, gates, sent = dispatch(
        links, activated, after_attn, small, row_slots, routes, weight_down, total, [cots]
    )
    rows, grads, *across = expert_rows(links.exchange(sent), cots, width, [])

    sums, expert_sums = None, []
    for c, whole in enumerate(gathered):
        if c < len(chunks) - 1:
            w_grads, *sums = expert(rows, grads, across, whole, sums, None)
            expert_sums.append(w_grads)
        else:
            back, results, acts, pre_grads = expert(rows, grads, across, whole, sums, cots)
    back = links.exchange(back)
    expert_sums.append(expert_grads(m, across, acts, pre_grads))

    def own_sum(grads):
        sums = lax.psum_scatter(grads.reshape(-1, grads.shape[-1]), "dp", scatter_dimension=0, tiled=True)
        return sums.reshape(grads.shape[1:])

    summed = [own_sum(expert_sums[0])]
    returned = links.exchange(results, [back])

    hidden_grad, down_in, small_3, centroid_grad, sums_down = gate_back(
        links, back, slots, routes, hidden, gates, small, cotangent, activated
    )
    twin_down = links.twins(sums_down)
    widened_grad, sums_up = widen_back(links, down_in, slope, second_in, weight_down)
    twin_up = links.twins(sums_up)
    down = links.fold([sums_down], twin_down, "fold_wide")
    down_got = links.across(down)
    after_grad, attn_grad, small_2, sums_out = second_back(
        links, widened_grad, after_attn, hidden_grad, mixed, small, weight_up, [returned]
    )
    twin_out = links.twins(sums_out)
    projected_grad = attend_back(attn_grad, projected, lse, segments, weight_out, [])
    up = links.fold([sums_up, sums_out], twin_up + twin_out)
    up_got = links.across(up)
    down = links.fold_again(down, down_got)
    down_got = links.across_again(down)
    tokens_grad, sums_small = tokens_back(
        links, projected_grad, tokens, after_grad, small, [small_2, small_3], centroid_grad, weight_in, []
    )
    twin_small = links.twins(sums_small)
    for grads in expert_sums[1:]:
        summed.append(own_sum(links.gated(grads, summed + [sums_small[0]])))
    sums_in = project_back(links, projected_grad, first_in, [])
    twin_in = links.twins(sums_in)
    up = links.fold_again(up, up_got, "fold_wait")
    up_got = links.across_again(up)
    inner = links.fold([sums_in, sums_small], twin_in + twin_small)
    inner_got = links.across(inner)
    down = links.fold_last(down, down_got)
    down_got = links.inward(down)
    inner = links.fold_again(inner, inner_got)
    inner_got = links.across_again(inner)
    up = links.fold_last(up, up_got)
    up_got = links.inward(up)
    inner = links.fold_last(inner, inner_got)
    inner_got = links.inward(inner)
    output = combine(returned, slots, hidden, gates)
    down = links.joined(down, down_got)
    down_got = links.middle(down)
    up = links.joined(up, up_got)
    up_got = links.middle(up)
    inner = links.joined(inner, inner_got)
    inner_got = links.middle(inner)
    down = links.joined(down, down_got)
    down_got = links.outward(down)
    up = links.joined(up, up_got)
    up_got = links.outward(up)
    inner = links.joined(inner, inner_got)
    inner_got = links.outward(inner)
    expert_sums = finish(summed)
    down_sum = links.settled(down, down_got)
    units, columns = dense_up.shape[1], project_in.shape[1]
    up_sum, out_sum = links.settled_across(up, up_got, units)
    in_sum, gains_sum, shifts_sum, centroids_sum = links.settled_small(inner, inner_got, columns, cols)

    return (
        output, tokens_grad, gains_sum, shifts_sum, in_sum.T, out_sum.T, up_sum,
        down_sum.T, centroids_sum, expert_sums[0][None], expert_sums[1][None],
    )


def solution(mesh):
    sizes = dict(mesh.shape)
    both, over = P(("dp", "expert"), None), P(None, "expert")
    expert_place = P("expert", None, "dp")
    return jax.shard_map(
        functools.partial(on_device, sizes["expert"], sizes["dp"]),
        mesh=mesh,
        in_specs=(both,) * 3 + (over,) * 7 + (expert_place,) * 2 + (both,),
        out_specs=(both,) * 2 + (over,) * 7 + (expert_place,) * 2,
        check_vma=False,
    )
```
